128 devices in a mesh: comp: 8 (over x, z_hi), band: 16 (over z_lo, y, core).
Axes of the slice: x: 4, y: 4, z: 4 (z_hi: 2, z_lo: 2; z = z_hi * 2 + z_lo), core: 2. Of those that a mesh axis runs over, the one named last changes fastest.
Arguments:
- estimate: float32 [1024, 256], P('band'), may hold values from -6 to 6
- residual: float32 [1024, 256], P('band'), may hold values from -50 to 50
- direction: float32 [1024, 256], P('band'), may hold values from -50 to 50
- kernels: bfloat16 [32, 65, 65], P('comp'), may hold values from -0.015625 to 0.015625
- weight_maps: bfloat16 [32, 1024, 256], P('comp', 'band'), may hold values from -6 to 6
- filters_in: float32 [64, 3, 3], replicated, may hold values from -2 to 2
- biases: float32 [64], replicated, may hold values from -3 to 3
- filters_out: float32 [64, 3, 3], replicated, may hold values from -0.25 to 0.25
Outputs:
- estimate_next: float32 [1024, 256], P('band')
- residual_next: float32 [1024, 256], P('band')
- direction_next: float32 [1024, 256], P('band')
- denoised: float32 [1024, 256], P('band', 'comp')
The draws below stay inside these ranges and needn't reach their ends.
All inputs are finite; a program needn't handle non-finite values.
Results may differ from the reference program's by a relative error of at most 0.0024.
Values may be sent and summed in bfloat16 or wider, within the bound.
A program may use at most 64 MiB of HBM per device.

```python
import jax
import jax.numpy as jnp
from jax import lax

K = 32
P_SIZE = 65
C = 64
W = 256
HALF = 32
H = 1024


def field_scales(key):
    rows = jnp.arange(H, dtype=jnp.float32) / max(H - 1, 1)
    column_exps = jax.random.uniform(jax.random.fold_in(key, 11), (W,), jnp.float32)
    return (10.0 ** rows)[:, None] * (10.0 ** column_exps)[None, :] / 10.0


def field_noise(key, salt):
    noise = jnp.clip(jax.random.normal(jax.random.fold_in(key, salt), (H, W), jnp.float32), -5.0, 5.0)
    return noise * field_scales(key)


def draw_residual(key, part):
    return field_noise(key, 21)


def draw_direction(key, part):
    return field_noise(key, 22)


def level_of(key, shape, cuts, least, largest):
    factor_of, own = 1.0, jax.random.fold_in(key, 6)
    for position, shards_of in cuts:
        steps = jnp.exp(jax.random.uniform(jax.random.fold_in(own, position), (shards_of,), jnp.float32, least / len(cuts), largest / len(cuts)))
        factor_of = factor_of * jnp.repeat(steps, shape[position] // shards_of).reshape([-1 if axis == position else 1 for axis in range(len(shape))])
    return factor_of


def bell_draw(key, shape, spread, limit, split=(), held_as=jnp.bfloat16):
    values = jax.random.normal(key, shape, jnp.float32) * spread
    if len(split) > 0:
        values = level_of(key, shape, split, -0.22, 0.18) * values
    return jnp.clip(values, min=-limit, max=limit).astype(held_as)


def setup_inputs(seed: int = 0) -> dict:
    keys = jax.random.split(jax.random.key(seed), 9)
    return {
        "estimate": bell_draw(keys[0], (H, W), 1.0, 6.0, ((0, 16),), jnp.float32),
        "residual": draw_residual(jax.random.fold_in(keys[8], 71), 0),
        "direction": draw_direction(jax.random.fold_in(keys[8], 71), 0),
        "kernels": bell_draw(keys[3], (K, P_SIZE, P_SIZE), (K * P_SIZE * P_SIZE) ** -0.5, 0.015625, ((0, 8),)),
        "weight_maps": bell_draw(keys[4], (K, H, W), 1.0, 6.0, ((0, 8), (1, 16))),
        "filters_in": bell_draw(keys[5], (C, 3, 3), 9 ** -0.5, 2.0, (), jnp.float32),
        "biases": bell_draw(keys[6], (C,), 0.5, 3.0, (), jnp.float32),
        "filters_out": bell_draw(keys[7], (C, 3, 3), (9 * C) ** -0.5, 0.25, (), jnp.float32),
    }


damping = 0.5
numbers = ("NCHW", "OIHW", "NCHW")


def reference(estimate, residual, direction, kernels, weight_maps, filters_in, biases, filters_out):
    maps_wide = weight_maps.astype(jnp.float32)
    shaped = (maps_wide * direction[None]).astype(jnp.bfloat16)
    image = lax.conv_general_dilated(shaped[None], kernels[None], (1, 1), [(HALF, HALF), (HALF, HALF)], dimension_numbers=numbers, preferred_element_type=jnp.float32)[0, 0]
    image = image.astype(jnp.bfloat16)
    flipped = kernels[:, None, ::-1, ::-1]
    back = lax.conv_general_dilated(image[None, None], flipped, (1, 1), [(HALF, HALF), (HALF, HALF)], dimension_numbers=numbers, preferred_element_type=jnp.float32)[0]
    normal = jnp.sum(maps_wide * back, axis=0)
    curved = normal + damping * direction
    old = jnp.sum(residual * residual)
    alpha = old / jnp.sum(direction * curved)
    estimate_next = estimate + alpha * direction
    residual_next = residual - alpha * curved
    new = jnp.sum(residual_next * residual_next)
    direction_next = residual_next + (new / old) * direction
    features = lax.conv_general_dilated(estimate_next[None, None], filters_in[:, None], (1, 1), [(1, 1), (1, 1)], dimension_numbers=numbers, precision=lax.Precision.HIGHEST)
    features = jax.nn.relu(features + biases[None, :, None, None])
    mixed = lax.conv_general_dilated(features, filters_out[None], (1, 1), [(1, 1), (1, 1)], dimension_numbers=numbers, precision=lax.Precision.HIGHEST)[0, 0]
    denoised = estimate_next - mixed
    return estimate_next, residual_next, direction_next, denoised
```

```python
import functools

import jax
import jax.numpy as jnp
from jax import lax
from jax.experimental import pallas as pl
from jax.experimental.pallas import tpu as pltpu
from jax.sharding import PartitionSpec as P

MESH = pl.DeviceIdType.MESH
F32 = jnp.float32
BF16 = jnp.bfloat16
DAMPING = 0.5
HALF = 32
SPAN = 65
ROWS = 64
WIDTH = 256
FINE = 4
COARSE = 8
GROUP = 40


def lane_shift(x, n):
    if n == 0:
        return x
    width = x.shape[1]
    col = lax.broadcasted_iota(jnp.int32, x.shape, 1)
    keep = col < width - n if n > 0 else col >= -n
    return jnp.where(keep, pltpu.roll(x, (-n) % width, 1), 0.0)


def fold(x):
    x = jnp.sum(x, axis=0, keepdims=True)
    return x[:, :128] + x[:, 128:]


def remote(src, dst, send, recv, comp, band):
    return pltpu.make_async_remote_copy(
        src_ref=src, dst_ref=dst, send_sem=send, recv_sem=recv,
        device_id=(comp, band), device_id_type=MESH,
    )


def kernel(
    nc, nb, unroll,
    est_ref, res_ref, dir_ref, ker_ref, w_ref, fin_ref, bias_ref, fout_ref,
    en_ref, rn_ref, dn_ref, den_ref,
    own, halo, edge, edge_halo, kscr, kt, ktj, gf, gz, hb, hz, shifted, ishift, acc,
    part, rsbuf, iblk, iwin, part2, rsbuf2, sca, sca_in, ag, scb, ext,
    h_s, h_r, rs_s, rs_r, iw_s, in_s, iw_r, rt_s, rt_r, sa_s, sa_r, ag_s, ag_r, sb_s, sb_r,
):
    ci = lax.axis_index("comp")
    bi = lax.axis_index("band")
    up = lax.rem(bi + nb - 1, nb)
    down = lax.rem(bi + 1, nb)
    comps = w_ref.shape[0]

    def peers(fn):
        def body(d, carry):
            fn(lax.rem(ci + d, nc))
            return carry
        lax.fori_loop(1, nc, body, 0)

    def bands(fn):
        def body(d, carry):
            fn(lax.rem(bi + d, nb))
            return carry
        lax.fori_loop(1, nb, body, 0)

    barrier = pltpu.get_barrier_semaphore()

    def greet(comp, band):
        pl.semaphore_signal(barrier, inc=1, device_id=(comp, band), device_id_type=MESH)

    peers(lambda j: greet(j, bi))

    def greet_both(c, carry):
        greet(c, up)
        greet(c, down)
        return carry
    lax.fori_loop(0, nc, greet_both, 0)

    def greet_far(d, carry):
        greet(ci, lax.rem(bi + d, nb))
        return carry
    lax.fori_loop(2, nb - 1, greet_far, 0)

    direction = dir_ref[...]
    for k in range(comps):
        shaped = (w_ref[k].astype(F32) * direction).astype(BF16)
        own[0, k] = shaped[:HALF]
        own[1, k] = shaped[HALF:]
    edge[0, 0] = est_ref[:8]
    edge[0, 1] = dir_ref[:8]
    edge[1, 0] = est_ref[ROWS - 8:]
    edge[1, 1] = dir_ref[ROWS - 8:]

    pl.semaphore_wait(barrier, nc - 1 + 2 * nc + nb - 3)

    halos = [
        remote(own.at[0], halo.at[1], h_s.at[0], h_r.at[1], ci, up),
        remote(own.at[1], halo.at[0], h_s.at[1], h_r.at[0], ci, down),
        remote(edge.at[0], edge_halo.at[1], h_s.at[2], h_r.at[3], ci, up),
        remote(edge.at[1], edge_halo.at[0], h_s.at[3], h_r.at[2], ci, down),
    ]
    for copy in halos:
        copy.start()

    size = 128
    kscr[...] = jnp.zeros_like(kscr)
    anti_r = lax.broadcasted_iota(jnp.int32, (size, size), 0)
    anti_c = lax.broadcasted_iota(jnp.int32, (size, size), 1)
    anti = (anti_r + anti_c == SPAN - 1).astype(BF16)
    for k in range(comps):
        kscr[k, 0:SPAN, 0:SPAN] = ker_ref[k].astype(F32)
    for k in range(comps):
        turned = kscr[k].T
        kt[k] = turned
        ktj[k] = jnp.dot(turned.astype(BF16), anti, preferred_element_type=F32)

    def band_matrix(table, k, b):
        row = table[k, pl.ds(b, 1), :]
        spread = jnp.broadcast_to(row, (ROWS, 128))
        return pltpu.roll(spread, 0, 1, stride=1, stride_axis=0).astype(BF16)

    def build_forward(s1, carry):
        at = pl.ds(pl.multiple_of(s1 * ROWS, ROWS), ROWS)
        for side, sign in ((0, 1), (1, -1)):
            for s0 in range(FINE):
                b = HALF + sign * (1 + s0 + FINE * s1)
                for k in range(comps):
                    lanes = pl.ds((s0 * comps + k) * 128, 128)
                    gf[side, at, lanes] = band_matrix(kt, k, b)
        return carry
    lax.fori_loop(0, COARSE, build_forward, 0)
    for k in range(comps):
        gz[:, pl.ds(k * 128, 128)] = band_matrix(kt, k, HALF)

    def all_shifts(x):
        x = x.astype(F32)
        yield 0, x.astype(BF16)
        for s0 in range(FINE):
            yield 1 + s0, lane_shift(x, 1 + s0).astype(BF16)
            yield 1 + FINE + s0, lane_shift(x, -1 - s0).astype(BF16)

    def shift_own(k, carry):
        for h in range(2):
            for at, value in all_shifts(own[h, k]):
                shifted[at, k, pl.ds(HALF * (1 + h), HALF), :] = value
        return carry
    lax.fori_loop(0, comps, shift_own, 0)

    for copy in halos:
        copy.wait_recv()
    inside = ((bi > 0).astype(F32), (bi < nb - 1).astype(F32))

    def shift_halo(k, carry):
        for h in range(2):
            for at, value in all_shifts(halo[h, k].astype(F32) * inside[h]):
                shifted[at, k, pl.ds(96 * h, HALF), :] = value
        return carry
    lax.fori_loop(0, comps, shift_halo, 0)

    depth = comps * 128
    total = jnp.dot(
        gz[...], shifted[0].reshape(depth, WIDTH), preferred_element_type=F32)
    for side, sign in ((0, 1), (1, -1)):
        source = shifted[pl.ds(1 + side * FINE, FINE)].reshape(FINE * depth, WIDTH)
        acc[...] = jnp.dot(gf[side], source, preferred_element_type=F32)
        for s1 in range(COARSE):
            total += lane_shift(acc[pl.ds(s1 * ROWS, ROWS), :], sign * FINE * s1)
    for j in range(8):
        r, c = j // 2, j % 2
        part[j] = total[16 * r:16 * r + 16, 128 * c:128 * c + 128]

    def rs(j, slot):
        return remote(part.at[j], rsbuf.at[slot], rs_s.at[j], rs_r.at[slot], j, bi)
    peers(lambda j: rs(j, ci).start())

    def build_back(s1, carry):
        at = pl.ds(pl.multiple_of(s1 * ROWS, ROWS), ROWS)
        for side, sign in ((0, 1), (1, -1)):
            for s0 in range(FINE):
                b = HALF - sign * (1 + s0 + FINE * s1)
                for k in range(comps):
                    hb[side, k, at, pl.ds(s0 * 128, 128)] = band_matrix(ktj, k, b)
        return carry
    lax.fori_loop(0, COARSE, build_back, 0)
    for k in range(comps):
        hz[k] = band_matrix(ktj, k, HALF)

    rsbuf[ci] = part[ci]
    peers(lambda j: rs(j, j).wait_recv())
    block = rsbuf[0]
    for j in range(1, nc):
        block += rsbuf[j]
    iblk[...] = block.astype(BF16)
    iwin[ci + 4] = iblk[...]
    far = lax.div(ci, 4)
    far_band = lax.rem(bi + nb - 1 + 2 * far, nb)
    far_slot = ci + 12 - 16 * far

    def to_peer(j):
        return remote(iblk, iwin.at[ci + 4], iw_s.at[j], iw_r.at[ci + 4], j, bi)

    def to_far(j):
        return remote(iblk, iwin.at[far_slot], in_s.at[j], iw_r.at[far_slot], j, far_band)

    def start_far(j, carry):
        to_far(j).start()
        return carry
    lax.fori_loop(0, nc, start_far, 0)
    peers(lambda j: to_peer(j).start())

    def window(at):
        return remote(iblk, iwin.at[at], iw_s.at[0], iw_r.at[at], ci, up)
    peers(lambda j: window(j + 4).wait_recv())

    def wait_far(j, carry):
        window(j).wait_recv()
        window(j + 12).wait_recv()
        return carry
    lax.fori_loop(0, 4, wait_far, 0)

    for r in range(8):
        pair = jnp.concatenate([iwin[2 * r].astype(F32), iwin[2 * r + 1].astype(F32)], axis=1)
        if r < 2:
            pair = pair * inside[0]
        if r >= 6:
            pair = pair * inside[1]
        for at, value in all_shifts(pair):
            ishift[at, pl.ds(16 * r, 16), :] = value

    part_sum = part2
    rsum = jnp.zeros((ROWS, WIDTH), F32)
    for k in range(comps):
        back = jnp.dot(hz[k], ishift[0], preferred_element_type=F32)
        for side, sign in ((0, 1), (1, -1)):
            source = ishift[pl.ds(1 + side * FINE, FINE)].reshape(FINE * 128, WIDTH)
            acc[...] = jnp.dot(hb[side, k], source, preferred_element_type=F32)
            for s1 in range(COARSE):
                back += lane_shift(acc[pl.ds(s1 * ROWS, ROWS), :], sign * FINE * s1)
        rsum += w_ref[k].astype(F32) * back
    for j in range(8):
        r, c = j // 2, j % 2
        part_sum[j] = rsum[16 * r:16 * r + 16, 128 * c:128 * c + 128]

    def rt(j, slot):
        return remote(part_sum.at[j], rsbuf2.at[slot], rt_s.at[j], rt_r.at[slot], j, bi)
    peers(lambda j: rt(j, ci).start())

    direction = dir_ref[...]
    residual = res_ref[...]
    sca[...] = jnp.zeros_like(sca)
    sca[0:1] = fold(direction * rsum)
    sca[1:2] = fold(direction * direction)
    sca[2:3] = fold(residual * residual)

    def sa(b, slot):
        return remote(sca, sca_in.at[slot], sa_s.at[b], sa_r.at[slot], ci, b)
    bands(lambda b: sa(b, bi).start())
    sca_in[bi] = sca[...]
    rsbuf2[ci] = part_sum[ci]

    peers(lambda j: rt(j, j).wait_recv())
    block = rsbuf2[0]
    for j in range(1, nc):
        block += rsbuf2[j]
    bands(lambda b: sa(b, b).wait_recv())
    scalars = sca_in[0]
    for b in range(1, nb):
        scalars += sca_in[b]
    ag[ci, 0:16] = block
    ag[ci, 16:24] = scalars

    def gather(j, slot):
        return remote(ag.at[ci], ag.at[slot], ag_s.at[j], ag_r.at[slot], j, bi)
    peers(lambda j: gather(j, ci).start())
    peers(lambda j: gather(j, j).wait_recv())

    product = ag[0, 16:17]
    for j in range(1, nc):
        product += ag[j, 16:17]
    product = product + DAMPING * ag[0, 17:18]
    old = jnp.sum(ag[0, 18:19], axis=1, keepdims=True)
    alpha = old / jnp.sum(product, axis=1, keepdims=True)

    for j in range(8):
        r, c = j // 2, j % 2
        at = (slice(16 * r, 16 * r + 16), slice(128 * c, 128 * c + 128))
        rn_ref[at] = res_ref[at] - alpha * (ag[j, 0:16] + DAMPING * dir_ref[at])
    updated = rn_ref[...]
    scb[nb] = jnp.broadcast_to(fold(updated * updated), (8, 128))

    def sb(b, slot):
        return remote(scb.at[nb], scb.at[slot], sb_s.at[b], sb_r.at[slot], ci, b)
    bands(lambda b: sb(b, bi).start())
    scb[bi] = scb[nb]

    estimate_next = est_ref[...] + alpha * dir_ref[...]
    en_ref[...] = estimate_next
    ext[0:8] = (edge_halo[0, 0] + alpha * edge_halo[0, 1]) * inside[0]
    ext[8:72] = estimate_next
    ext[72:80] = (edge_halo[1, 0] + alpha * edge_halo[1, 1]) * inside[1]
    framed = ext[...]
    columns = WIDTH // nc
    start = ci * columns
    pick_r = lax.broadcasted_iota(jnp.int32, (WIDTH, 128), 0)
    pick_c = lax.broadcasted_iota(jnp.int32, (WIDTH, 128), 1)
    group = (pick_c >= GROUP).astype(jnp.int32) + (pick_c >= 2 * GROUP).astype(jnp.int32)
    pick = (pick_r == start - 2 + pick_c - GROUP * group).astype(BF16)
    high = framed.astype(BF16)
    rest = framed - high.astype(F32)
    middle = rest.astype(BF16)
    low = (rest - middle.astype(F32)).astype(BF16)
    tile = (
        jnp.dot(high, pick, preferred_element_type=F32)
        + jnp.dot(middle, pick, preferred_element_type=F32)
        + jnp.dot(low, pick, preferred_element_type=F32)
    )
    tile = jnp.concatenate([tile[6:80], jnp.zeros((14, 128), F32)], axis=0)
    lane = lax.broadcasted_iota(jnp.int32, (24, 128), 1)
    row = lax.broadcasted_iota(jnp.int32, (24, 128), 0)
    third = (lane >= GROUP).astype(jnp.int32) + (lane >= 2 * GROUP).astype(jnp.int32)
    taps = []
    for a in range(3):
        packed = jnp.where(
            third == 0, tile[a:a + 24], jnp.where(third == 1, tile[24 + a:48 + a], tile[48 + a:72 + a]))
        for b in range(3):
            taps.append(packed if b == 0 else pltpu.roll(packed, 128 - b, 1))
    image_row = bi * ROWS - 1 + row + 24 * third
    image_col = start - 1 + lane - GROUP * third
    valid = (image_row >= 0) & (image_row < nb * ROWS) & (image_col >= 0) & (image_col < WIDTH)
    channels = bias_ref.shape[0]
    spreads = []
    for part_of in range(3):
        rows = slice(8 * part_of, 8 * part_of + 8)
        mine = [tap[rows] for tap in taps]

        def channel(c, sums):
            value = mine[0] * fin_ref[c * 9] + bias_ref[c]
            for t in range(1, 9):
                value += mine[t] * fin_ref[c * 9 + t]
            value = jnp.maximum(value, 0.0)
            return tuple(sums[t] + value * fout_ref[c * 9 + t] for t in range(9))

        sums = lax.fori_loop(
            0, channels, channel, tuple(jnp.zeros((8, 128), F32) for t in range(9)), unroll=unroll)
        spreads.append(sums)
    mixed = jnp.zeros((ROWS, 128), F32)
    for t in range(9):
        a, b = t // 3, t % 3
        whole = jnp.where(valid, jnp.concatenate([s[t] for s in spreads], axis=0), 0.0)
        column = jnp.concatenate(
            [pltpu.roll(whole, (128 - GROUP * g - b) % 128, 1) for g in range(3)], axis=0)
        mixed += column[a:a + ROWS]
    centre = pltpu.roll(tile[2:2 + ROWS], 126, 1)
    den_ref[...] = (centre - mixed)[:, :columns]

    bands(lambda b: sb(b, b).wait_recv())
    new = scb[0, 0:1]
    for b in range(1, nb):
        new += scb[b, 0:1]
    new = jnp.sum(new, axis=1, keepdims=True)
    dn_ref[...] = rn_ref[...] + (new / old) * dir_ref[...]

    for copy in halos:
        copy.wait_send()
    peers(lambda j: rs(j, ci).wait_send())
    peers(lambda j: to_peer(j).wait_send())

    def end_far(j, carry):
        to_far(j).wait_send()
        return carry
    lax.fori_loop(0, nc, end_far, 0)
    peers(lambda j: rt(j, ci).wait_send())
    bands(lambda b: sa(b, bi).wait_send())
    peers(lambda j: gather(j, ci).wait_send())
    bands(lambda b: sb(b, bi).wait_send())


def per_device(nc, nb, unroll, estimate, residual, direction, kernels, weight_maps, filters_in, biases, filters_out):
    comps = weight_maps.shape[0]
    columns = WIDTH // nc
    vmem = pl.BlockSpec(memory_space=pltpu.VMEM)
    smem = pl.BlockSpec(memory_space=pltpu.SMEM)
    band = jax.ShapeDtypeStruct((ROWS, WIDTH), F32)
    dma = pltpu.SemaphoreType.DMA
    return pl.pallas_call(
        functools.partial(kernel, nc, nb, unroll),
        out_shape=(band, band, band, jax.ShapeDtypeStruct((ROWS, columns), F32)),
        in_specs=[vmem] * 5 + [smem] * 3,
        out_specs=(vmem,) * 4,
        scratch_shapes=[
            pltpu.VMEM((2, comps, HALF, WIDTH), BF16),
            pltpu.VMEM((2, comps, HALF, WIDTH), BF16),
            pltpu.VMEM((2, 2, 8, WIDTH), F32),
            pltpu.VMEM((2, 2, 8, WIDTH), F32),
            pltpu.VMEM((comps, 128, 128), F32),
            pltpu.VMEM((comps, 128, 128), F32),
            pltpu.VMEM((comps, 128, 128), F32),
            pltpu.VMEM((2, COARSE * ROWS, FINE * comps * 128), BF16),
            pltpu.VMEM((ROWS, comps * 128), BF16),
            pltpu.VMEM((2, comps, COARSE * ROWS, FINE * 128), BF16),
            pltpu.VMEM((comps, ROWS, 128), BF16),
            pltpu.VMEM((1 + 2 * FINE, comps, 128, WIDTH), BF16),
            pltpu.VMEM((1 + 2 * FINE, 128, WIDTH), BF16),
            pltpu.VMEM((COARSE * ROWS, WIDTH), F32),
            pltpu.VMEM((8, 16, 128), F32),
            pltpu.VMEM((8, 16, 128), F32),
            pltpu.VMEM((16, 128), BF16),
            pltpu.VMEM((16, 16, 128), BF16),
            pltpu.VMEM((8, 16, 128), F32),
            pltpu.VMEM((8, 16, 128), F32),
            pltpu.VMEM((8, 128), F32),
            pltpu.VMEM((nb, 8, 128), F32),
            pltpu.VMEM((nc, 24, 128), F32),
            pltpu.VMEM((nb + 1, 8, 128), F32),
            pltpu.VMEM((80, WIDTH), F32),
            dma((4,)), dma((4,)),
            dma((nc,)), dma((nc,)),
            dma((nc,)), dma((nc,)), dma((16,)),
            dma((nc,)), dma((nc,)),
            dma((nb,)), dma((nb,)),
            dma((nc,)), dma((nc,)),
            dma((nb,)), dma((nb,)),
        ],
        compiler_params=pltpu.CompilerParams(
            collective_id=0, has_side_effects=True, vmem_limit_bytes=48 * 1024 * 1024),
        cost_estimate=pl.CostEstimate(
            flops=4 * 65 * comps * 64 * 128 * 256, bytes_accessed=1 << 20, transcendentals=0),
    )(estimate, residual, direction, kernels, weight_maps,
      filters_in.reshape(-1), biases, filters_out.reshape(-1))


def solution(mesh):
    nc, nb = mesh.shape["comp"], mesh.shape["band"]
    return jax.shard_map(
        functools.partial(per_device, nc, nb, 4),
        mesh=mesh,
        in_specs=(
            P("band", None),
            P("band", None),
            P("band", None),
            P("comp", None, None),
            P("comp", "band", None),
            P(),
            P(),
            P(),
        ),
        out_specs=(P("band", None), P("band", None), P("band", None), P("band", "comp")),
        check_vma=False,
    )
```

```python
import functools

import jax
import jax.numpy as jnp
from jax import lax
from jax.experimental import pallas as pl
from jax.experimental.pallas import tpu as pltpu
from jax.sharding import PartitionSpec as P

MESH = pl.DeviceIdType.MESH
F32 = jnp.float32
BF16 = jnp.bfloat16
DAMPING = 0.5
HALF = 32
SPAN = 65
ROWS = 64
WIDTH = 256
FINE = 8
COARSE = 4
GROUP = 40


def lane_shift(x, n):
    if n == 0:
        return x
    width = x.shape[1]
    col = lax.broadcasted_iota(jnp.int32, x.shape, 1)
    keep = col < width - n if n > 0 else col >= -n
    return jnp.where(keep, pltpu.roll(x, (-n) % width, 1), jnp.zeros((), x.dtype))


def fold(x):
    x = jnp.sum(x, axis=0, keepdims=True)
    return x[:, :128] + x[:, 128:]


def all_shifts(x):
    yield 0, x
    for s0 in range(FINE):
        yield 1 + s0, lane_shift(x, 1 + s0)
        yield 1 + FINE + s0, lane_shift(x, -1 - s0)


def loop(low, high, fn):
    def body(i, carry):
        fn(i)
        return carry
    lax.fori_loop(low, high, body, 0)


def remote(src, dst, send, recv, comp, band):
    return pltpu.make_async_remote_copy(
        src_ref=src, dst_ref=dst, send_sem=send, recv_sem=recv,
        device_id=(comp, band), device_id_type=MESH,
    )


def kernel(
    nc, nb, unroll,
    est_ref, res_ref, dir_ref, ker_ref, w_ref, fin_ref, bias_ref, fout_ref,
    en_ref, rn_ref, dn_ref, den_ref,
    edge, edge_halo, kscr, kt, ktj, gf, gz, hb, hz, shifted, ishift, acc,
    part, rsbuf, iblk, iwin, part2, rsbuf2, sca, sca_in, ag, scb, ext,
    h_s, h_r, rs_s, rs_r, iw_s, in_s, iw_r, rt_s, rt_r, sa_s, sa_r, ag_s, ag_r, sb_s, sb_r,
):
    ci = lax.axis_index("comp")
    bi = lax.axis_index("band")
    up = lax.rem(bi + nb - 1, nb)
    down = lax.rem(bi + 1, nb)
    comps = w_ref.shape[0]
    half_nc = nc // 2

    def peers(fn):
        loop(1, nc, lambda d: fn(lax.rem(ci + d, nc)))

    def bands(fn):
        loop(1, nb, lambda d: fn(lax.rem(bi + d, nb)))

    barrier = pltpu.get_barrier_semaphore()

    def greet(comp, band):
        pl.semaphore_signal(barrier, inc=1, device_id=(comp, band), device_id_type=MESH)

    def greet_both(c):
        greet(c, up)
        greet(c, down)
    loop(0, nc, greet_both)
    peers(lambda j: greet(j, bi))
    loop(2, nb - 1, lambda d: greet(ci, lax.rem(bi + d, nb)))

    direction = dir_ref[...]
    for k in range(comps):
        shaped = (w_ref[k].astype(F32) * direction).astype(BF16)
        for at, value in all_shifts(shaped):
            shifted[at, pl.ds(k * ROWS, ROWS), :] = value
    edge[0, 0] = est_ref[:8]
    edge[0, 1] = dir_ref[:8]
    edge[1, 0] = est_ref[ROWS - 8:]
    edge[1, 1] = dir_ref[ROWS - 8:]
    residual = res_ref[...]
    sca[...] = jnp.zeros_like(sca)
    sca[1:2] = fold(direction * direction)
    sca[2:3] = fold(residual * residual)

    size = 128
    kscr[...] = jnp.zeros_like(kscr)
    anti_r = lax.broadcasted_iota(jnp.int32, (size, size), 0)
    anti_c = lax.broadcasted_iota(jnp.int32, (size, size), 1)
    anti = (anti_r + anti_c == SPAN - 1).astype(BF16)
    for k in range(comps):
        kscr[k, 0:SPAN, 0:SPAN] = ker_ref[k].astype(F32)
    for k in range(comps):
        turned = kscr[k].T
        kt[k] = turned
        ktj[k] = jnp.dot(turned.astype(BF16), anti, preferred_element_type=F32)

    def band_matrix(table, k, b, first=0):
        row = table[k, pl.ds(b, 1), :]
        spread = jnp.broadcast_to(row, (ROWS, 128))
        return pltpu.roll(spread, first, 1, stride=1, stride_axis=0)

    left = lax.broadcasted_iota(jnp.int32, (ROWS, 128), 1) < ROWS

    def forward_pair(k, b):
        even = band_matrix(kt, k, b)
        odd = band_matrix(kt, k + 1, b, ROWS)
        lower = jnp.where(left, even, odd).astype(BF16)
        upper = jnp.where(left, odd, even).astype(BF16)
        return lower, upper

    def build_forward(s1):
        at = pl.ds(pl.multiple_of(s1 * ROWS, ROWS), ROWS)
        for side, sign in ((0, 1), (1, -1)):
            for s0 in range(FINE):
                b = HALF + sign * (1 + s0 + FINE * s1)
                for k in range(0, comps, 2):
                    lanes = pl.ds(s0 * comps * ROWS + k * ROWS, 128)
                    gf[side, 0, at, lanes], gf[side, 1, at, lanes] = forward_pair(k, b)
    loop(0, COARSE, build_forward)
    for k in range(0, comps, 2):
        gz[0, :, pl.ds(k * ROWS, 128)], gz[1, :, pl.ds(k * ROWS, 128)] = forward_pair(k, HALF)

    depth = comps * ROWS

    def taken(at, where):
        if where == 0:
            return shifted[at]
        return jnp.concatenate(
            [shifted[at, pl.ds((k ^ 1) * ROWS, ROWS), :] for k in range(comps)], axis=0)

    for where in range(2):
        total = jnp.dot(gz[where], taken(0, where), preferred_element_type=F32)
        for side, sign in ((0, 1), (1, -1)):
            source = jnp.concatenate(
                [taken(1 + side * FINE + s0, where) for s0 in range(FINE)], axis=0)
            acc[...] = jnp.dot(gf[side, where], source, preferred_element_type=F32)
            for s1 in range(COARSE):
                total += lane_shift(acc[pl.ds(s1 * ROWS, ROWS), :], sign * FINE * s1)
        base = 8 * (1 - where)
        for q in range(8):
            part[base + q] = total[8 * q:8 * q + 8]

    pl.semaphore_wait(barrier, nc - 1 + 2 * nc + nb - 3)

    def rs_up(c):
        return remote(part.at[c], rsbuf.at[nc + ci], rs_s.at[c], rs_r.at[nc + ci], c + half_nc, up)

    def rs_down(c):
        return remote(
            part.at[12 + c], rsbuf.at[nc + ci], rs_s.at[12 + c], rs_r.at[nc + ci], c, down)

    def rs(j):
        return remote(part.at[4 + j], rsbuf.at[ci], rs_s.at[4 + j], rs_r.at[ci], j, bi)

    def rs_in(slot):
        return remote(part.at[0], rsbuf.at[slot], rs_s.at[0], rs_r.at[slot], ci, up)

    def start_far(c):
        rs_up(c).start()
        rs_down(c).start()
    loop(0, half_nc, start_far)
    peers(lambda j: rs(j).start())
    edges = [
        remote(edge.at[0], edge_halo.at[1], h_s.at[0], h_r.at[1], ci, up),
        remote(edge.at[1], edge_halo.at[0], h_s.at[1], h_r.at[0], ci, down),
    ]
    for copy in edges:
        copy.start()

    def build_back(s1):
        at = pl.ds(pl.multiple_of(s1 * ROWS, ROWS), ROWS)
        for side, sign in ((0, 1), (1, -1)):
            for s0 in range(FINE):
                b = HALF - sign * (1 + s0 + FINE * s1)
                for k in range(comps):
                    hb[side, k, at, pl.ds(s0 * 128, 128)] = band_matrix(ktj, k, b).astype(BF16)
    loop(0, COARSE, build_back)
    for k in range(comps):
        hz[k] = band_matrix(ktj, k, HALF).astype(BF16)

    rsbuf[ci] = part[4 + ci]
    peers(lambda j: rs_in(j).wait_recv())
    loop(0, nc, lambda j: rs_in(nc + j).wait_recv())
    far = lax.div(ci, half_nc)
    near = rsbuf[0]
    away = rsbuf[nc]
    for j in range(1, nc):
        near += rsbuf[j]
        away += rsbuf[nc + j]
    linked = ((bi > 0) | (far == 1)) & ((bi < nb - 1) | (far == 0))
    block = near + jnp.where(linked, away, 0.0)
    iblk[...] = block.astype(BF16).astype(F32)
    iwin[ci + 4] = iblk[...]
    far_band = lax.rem(bi + nb - 1 + 2 * far, nb)
    far_slot = ci + 12 - 16 * far

    def to_peer(j):
        return remote(iblk, iwin.at[ci + 4], iw_s.at[j], iw_r.at[ci + 4], j, bi)

    def to_far(j):
        return remote(iblk, iwin.at[far_slot], in_s.at[j], iw_r.at[far_slot], j, far_band)
    loop(0, nc, lambda j: to_far(j).start())
    peers(lambda j: to_peer(j).start())

    def window(at):
        return remote(iblk, iwin.at[at], iw_s.at[0], iw_r.at[at], ci, up)
    peers(lambda j: window(j + 4).wait_recv())

    def wait_far(j):
        window(j).wait_recv()
        window(j + 12).wait_recv()
    loop(0, 4, wait_far)

    inside = ((bi > 0).astype(F32), (bi < nb - 1).astype(F32))
    for r in range(0, 16, 2):
        pair = jnp.concatenate([iwin[r], iwin[r + 1]], axis=0)
        if r < 4:
            pair = pair * inside[0]
        if r >= 12:
            pair = pair * inside[1]
        for at, value in all_shifts(pair.astype(BF16)):
            ishift[at, pl.ds(8 * r, 16), :] = value

    rsum = jnp.zeros((ROWS, WIDTH), F32)
    for k in range(comps):
        back = jnp.dot(hz[k], ishift[0], preferred_element_type=F32)
        for side, sign in ((0, 1), (1, -1)):
            source = ishift[pl.ds(1 + side * FINE, FINE)].reshape(FINE * 128, WIDTH)
            acc[...] = jnp.dot(hb[side, k], source, preferred_element_type=F32)
            for s1 in range(COARSE):
                back += lane_shift(acc[pl.ds(s1 * ROWS, ROWS), :], sign * FINE * s1)
        rsum += w_ref[k].astype(F32) * back
    for j in range(8):
        part2[j] = rsum[8 * j:8 * j + 8]

    def rt(j, slot):
        return remote(part2.at[j], rsbuf2.at[slot], rt_s.at[j], rt_r.at[slot], j, bi)
    peers(lambda j: rt(j, ci).start())
    sca[0:1] = fold(dir_ref[...] * rsum)

    def sa(b, slot):
        return remote(sca, sca_in.at[slot], sa_s.at[b], sa_r.at[slot], ci, b)
    bands(lambda b: sa(b, bi).start())
    sca_in[bi] = sca[...]
    rsbuf2[ci] = part2[ci]

    peers(lambda j: rt(j, j).wait_recv())
    block = rsbuf2[0]
    for j in range(1, nc):
        block += rsbuf2[j]
    bands(lambda b: sa(b, b).wait_recv())
    scalars = sca_in[0]
    for b in range(1, nb):
        scalars += sca_in[b]
    ag[ci, 0] = block[:, :128]
    ag[ci, 1] = block[:, 128:]
    ag[ci, 2] = scalars

    def gather(j, slot):
        return remote(ag.at[ci], ag.at[slot], ag_s.at[j], ag_r.at[slot], j, bi)
    peers(lambda j: gather(j, ci).start())
    peers(lambda j: gather(j, j).wait_recv())

    product = ag[0, 2, 0:1]
    for j in range(1, nc):
        product += ag[j, 2, 0:1]
    product = product + DAMPING * ag[0, 2, 1:2]
    old = jnp.sum(ag[0, 2, 2:3], axis=1, keepdims=True)
    alpha = old / jnp.sum(product, axis=1, keepdims=True)

    for j in range(8):
        for c in range(2):
            at = (slice(8 * j, 8 * j + 8), slice(128 * c, 128 * c + 128))
            rn_ref[at] = res_ref[at] - alpha * (ag[j, c] + DAMPING * dir_ref[at])
    updated = rn_ref[...]
    scb[nb] = jnp.broadcast_to(fold(updated * updated), (8, 128))

    def sb(b, slot):
        return remote(scb.at[nb], scb.at[slot], sb_s.at[b], sb_r.at[slot], ci, b)
    bands(lambda b: sb(b, bi).start())
    scb[bi] = scb[nb]
    for copy in edges:
        copy.wait_recv()

    estimate_next = est_ref[...] + alpha * dir_ref[...]
    en_ref[...] = estimate_next
    ext[0:8] = (edge_halo[0, 0] + alpha * edge_halo[0, 1]) * inside[0]
    ext[8:72] = estimate_next
    ext[72:80] = (edge_halo[1, 0] + alpha * edge_halo[1, 1]) * inside[1]
    framed = ext[...]
    columns = WIDTH // nc
    start = ci * columns
    pick_r = lax.broadcasted_iota(jnp.int32, (WIDTH, 128), 0)
    pick_c = lax.broadcasted_iota(jnp.int32, (WIDTH, 128), 1)
    group = (pick_c >= GROUP).astype(jnp.int32) + (pick_c >= 2 * GROUP).astype(jnp.int32)
    pick = (pick_r == start - 2 + pick_c - GROUP * group).astype(BF16)
    high = framed.astype(BF16)
    rest = framed - high.astype(F32)
    middle = rest.astype(BF16)
    low = (rest - middle.astype(F32)).astype(BF16)
    tile = (
        jnp.dot(high, pick, preferred_element_type=F32)
        + jnp.dot(middle, pick, preferred_element_type=F32)
        + jnp.dot(low, pick, preferred_element_type=F32)
    )
    tile = jnp.concatenate([tile[6:80], jnp.zeros((14, 128), F32)], axis=0)
    lane = lax.broadcasted_iota(jnp.int32, (24, 128), 1)
    row = lax.broadcasted_iota(jnp.int32, (24, 128), 0)
    third = (lane >= GROUP).astype(jnp.int32) + (lane >= 2 * GROUP).astype(jnp.int32)
    taps = []
    for a in range(3):
        packed = jnp.where(
            third == 0, tile[a:a + 24], jnp.where(third == 1, tile[24 + a:48 + a], tile[48 + a:72 + a]))
        for b in range(3):
            taps.append(packed if b == 0 else pltpu.roll(packed, 128 - b, 1))
    image_row = bi * ROWS - 1 + row + 24 * third
    image_col = start - 1 + lane - GROUP * third
    valid = (image_row >= 0) & (image_row < nb * ROWS) & (image_col >= 0) & (image_col < WIDTH)
    channels = bias_ref.shape[0]
    spreads = []
    for part_of in range(3):
        rows = slice(8 * part_of, 8 * part_of + 8)
        mine = [tap[rows] for tap in taps]

        def channel(c, sums):
            value = mine[0] * fin_ref[0, 0, c] + bias_ref[c]
            for t in range(1, 9):
                value += mine[t] * fin_ref[t // 3, t % 3, c]
            value = jnp.maximum(value, 0.0)
            return tuple(sums[t] + value * fout_ref[t // 3, t % 3, c] for t in range(9))

        sums = lax.fori_loop(
            0, channels, channel, tuple(jnp.zeros((8, 128), F32) for t in range(9)), unroll=unroll)
        spreads.append(sums)
    mixed = jnp.zeros((ROWS, 128), F32)
    for t in range(9):
        a, b = t // 3, t % 3
        whole = jnp.where(valid, jnp.concatenate([s[t] for s in spreads], axis=0), 0.0)
        column = jnp.concatenate(
            [pltpu.roll(whole, (128 - GROUP * g - b) % 128, 1) for g in range(3)], axis=0)
        mixed += column[a:a + ROWS]
    centre = pltpu.roll(tile[2:2 + ROWS], 126, 1)
    den_ref[...] = (centre - mixed).T[:columns]

    bands(lambda b: sb(b, b).wait_recv())
    new = scb[0, 0:1]
    for b in range(1, nb):
        new += scb[b, 0:1]
    new = jnp.sum(new, axis=1, keepdims=True)
    dn_ref[...] = rn_ref[...] + (new / old) * dir_ref[...]

    def end_far(c):
        rs_up(c).wait_send()
        rs_down(c).wait_send()
    loop(0, half_nc, end_far)
    peers(lambda j: rs(j).wait_send())
    for copy in edges:
        copy.wait_send()
    peers(lambda j: to_peer(j).wait_send())
    loop(0, nc, lambda j: to_far(j).wait_send())
    peers(lambda j: rt(j, ci).wait_send())
    bands(lambda b: sa(b, bi).wait_send())
    peers(lambda j: gather(j, ci).wait_send())
    bands(lambda b: sb(b, bi).wait_send())


def place(*refs):
    count = len(refs) // 2
    sources, targets, sems = refs[:count], refs[count:2 * count], refs[-1]
    copies = [
        pltpu.make_async_copy(source, target, sems.at[i])
        for i, (source, target) in enumerate(zip(sources, targets))
    ]
    for copy in copies:
        copy.start()
    for copy in copies:
        copy.wait()


def per_device(nc, nb, unroll, estimate, residual, direction, kernels, weight_maps, filters_in, biases, filters_out):
    comps = weight_maps.shape[0]
    columns = WIDTH // nc
    vmem = pl.BlockSpec(memory_space=pltpu.VMEM)
    smem = pl.BlockSpec(memory_space=pltpu.SMEM)
    anywhere = pl.BlockSpec(memory_space=pl.ANY)
    band = jax.ShapeDtypeStruct((ROWS, WIDTH), F32)
    shapes = (band, band, band, jax.ShapeDtypeStruct((columns, ROWS), F32))
    dma = pltpu.SemaphoreType.DMA
    results = pl.pallas_call(
        functools.partial(kernel, nc, nb, unroll),
        out_shape=shapes,
        in_specs=[vmem] * 5 + [smem] * 3,
        out_specs=(vmem,) * 4,
        scratch_shapes=[
            pltpu.VMEM((2, 2, 8, WIDTH), F32),
            pltpu.VMEM((2, 2, 8, WIDTH), F32),
            pltpu.VMEM((comps, 128, 128), F32),
            pltpu.VMEM((comps, 128, 128), F32),
            pltpu.VMEM((comps, 128, 128), F32),
            pltpu.VMEM((2, 2, COARSE * ROWS, FINE * comps * ROWS), BF16),
            pltpu.VMEM((2, ROWS, comps * ROWS), BF16),
            pltpu.VMEM((2, comps, COARSE * ROWS, FINE * 128), BF16),
            pltpu.VMEM((comps, ROWS, 128), BF16),
            pltpu.VMEM((1 + 2 * FINE, comps * ROWS, WIDTH), BF16),
            pltpu.VMEM((1 + 2 * FINE, 128, WIDTH), BF16),
            pltpu.VMEM((COARSE * ROWS, WIDTH), F32),
            pltpu.VMEM((16, 8, WIDTH), F32),
            pltpu.VMEM((2 * nc, 8, WIDTH), F32),
            pltpu.VMEM((8, WIDTH), F32),
            pltpu.VMEM((16, 8, WIDTH), F32),
            pltpu.VMEM((8, 8, WIDTH), F32),
            pltpu.VMEM((8, 8, WIDTH), F32),
            pltpu.VMEM((8, 128), F32),
            pltpu.VMEM((nb, 8, 128), F32),
            pltpu.VMEM((nc, 3, 8, 128), F32),
            pltpu.VMEM((nb + 1, 8, 128), F32),
            pltpu.VMEM((80, WIDTH), F32),
            dma((2,)), dma((2,)),
            dma((16,)), dma((2 * nc,)),
            dma((nc,)), dma((nc,)), dma((16,)),
            dma((nc,)), dma((nc,)),
            dma((nb,)), dma((nb,)),
            dma((nc,)), dma((nc,)),
            dma((nb,)), dma((nb,)),
        ],
        compiler_params=pltpu.CompilerParams(
            collective_id=0, has_side_effects=True, vmem_limit_bytes=48 * 1024 * 1024),
        cost_estimate=pl.CostEstimate(
            flops=4 * 65 * comps * 64 * 128 * 256, bytes_accessed=1 << 20, transcendentals=0),
    )(estimate, residual, direction, kernels, weight_maps,
      filters_in.transpose(1, 2, 0), biases, filters_out.transpose(1, 2, 0))
    estimate_next, residual_next, direction_next, turned = pl.pallas_call(
        place,
        out_shape=shapes,
        in_specs=[vmem] * 4,
        out_specs=(anywhere,) * 4,
        scratch_shapes=[dma((4,))],
        compiler_params=pltpu.CompilerParams(vmem_limit_bytes=4 * 1024 * 1024),
    )(*results)
    return estimate_next, residual_next, direction_next, turned.T


def solution(mesh):
    nc, nb = mesh.shape["comp"], mesh.shape["band"]
    return jax.shard_map(
        functools.partial(per_device, nc, nb, 4),
        mesh=mesh,
        in_specs=(
            P("band", None),
            P("band", None),
            P("band", None),
            P("comp", None, None),
            P("comp", "band", None),
            P(),
            P(),
            P(),
        ),
        out_specs=(P("band", None), P("band", None), P("band", None), P("band", "comp")),
        check_vma=False,
    )
```

```python
import functools

import jax
import jax.numpy as jnp
from jax import lax
from jax.experimental import pallas as pl
from jax.experimental.pallas import tpu as pltpu
from jax.sharding import PartitionSpec as P

MESH = pl.DeviceIdType.MESH
F32 = jnp.float32
BF16 = jnp.bfloat16
DAMPING = 0.5
HALF = 32
SPAN = 65
ROWS = 64
WIDTH = 256
FINE = 8
COARSE = 4
GROUP = 40


def lane_shift(x, n):
    if n == 0:
        return x
    width = x.shape[1]
    col = lax.broadcasted_iota(jnp.int32, x.shape, 1)
    keep = col < width - n if n > 0 else col >= -n
    return jnp.where(keep, pltpu.roll(x, (-n) % width, 1), jnp.zeros((), x.dtype))


def fold(x):
    x = jnp.sum(x, axis=0, keepdims=True)
    return x[:, :128] + x[:, 128:]


def all_shifts(x):
    yield 0, x
    for s0 in range(FINE):
        yield 1 + s0, lane_shift(x, 1 + s0)
        yield 1 + FINE + s0, lane_shift(x, -1 - s0)


def loop(low, high, fn):
    def body(i, carry):
        fn(i)
        return carry
    lax.fori_loop(low, high, body, 0)


def remote(src, dst, send, recv, comp, band):
    return pltpu.make_async_remote_copy(
        src_ref=src, dst_ref=dst, send_sem=send, recv_sem=recv,
        device_id=(comp, band), device_id_type=MESH,
    )


def kernel(
    nc, nb, unroll,
    est_hbm, res_hbm, dir_hbm, ker_hbm, w_hbm, fin_hbm, bias_hbm, fout_hbm,
    en_ref, rn_ref, dn_ref, den_ref,
    est_ref, res_ref, dir_ref, ker_ref, w_ref, fin_ref, bias_ref, fout_ref, fetch_s,
    edge, edge_halo, kscr, kt, ktj, gf, gz, hb, hz, shifted, ishift, acc,
    part, rsbuf, iblk, iwin, part2, rsbuf2, sca, sca_in, ag, scb, ext,
    h_s, h_r, rs_s, rs_r, iw_s, in_s, iw_r, rt_s, rt_r, sa_s, sa_r, ag_s, ag_r, sb_s, sb_r,
):
    ci = lax.axis_index("comp")
    bi = lax.axis_index("band")
    up = lax.rem(bi + nb - 1, nb)
    down = lax.rem(bi + 1, nb)
    comps = w_ref.shape[0]
    half_nc = nc // 2

    def peers(fn):
        loop(1, nc, lambda d: fn(lax.rem(ci + d, nc)))

    def bands(fn):
        loop(1, nb, lambda d: fn(lax.rem(bi + d, nb)))

    fetches = [
        pltpu.make_async_copy(source, target, fetch_s.at[i])
        for i, (source, target) in enumerate((
            (ker_hbm, ker_ref), (dir_hbm, dir_ref), (w_hbm, w_ref), (res_hbm, res_ref),
            (est_hbm, est_ref), (fin_hbm, fin_ref), (bias_hbm, bias_ref), (fout_hbm, fout_ref)))
    ]
    for copy in fetches:
        copy.start()
    ends = []

    barrier = pltpu.get_barrier_semaphore()

    def greet(comp, band):
        pl.semaphore_signal(barrier, inc=1, device_id=(comp, band), device_id_type=MESH)

    def greet_both(c):
        greet(c, up)
        greet(c, down)
    loop(0, nc, greet_both)
    peers(lambda j: greet(j, bi))
    loop(2, nb - 1, lambda d: greet(ci, lax.rem(bi + d, nb)))

    size = 128
    kscr[...] = jnp.zeros_like(kscr)
    anti_r = lax.broadcasted_iota(jnp.int32, (size, size), 0)
    anti_c = lax.broadcasted_iota(jnp.int32, (size, size), 1)
    anti = (anti_r + anti_c == SPAN - 1).astype(BF16)
    fetches[0].wait()
    for a in range(SPAN):
        kscr[:, a, 0:SPAN] = ker_ref[a].astype(F32)
    for k in range(comps):
        turned = kscr[k].T
        kt[k] = turned
        ktj[k] = jnp.dot(turned.astype(BF16), anti, preferred_element_type=F32)

    fetches[1].wait()
    fetches[2].wait()
    direction = dir_ref[...]
    for k in range(comps):
        shaped = (w_ref[k].astype(F32) * direction).astype(BF16)
        for at, value in all_shifts(shaped):
            shifted[at, pl.ds(k * ROWS, ROWS), :] = value
    def band_matrix(table, k, b, first=0):
        row = table[k, pl.ds(b, 1), :]
        spread = jnp.broadcast_to(row, (ROWS, 128))
        return pltpu.roll(spread, first, 1, stride=1, stride_axis=0)

    left = lax.broadcasted_iota(jnp.int32, (ROWS, 128), 1) < ROWS

    def forward_pair(k, b):
        even = band_matrix(kt, k, b)
        odd = band_matrix(kt, k + 1, b, ROWS)
        lower = jnp.where(left, even, odd).astype(BF16)
        upper = jnp.where(left, odd, even).astype(BF16)
        return lower, upper

    def build_forward(s1):
        at = pl.ds(pl.multiple_of(s1 * ROWS, ROWS), ROWS)
        for side, sign in ((0, 1), (1, -1)):
            for s0 in range(FINE):
                b = HALF + sign * (1 + s0 + FINE * s1)
                for k in range(0, comps, 2):
                    lanes = pl.ds(s0 * comps * ROWS + k * ROWS, 128)
                    gf[side, 0, at, lanes], gf[side, 1, at, lanes] = forward_pair(k, b)
    loop(0, COARSE, build_forward)
    for k in range(0, comps, 2):
        gz[0, :, pl.ds(k * ROWS, 128)], gz[1, :, pl.ds(k * ROWS, 128)] = forward_pair(k, HALF)

    depth = comps * ROWS

    def taken(at, where):
        if where == 0:
            return shifted[at]
        return jnp.concatenate(
            [shifted[at, pl.ds((k ^ 1) * ROWS, ROWS), :] for k in range(comps)], axis=0)

    for where in range(2):
        total = jnp.dot(gz[where], taken(0, where), preferred_element_type=F32)
        for side, sign in ((0, 1), (1, -1)):
            source = jnp.concatenate(
                [taken(1 + side * FINE + s0, where) for s0 in range(FINE)], axis=0)
            acc[...] = jnp.dot(gf[side, where], source, preferred_element_type=F32)
            for s1 in range(COARSE):
                total += lane_shift(acc[pl.ds(s1 * ROWS, ROWS), :], sign * FINE * s1)
        base = 8 * (1 - where)
        for q in range(8):
            part[base + q] = total[8 * q:8 * q + 8]

    for copy in fetches[3:]:
        copy.wait()
    edge[0, 0] = est_ref[:8]
    edge[0, 1] = dir_ref[:8]
    edge[1, 0] = est_ref[ROWS - 8:]
    edge[1, 1] = dir_ref[ROWS - 8:]
    residual = res_ref[...]
    sca[...] = jnp.zeros_like(sca)
    sca[1:2] = fold(direction * direction)
    sca[2:3] = fold(residual * residual)
    pl.semaphore_wait(barrier, nc - 1 + 2 * nc + nb - 3)

    def rs_up(c):
        return remote(part.at[c], rsbuf.at[nc + ci], rs_s.at[c], rs_r.at[nc + ci], c + half_nc, up)

    def rs_down(c):
        return remote(
            part.at[12 + c], rsbuf.at[nc + ci], rs_s.at[12 + c], rs_r.at[nc + ci], c, down)

    def rs(j):
        return remote(part.at[4 + j], rsbuf.at[ci], rs_s.at[4 + j], rs_r.at[ci], j, bi)

    def rs_in(slot):
        return remote(part.at[0], rsbuf.at[slot], rs_s.at[0], rs_r.at[slot], ci, up)

    def start_far(c):
        rs_up(c).start()
        rs_down(c).start()
    loop(0, half_nc, start_far)
    peers(lambda j: rs(j).start())
    edges = [
        remote(edge.at[0], edge_halo.at[1], h_s.at[0], h_r.at[1], ci, up),
        remote(edge.at[1], edge_halo.at[0], h_s.at[1], h_r.at[0], ci, down),
    ]
    for copy in edges:
        copy.start()

    def end_far(c):
        rs_up(c).wait_send()
        rs_down(c).wait_send()
    ends.append(lambda: loop(0, half_nc, end_far))
    ends.append(lambda: peers(lambda j: rs(j).wait_send()))
    ends.extend(copy.wait_send for copy in edges)

    def build_back(s1):
        at = pl.ds(pl.multiple_of(s1 * ROWS, ROWS), ROWS)
        for side, sign in ((0, 1), (1, -1)):
            for s0 in range(FINE):
                b = HALF - sign * (1 + s0 + FINE * s1)
                for k in range(comps):
                    hb[side, k, at, pl.ds(s0 * 128, 128)] = band_matrix(ktj, k, b).astype(BF16)
    loop(0, COARSE, build_back)
    for k in range(comps):
        hz[k] = band_matrix(ktj, k, HALF).astype(BF16)

    rsbuf[ci] = part[4 + ci]
    peers(lambda j: rs_in(j).wait_recv())
    loop(0, nc, lambda j: rs_in(nc + j).wait_recv())
    far = lax.div(ci, half_nc)
    near = rsbuf[0]
    away = rsbuf[nc]
    for j in range(1, nc):
        near += rsbuf[j]
        away += rsbuf[nc + j]
    linked = ((bi > 0) | (far == 1)) & ((bi < nb - 1) | (far == 0))
    block = near + jnp.where(linked, away, 0.0)
    iblk[...] = block.astype(BF16).astype(F32)
    iwin[ci + 4] = iblk[...]
    far_band = lax.rem(bi + nb - 1 + 2 * far, nb)
    far_slot = ci + 12 - 16 * far

    def to_peer(j):
        return remote(iblk, iwin.at[ci + 4], iw_s.at[j], iw_r.at[ci + 4], j, bi)

    def to_far(j):
        return remote(iblk, iwin.at[far_slot], in_s.at[j], iw_r.at[far_slot], j, far_band)
    loop(0, nc, lambda j: to_far(j).start())
    peers(lambda j: to_peer(j).start())
    ends.append(lambda: peers(lambda j: to_peer(j).wait_send()))
    ends.append(lambda: loop(0, nc, lambda j: to_far(j).wait_send()))

    def window(at):
        return remote(iblk, iwin.at[at], iw_s.at[0], iw_r.at[at], ci, up)
    peers(lambda j: window(j + 4).wait_recv())

    def wait_far(j):
        window(j).wait_recv()
        window(j + 12).wait_recv()
    loop(0, 4, wait_far)

    inside = ((bi > 0).astype(F32), (bi < nb - 1).astype(F32))
    for r in range(0, 16, 2):
        pair = jnp.concatenate([iwin[r], iwin[r + 1]], axis=0)
        if r < 4:
            pair = pair * inside[0]
        if r >= 12:
            pair = pair * inside[1]
        for at, value in all_shifts(pair.astype(BF16)):
            ishift[at, pl.ds(8 * r, 16), :] = value

    rsum = jnp.zeros((ROWS, WIDTH), F32)
    for k in range(comps):
        back = jnp.dot(hz[k], ishift[0], preferred_element_type=F32)
        for side, sign in ((0, 1), (1, -1)):
            source = ishift[pl.ds(1 + side * FINE, FINE)].reshape(FINE * 128, WIDTH)
            acc[...] = jnp.dot(hb[side, k], source, preferred_element_type=F32)
            for s1 in range(COARSE):
                back += lane_shift(acc[pl.ds(s1 * ROWS, ROWS), :], sign * FINE * s1)
        rsum += w_ref[k].astype(F32) * back
    for j in range(8):
        part2[j] = rsum[8 * j:8 * j + 8]

    def rt(j, slot):
        return remote(part2.at[j], rsbuf2.at[slot], rt_s.at[j], rt_r.at[slot], j, bi)
    peers(lambda j: rt(j, ci).start())
    ends.append(lambda: peers(lambda j: rt(j, ci).wait_send()))
    sca[0:1] = fold(dir_ref[...] * rsum)

    def sa(b, slot):
        return remote(sca, sca_in.at[slot], sa_s.at[b], sa_r.at[slot], ci, b)
    bands(lambda b: sa(b, bi).start())
    ends.append(lambda: bands(lambda b: sa(b, bi).wait_send()))
    sca_in[bi] = sca[...]
    rsbuf2[ci] = part2[ci]

    peers(lambda j: rt(j, j).wait_recv())
    block = rsbuf2[0]
    for j in range(1, nc):
        block += rsbuf2[j]
    bands(lambda b: sa(b, b).wait_recv())
    scalars = sca_in[0]
    for b in range(1, nb):
        scalars += sca_in[b]
    ag[ci, 0] = block[:, :128]
    ag[ci, 1] = block[:, 128:]
    ag[ci, 2] = scalars

    def gather(j, slot):
        return remote(ag.at[ci], ag.at[slot], ag_s.at[j], ag_r.at[slot], j, bi)
    peers(lambda j: gather(j, ci).start())
    ends.append(lambda: peers(lambda j: gather(j, ci).wait_send()))
    peers(lambda j: gather(j, j).wait_recv())

    product = ag[0, 2, 0:1]
    for j in range(1, nc):
        product += ag[j, 2, 0:1]
    product = product + DAMPING * ag[0, 2, 1:2]
    old = jnp.sum(ag[0, 2, 2:3], axis=1, keepdims=True)
    alpha = old / jnp.sum(product, axis=1, keepdims=True)

    for j in range(8):
        for c in range(2):
            at = (slice(8 * j, 8 * j + 8), slice(128 * c, 128 * c + 128))
            rn_ref[at] = res_ref[at] - alpha * (ag[j, c] + DAMPING * dir_ref[at])
    updated = rn_ref[...]
    scb[nb] = jnp.broadcast_to(fold(updated * updated), (8, 128))

    def sb(b, slot):
        return remote(scb.at[nb], scb.at[slot], sb_s.at[b], sb_r.at[slot], ci, b)
    bands(lambda b: sb(b, bi).start())
    ends.append(lambda: bands(lambda b: sb(b, bi).wait_send()))
    scb[bi] = scb[nb]
    for copy in edges:
        copy.wait_recv()

    estimate_next = est_ref[...] + alpha * dir_ref[...]
    en_ref[...] = estimate_next
    ext[0:8] = (edge_halo[0, 0] + alpha * edge_halo[0, 1]) * inside[0]
    ext[8:72] = estimate_next
    ext[72:80] = (edge_halo[1, 0] + alpha * edge_halo[1, 1]) * inside[1]
    framed = ext[...]
    columns = WIDTH // nc
    start = ci * columns
    pick_r = lax.broadcasted_iota(jnp.int32, (WIDTH, 128), 0)
    pick_c = lax.broadcasted_iota(jnp.int32, (WIDTH, 128), 1)
    group = (pick_c >= GROUP).astype(jnp.int32) + (pick_c >= 2 * GROUP).astype(jnp.int32)
    pick = (pick_r == start - 2 + pick_c - GROUP * group).astype(BF16)
    high = framed.astype(BF16)
    rest = framed - high.astype(F32)
    middle = rest.astype(BF16)
    low = (rest - middle.astype(F32)).astype(BF16)
    tile = (
        jnp.dot(high, pick, preferred_element_type=F32)
        + jnp.dot(middle, pick, preferred_element_type=F32)
        + jnp.dot(low, pick, preferred_element_type=F32)
    )
    tile = jnp.concatenate([tile[6:80], jnp.zeros((14, 128), F32)], axis=0)
    lane = lax.broadcasted_iota(jnp.int32, (24, 128), 1)
    row = lax.broadcasted_iota(jnp.int32, (24, 128), 0)
    third = (lane >= GROUP).astype(jnp.int32) + (lane >= 2 * GROUP).astype(jnp.int32)
    taps = []
    for a in range(3):
        packed = jnp.where(
            third == 0, tile[a:a + 24], jnp.where(third == 1, tile[24 + a:48 + a], tile[48 + a:72 + a]))
        for b in range(3):
            taps.append(packed if b == 0 else pltpu.roll(packed, 128 - b, 1))
    image_row = bi * ROWS - 1 + row + 24 * third
    image_col = start - 1 + lane - GROUP * third
    valid = (image_row >= 0) & (image_row < nb * ROWS) & (image_col >= 0) & (image_col < WIDTH)
    channels = bias_ref.shape[0]
    spreads = []
    for part_of in range(3):
        rows = slice(8 * part_of, 8 * part_of + 8)
        mine = [tap[rows] for tap in taps]

        def channel(c, sums):
            value = mine[0] * fin_ref[0, 0, c] + bias_ref[c]
            for t in range(1, 9):
                value += mine[t] * fin_ref[t // 3, t % 3, c]
            value = jnp.maximum(value, 0.0)
            return tuple(sums[t] + value * fout_ref[t // 3, t % 3, c] for t in range(9))

        sums = lax.fori_loop(
            0, channels, channel, tuple(jnp.zeros((8, 128), F32) for t in range(9)), unroll=unroll)
        spreads.append(sums)
    mixed = jnp.zeros((ROWS, 128), F32)
    for t in range(9):
        a, b = t // 3, t % 3
        whole = jnp.where(valid, jnp.concatenate([s[t] for s in spreads], axis=0), 0.0)
        column = jnp.concatenate(
            [pltpu.roll(whole, (128 - GROUP * g - b) % 128, 1) for g in range(3)], axis=0)
        mixed += column[a:a + ROWS]
    centre = pltpu.roll(tile[2:2 + ROWS], 126, 1)
    den_ref[...] = (centre - mixed).T[:columns]

    bands(lambda b: sb(b, b).wait_recv())
    new = scb[0, 0:1]
    for b in range(1, nb):
        new += scb[b, 0:1]
    new = jnp.sum(new, axis=1, keepdims=True)
    dn_ref[...] = rn_ref[...] + (new / old) * dir_ref[...]

    for end in ends:
        end()


def place(*refs):
    count = len(refs) // 2
    sources, targets, sems = refs[:count], refs[count:2 * count], refs[-1]
    copies = [
        pltpu.make_async_copy(source, target, sems.at[i])
        for i, (source, target) in enumerate(zip(sources, targets))
    ]
    for copy in copies:
        copy.start()
    for copy in copies:
        copy.wait()


def per_device(nc, nb, unroll, estimate, residual, direction, kernels, weight_maps, filters_in, biases, filters_out):
    comps = weight_maps.shape[0]
    columns = WIDTH // nc
    vmem = pl.BlockSpec(memory_space=pltpu.VMEM)
    hbm = pl.BlockSpec(memory_space=pltpu.HBM)
    anywhere = pl.BlockSpec(memory_space=pl.ANY)
    band = jax.ShapeDtypeStruct((ROWS, WIDTH), F32)
    shapes = (band, band, band, jax.ShapeDtypeStruct((columns, ROWS), F32))
    dma = pltpu.SemaphoreType.DMA
    results = pl.pallas_call(
        functools.partial(kernel, nc, nb, unroll),
        out_shape=shapes,
        in_specs=[hbm] * 8,
        out_specs=(vmem,) * 4,
        scratch_shapes=[
            pltpu.VMEM((ROWS, WIDTH), F32),
            pltpu.VMEM((ROWS, WIDTH), F32),
            pltpu.VMEM((ROWS, WIDTH), F32),
            pltpu.VMEM((SPAN, comps, SPAN), BF16),
            pltpu.VMEM((comps, ROWS, WIDTH), BF16),
            pltpu.SMEM((3, 3, filters_in.shape[0]), F32),
            pltpu.SMEM(biases.shape, F32),
            pltpu.SMEM((3, 3, filters_in.shape[0]), F32),
            dma((8,)),
            pltpu.VMEM((2, 2, 8, WIDTH), F32),
            pltpu.VMEM((2, 2, 8, WIDTH), F32),
            pltpu.VMEM((comps, 128, 128), F32),
            pltpu.VMEM((comps, 128, 128), F32),
            pltpu.VMEM((comps, 128, 128), F32),
            pltpu.VMEM((2, 2, COARSE * ROWS, FINE * comps * ROWS), BF16),
            pltpu.VMEM((2, ROWS, comps * ROWS), BF16),
            pltpu.VMEM((2, comps, COARSE * ROWS, FINE * 128), BF16),
            pltpu.VMEM((comps, ROWS, 128), BF16),
            pltpu.VMEM((1 + 2 * FINE, comps * ROWS, WIDTH), BF16),
            pltpu.VMEM((1 + 2 * FINE, 128, WIDTH), BF16),
            pltpu.VMEM((COARSE * ROWS, WIDTH), F32),
            pltpu.VMEM((16, 8, WIDTH), F32),
            pltpu.VMEM((2 * nc, 8, WIDTH), F32),
            pltpu.VMEM((8, WIDTH), F32),
            pltpu.VMEM((16, 8, WIDTH), F32),
            pltpu.VMEM((8, 8, WIDTH), F32),
            pltpu.VMEM((8, 8, WIDTH), F32),
            pltpu.VMEM((8, 128), F32),
            pltpu.VMEM((nb, 8, 128), F32),
            pltpu.VMEM((nc, 3, 8, 128), F32),
            pltpu.VMEM((nb + 1, 8, 128), F32),
            pltpu.VMEM((80, WIDTH), F32),
            dma((2,)), dma((2,)),
            dma((16,)), dma((2 * nc,)),
            dma((nc,)), dma((nc,)), dma((16,)),
            dma((nc,)), dma((nc,)),
            dma((nb,)), dma((nb,)),
            dma((nc,)), dma((nc,)),
            dma((nb,)), dma((nb,)),
        ],
        compiler_params=pltpu.CompilerParams(
            collective_id=0, has_side_effects=True, vmem_limit_bytes=54960 * 1024),
        cost_estimate=pl.CostEstimate(
            flops=4 * 65 * comps * 64 * 128 * 256, bytes_accessed=1 << 20, transcendentals=0),
    )(estimate, residual, direction, kernels.transpose(1, 0, 2), weight_maps,
      filters_in.transpose(1, 2, 0), biases, filters_out.transpose(1, 2, 0))
    estimate_next, residual_next, direction_next, turned = pl.pallas_call(
        place,
        out_shape=shapes,
        in_specs=[vmem] * 4,
        out_specs=(anywhere,) * 4,
        scratch_shapes=[dma((4,))],
        compiler_params=pltpu.CompilerParams(vmem_limit_bytes=4 * 1024 * 1024),
    )(*results)
    return estimate_next, residual_next, direction_next, turned.T


def solution(mesh):
    nc, nb = mesh.shape["comp"], mesh.shape["band"]
    return jax.shard_map(
        functools.partial(per_device, nc, nb, 4),
        mesh=mesh,
        in_specs=(
            P("band", None),
            P("band", None),
            P("band", None),
            P("comp", None, None),
            P("comp", "band", None),
            P(),
            P(),
            P(),
        ),
        out_specs=(P("band", None), P("band", None), P("band", None), P("band", "comp")),
        check_vma=False,
    )
```

```python
import functools

import jax
import jax.numpy as jnp
from jax import lax
from jax.experimental import pallas as pl
from jax.experimental.pallas import tpu as pltpu
from jax.sharding import PartitionSpec as P

MESH = pl.DeviceIdType.MESH
F32 = jnp.float32
BF16 = jnp.bfloat16
DAMPING = 0.5
HALF = 32
SPAN = 65
ROWS = 64
WIDTH = 256
FINE = 8
COARSE = 4
GROUP = 40


def lane_shift(x, n):
    if n == 0:
        return x
    width = x.shape[1]
    col = lax.broadcasted_iota(jnp.int32, x.shape, 1)
    keep = col < width - n if n > 0 else col >= -n
    return jnp.where(keep, pltpu.roll(x, (-n) % width, 1), jnp.zeros((), x.dtype))


def fold(x):
    x = jnp.sum(x, axis=0, keepdims=True)
    return x[:, :128] + x[:, 128:]


def all_shifts(x):
    yield 0, x
    for s0 in range(FINE):
        yield 1 + s0, lane_shift(x, 1 + s0)
        yield 1 + FINE + s0, lane_shift(x, -1 - s0)


def loop(low, high, fn):
    def body(i, carry):
        fn(i)
        return carry
    lax.fori_loop(low, high, body, 0)


def remote(src, dst, send, recv, comp, band):
    return pltpu.make_async_remote_copy(
        src_ref=src, dst_ref=dst, send_sem=send, recv_sem=recv,
        device_id=(comp, band), device_id_type=MESH,
    )


def kernel(
    nc, nb, unroll,
    est_hbm, res_hbm, dir_hbm, ker_hbm, w_hbm, fin_hbm, bias_hbm, fout_hbm,
    en_ref, rn_ref, dn_ref, den_ref,
    est_ref, res_ref, dir_ref, ker_ref, w_ref, fin_ref, bias_ref, fout_ref, fetch_s,
    edge, edge_halo, kscr, kt, ktj, gf, gz, hb, hz, shifted, ishift, acc,
    part, rsbuf, iblk, iwin, part2, rsbuf2, sca, sca_in, ag, scb, ext,
    h_s, h_r, rs_s, rs_r, iw_s, in_s, iw_r, rt_s, rt_r, sa_s, sa_r, ag_s, ag_r, sb_s, sb_r,
):
    ci = lax.axis_index("comp")
    bi = lax.axis_index("band")
    up = lax.rem(bi + nb - 1, nb)
    down = lax.rem(bi + 1, nb)
    comps = w_ref.shape[0]
    half_nc = nc // 2

    def peers(fn):
        loop(1, nc, lambda d: fn(lax.rem(ci + d, nc)))

    def bands(fn):
        loop(1, nb, lambda d: fn(lax.rem(bi + d, nb)))

    fetches = [
        pltpu.make_async_copy(source, target, fetch_s.at[i])
        for i, (source, target) in enumerate((
            (ker_hbm, ker_ref), (dir_hbm, dir_ref), (w_hbm, w_ref), (res_hbm, res_ref),
            (est_hbm, est_ref), (fin_hbm, fin_ref), (bias_hbm, bias_ref), (fout_hbm, fout_ref)))
    ]
    for copy in fetches:
        copy.start()
    ends = []

    barrier = pltpu.get_barrier_semaphore()

    def greet(comp, band):
        pl.semaphore_signal(barrier, inc=1, device_id=(comp, band), device_id_type=MESH)

    def greet_both(c):
        greet(c, up)
        greet(c, down)
    loop(0, nc, greet_both)
    peers(lambda j: greet(j, bi))
    loop(2, nb - 1, lambda d: greet(ci, lax.rem(bi + d, nb)))

    size = 128
    kscr[...] = jnp.zeros_like(kscr)
    anti_r = lax.broadcasted_iota(jnp.int32, (size, size), 0)
    anti_c = lax.broadcasted_iota(jnp.int32, (size, size), 1)
    anti = (anti_r + anti_c == SPAN - 1).astype(BF16)
    fetches[0].wait()
    for a in range(SPAN):
        kscr[:, a, 0:SPAN] = ker_ref[a].astype(F32)
    for k in range(comps):
        turned = kscr[k].T
        kt[k] = turned
        ktj[k] = jnp.dot(turned.astype(BF16), anti, preferred_element_type=F32)

    fetches[1].wait()
    fetches[2].wait()
    direction = dir_ref[...]
    for k in range(comps):
        shaped = (w_ref[k].astype(F32) * direction).astype(BF16)
        for at, value in all_shifts(shaped):
            shifted[at, pl.ds(k * ROWS, ROWS), :] = value
    def band_matrix(table, k, b, first=0):
        row = table[k, pl.ds(b, 1), :]
        spread = jnp.broadcast_to(row, (ROWS, 128))
        return pltpu.roll(spread, first, 1, stride=1, stride_axis=0)

    left = lax.broadcasted_iota(jnp.int32, (ROWS, 128), 1) < ROWS

    def forward_pair(k, b):
        even = band_matrix(kt, k, b)
        odd = band_matrix(kt, k + 1, b, ROWS)
        lower = jnp.where(left, even, odd).astype(BF16)
        upper = jnp.where(left, odd, even).astype(BF16)
        return lower, upper

    def build_forward(s1):
        at = pl.ds(pl.multiple_of(s1 * ROWS, ROWS), ROWS)
        for side, sign in ((0, 1), (1, -1)):
            for s0 in range(FINE):
                b = HALF + sign * (1 + s0 + FINE * s1)
                for k in range(0, comps, 2):
                    lanes = pl.ds(s0 * comps * ROWS + k * ROWS, 128)
                    gf[side, 0, at, lanes], gf[side, 1, at, lanes] = forward_pair(k, b)
    loop(0, COARSE, build_forward)
    for k in range(0, comps, 2):
        gz[0, :, pl.ds(k * ROWS, 128)], gz[1, :, pl.ds(k * ROWS, 128)] = forward_pair(k, HALF)

    depth = comps * ROWS

    def taken(at, where):
        if where == 0:
            return shifted[at]
        return jnp.concatenate(
            [shifted[at, pl.ds((k ^ 1) * ROWS, ROWS), :] for k in range(comps)], axis=0)

    for where in range(2):
        total = jnp.dot(gz[where], taken(0, where), preferred_element_type=F32)
        for side, sign in ((0, 1), (1, -1)):
            source = jnp.concatenate(
                [taken(1 + side * FINE + s0, where) for s0 in range(FINE)], axis=0)
            acc[...] = jnp.dot(gf[side, where], source, preferred_element_type=F32)
            for s1 in range(COARSE):
                total += lane_shift(acc[pl.ds(s1 * ROWS, ROWS), :], sign * FINE * s1)
        base = 8 * (1 - where)
        for q in range(8):
            part[base + q] = total[8 * q:8 * q + 8]

    for copy in fetches[3:]:
        copy.wait()
    edge[0, 0] = est_ref[:8]
    edge[0, 1] = dir_ref[:8]
    edge[1, 0] = est_ref[ROWS - 8:]
    edge[1, 1] = dir_ref[ROWS - 8:]
    residual = res_ref[...]
    sca[...] = jnp.zeros_like(sca)
    sca[1:2] = fold(direction * direction)
    sca[2:3] = fold(residual * residual)
    pl.semaphore_wait(barrier, nc - 1 + 2 * nc + nb - 3)

    def rs_up(c):
        return remote(part.at[c], rsbuf.at[nc + ci], rs_s.at[c], rs_r.at[nc + ci], c + half_nc, up)

    def rs_down(c):
        return remote(
            part.at[12 + c], rsbuf.at[nc + ci], rs_s.at[12 + c], rs_r.at[nc + ci], c, down)

    def rs(j):
        return remote(part.at[4 + j], rsbuf.at[ci], rs_s.at[4 + j], rs_r.at[ci], j, bi)

    def rs_in(slot):
        return remote(part.at[0], rsbuf.at[slot], rs_s.at[0], rs_r.at[slot], ci, up)

    def start_far(c):
        rs_up(c).start()
        rs_down(c).start()
    loop(0, half_nc, start_far)
    peers(lambda j: rs(j).start())
    edges = [
        remote(edge.at[0], edge_halo.at[1], h_s.at[0], h_r.at[1], ci, up),
        remote(edge.at[1], edge_halo.at[0], h_s.at[1], h_r.at[0], ci, down),
    ]
    for copy in edges:
        copy.start()

    def end_far(c):
        rs_up(c).wait_send()
        rs_down(c).wait_send()
    ends.append(lambda: loop(0, half_nc, end_far))
    ends.append(lambda: peers(lambda j: rs(j).wait_send()))
    ends.extend(copy.wait_send for copy in edges)

    def build_back(s1):
        at = pl.ds(pl.multiple_of(s1 * ROWS, ROWS), ROWS)
        for side, sign in ((0, 1), (1, -1)):
            for s0 in range(FINE):
                b = HALF - sign * (1 + s0 + FINE * s1)
                for k in range(comps):
                    hb[side, k, at, pl.ds(s0 * 128, 128)] = band_matrix(ktj, k, b).astype(BF16)
    loop(0, COARSE, build_back)
    for k in range(comps):
        hz[k] = band_matrix(ktj, k, HALF).astype(BF16)

    rsbuf[ci] = part[4 + ci]
    peers(lambda j: rs_in(j).wait_recv())
    loop(0, nc, lambda j: rs_in(nc + j).wait_recv())
    far = lax.div(ci, half_nc)
    near = rsbuf[0]
    away = rsbuf[nc]
    for j in range(1, nc):
        near += rsbuf[j]
        away += rsbuf[nc + j]
    linked = ((bi > 0) | (far == 1)) & ((bi < nb - 1) | (far == 0))
    block = near + jnp.where(linked, away, 0.0)
    iblk[...] = block.astype(BF16).astype(F32)
    iwin[ci + 4] = iblk[...]
    far_band = lax.rem(bi + nb - 1 + 2 * far, nb)
    far_slot = ci + 12 - 16 * far

    def to_peer(j):
        return remote(iblk, iwin.at[ci + 4], iw_s.at[j], iw_r.at[ci + 4], j, bi)

    def to_far(j):
        return remote(iblk, iwin.at[far_slot], in_s.at[j], iw_r.at[far_slot], j, far_band)
    loop(0, nc, lambda j: to_far(j).start())
    peers(lambda j: to_peer(j).start())
    ends.append(lambda: peers(lambda j: to_peer(j).wait_send()))
    ends.append(lambda: loop(0, nc, lambda j: to_far(j).wait_send()))

    def window(at):
        return remote(iblk, iwin.at[at], iw_s.at[0], iw_r.at[at], ci, up)
    peers(lambda j: window(j + 4).wait_recv())

    def wait_far(j):
        window(j).wait_recv()
        window(j + 12).wait_recv()
    loop(0, 4, wait_far)

    inside = ((bi > 0).astype(F32), (bi < nb - 1).astype(F32))
    for r in range(0, 16, 2):
        pair = jnp.concatenate([iwin[r], iwin[r + 1]], axis=0)
        if r < 4:
            pair = pair * inside[0]
        if r >= 12:
            pair = pair * inside[1]
        for at, value in all_shifts(pair.astype(BF16)):
            ishift[at, pl.ds(8 * r, 16), :] = value

    rsum = jnp.zeros((ROWS, WIDTH), F32)
    for k in range(comps):
        back = jnp.dot(hz[k], ishift[0], preferred_element_type=F32)
        for side, sign in ((0, 1), (1, -1)):
            source = ishift[pl.ds(1 + side * FINE, FINE)].reshape(FINE * 128, WIDTH)
            acc[...] = jnp.dot(hb[side, k], source, preferred_element_type=F32)
            for s1 in range(COARSE):
                back += lane_shift(acc[pl.ds(s1 * ROWS, ROWS), :], sign * FINE * s1)
        rsum += w_ref[k].astype(F32) * back
    for j in range(8):
        part2[j] = rsum[8 * j:8 * j + 8]

    def rt(j, slot):
        return remote(part2.at[j], rsbuf2.at[slot], rt_s.at[j], rt_r.at[slot], j, bi)
    peers(lambda j: rt(j, ci).start())
    ends.append(lambda: peers(lambda j: rt(j, ci).wait_send()))
    sca[0:1] = fold(dir_ref[...] * rsum)

    def sa(b, slot):
        return remote(sca, sca_in.at[slot], sa_s.at[b], sa_r.at[slot], ci, b)
    bands(lambda b: sa(b, bi).start())
    ends.append(lambda: bands(lambda b: sa(b, bi).wait_send()))
    sca_in[bi] = sca[...]
    rsbuf2[ci] = part2[ci]

    peers(lambda j: rt(j, j).wait_recv())
    block = rsbuf2[0]
    for j in range(1, nc):
        block += rsbuf2[j]
    bands(lambda b: sa(b, b).wait_recv())
    scalars = sca_in[0]
    for b in range(1, nb):
        scalars += sca_in[b]
    ag[ci, 0] = block[:, :128]
    ag[ci, 1] = block[:, 128:]
    ag[ci, 2] = scalars

    def gather(j, slot):
        return remote(ag.at[ci], ag.at[slot], ag_s.at[j], ag_r.at[slot], j, bi)
    peers(lambda j: gather(j, ci).start())
    ends.append(lambda: peers(lambda j: gather(j, ci).wait_send()))
    peers(lambda j: gather(j, j).wait_recv())

    product = ag[0, 2, 0:1]
    for j in range(1, nc):
        product += ag[j, 2, 0:1]
    product = product + DAMPING * ag[0, 2, 1:2]
    old = jnp.sum(ag[0, 2, 2:3], axis=1, keepdims=True)
    alpha = old / jnp.sum(product, axis=1, keepdims=True)

    for j in range(8):
        for c in range(2):
            at = (slice(8 * j, 8 * j + 8), slice(128 * c, 128 * c + 128))
            rn_ref[at] = res_ref[at] - alpha * (ag[j, c] + DAMPING * dir_ref[at])
    updated = rn_ref[...]
    scb[nb] = jnp.broadcast_to(fold(updated * updated), (8, 128))

    def sb(b, slot):
        return remote(scb.at[nb], scb.at[slot], sb_s.at[b], sb_r.at[slot], ci, b)
    bands(lambda b: sb(b, bi).start())
    ends.append(lambda: bands(lambda b: sb(b, bi).wait_send()))
    scb[bi] = scb[nb]
    for copy in edges:
        copy.wait_recv()

    estimate_next = est_ref[...] + alpha * dir_ref[...]
    en_ref[...] = estimate_next
    ext[0:8] = (edge_halo[0, 0] + alpha * edge_halo[0, 1]) * inside[0]
    ext[8:72] = estimate_next
    ext[72:80] = (edge_halo[1, 0] + alpha * edge_halo[1, 1]) * inside[1]
    framed = ext[...]
    columns = WIDTH // nc
    start = ci * columns
    pick_r = lax.broadcasted_iota(jnp.int32, (WIDTH, 128), 0)
    pick_c = lax.broadcasted_iota(jnp.int32, (WIDTH, 128), 1)
    group = (pick_c >= GROUP).astype(jnp.int32) + (pick_c >= 2 * GROUP).astype(jnp.int32)
    pick = (pick_r == start - 2 + pick_c - GROUP * group).astype(BF16)
    high = framed.astype(BF16)
    rest = framed - high.astype(F32)
    middle = rest.astype(BF16)
    low = (rest - middle.astype(F32)).astype(BF16)
    tile = (
        jnp.dot(high, pick, preferred_element_type=F32)
        + jnp.dot(middle, pick, preferred_element_type=F32)
        + jnp.dot(low, pick, preferred_element_type=F32)
    )
    tile = jnp.concatenate([tile[6:80], jnp.zeros((14, 128), F32)], axis=0)
    lane = lax.broadcasted_iota(jnp.int32, (24, 128), 1)
    row = lax.broadcasted_iota(jnp.int32, (24, 128), 0)
    third = (lane >= GROUP).astype(jnp.int32) + (lane >= 2 * GROUP).astype(jnp.int32)
    taps = []
    for a in range(3):
        packed = jnp.where(
            third == 0, tile[a:a + 24], jnp.where(third == 1, tile[24 + a:48 + a], tile[48 + a:72 + a]))
        for b in range(3):
            taps.append(packed if b == 0 else pltpu.roll(packed, 128 - b, 1))
    image_row = bi * ROWS - 1 + row + 24 * third
    image_col = start - 1 + lane - GROUP * third
    valid = (image_row >= 0) & (image_row < nb * ROWS) & (image_col >= 0) & (image_col < WIDTH)
    channels = bias_ref.shape[0]
    spreads = []
    for part_of in range(3):
        rows = slice(8 * part_of, 8 * part_of + 8)
        mine = [tap[rows] for tap in taps]

        def channel(c, sums):
            value = mine[0] * fin_ref[0, 0, c] + bias_ref[c]
            for t in range(1, 9):
                value += mine[t] * fin_ref[t // 3, t % 3, c]
            value = jnp.maximum(value, 0.0)
            return tuple(sums[t] + value * fout_ref[t // 3, t % 3, c] for t in range(9))

        sums = lax.fori_loop(
            0, channels, channel, tuple(jnp.zeros((8, 128), F32) for t in range(9)), unroll=unroll)
        spreads.append(sums)
    mixed = jnp.zeros((ROWS, 128), F32)
    for t in range(9):
        a, b = t // 3, t % 3
        whole = jnp.where(valid, jnp.concatenate([s[t] for s in spreads], axis=0), 0.0)
        column = jnp.concatenate(
            [pltpu.roll(whole, (128 - GROUP * g - b) % 128, 1) for g in range(3)], axis=0)
        mixed += column[a:a + ROWS]
    centre = pltpu.roll(tile[2:2 + ROWS], 126, 1)
    den_ref[...] = (centre - mixed).T[:columns]

    bands(lambda b: sb(b, b).wait_recv())
    new = scb[0, 0:1]
    for b in range(1, nb):
        new += scb[b, 0:1]
    new = jnp.sum(new, axis=1, keepdims=True)
    dn_ref[...] = rn_ref[...] + (new / old) * dir_ref[...]

    for end in ends:
        end()


def place(*refs):
    count = len(refs) // 2
    sources, targets, sems = refs[:count], refs[count:2 * count], refs[-1]
    copies = [
        pltpu.make_async_copy(source, target, sems.at[i])
        for i, (source, target) in enumerate(zip(sources, targets))
    ]
    for copy in copies:
        copy.start()
    for copy in copies:
        copy.wait()


def per_device(nc, nb, unroll, estimate, residual, direction, kernels, weight_maps, filters_in, biases, filters_out):
    comps = weight_maps.shape[0]
    columns = WIDTH // nc
    vmem = pl.BlockSpec(memory_space=pltpu.VMEM)
    hbm = pl.BlockSpec(memory_space=pltpu.HBM)
    anywhere = pl.BlockSpec(memory_space=pl.ANY)
    band = jax.ShapeDtypeStruct((ROWS, WIDTH), F32)
    shapes = (band, band, band, jax.ShapeDtypeStruct((columns, ROWS), F32))
    dma = pltpu.SemaphoreType.DMA
    results = pl.pallas_call(
        functools.partial(kernel, nc, nb, unroll),
        out_shape=shapes,
        in_specs=[hbm] * 8,
        out_specs=(vmem,) * 4,
        scratch_shapes=[
            pltpu.VMEM((ROWS, WIDTH), F32),
            pltpu.VMEM((ROWS, WIDTH), F32),
            pltpu.VMEM((ROWS, WIDTH), F32),
            pltpu.VMEM((SPAN, comps, SPAN), BF16),
            pltpu.VMEM((comps, ROWS, WIDTH), BF16),
            pltpu.SMEM((3, 3, filters_in.shape[0]), F32),
            pltpu.SMEM(biases.shape, F32),
            pltpu.SMEM((3, 3, filters_in.shape[0]), F32),
            dma((8,)),
            pltpu.VMEM((2, 2, 8, WIDTH), F32),
            pltpu.VMEM((2, 2, 8, WIDTH), F32),
            pltpu.VMEM((comps, 128, 128), F32),
            pltpu.VMEM((comps, 128, 128), F32),
            pltpu.VMEM((comps, 128, 128), F32),
            pltpu.VMEM((2, 2, COARSE * ROWS, FINE * comps * ROWS), BF16),
            pltpu.VMEM((2, ROWS, comps * ROWS), BF16),
            pltpu.VMEM((2, comps, COARSE * ROWS, FINE * 128), BF16),
            pltpu.VMEM((comps, ROWS, 128), BF16),
            pltpu.VMEM((1 + 2 * FINE, comps * ROWS, WIDTH), BF16),
            pltpu.VMEM((1 + 2 * FINE, 128, WIDTH), BF16),
            pltpu.VMEM((COARSE * ROWS, WIDTH), F32),
            pltpu.VMEM((16, 8, WIDTH), F32),
            pltpu.VMEM((2 * nc, 8, WIDTH), F32),
            pltpu.VMEM((8, WIDTH), F32),
            pltpu.VMEM((16, 8, WIDTH), F32),
            pltpu.VMEM((8, 8, WIDTH), F32),
            pltpu.VMEM((8, 8, WIDTH), F32),
            pltpu.VMEM((8, 128), F32),
            pltpu.VMEM((nb, 8, 128), F32),
            pltpu.VMEM((nc, 3, 8, 128), F32),
            pltpu.VMEM((nb + 1, 8, 128), F32),
            pltpu.VMEM((80, WIDTH), F32),
            dma((2,)), dma((2,)),
            dma((16,)), dma((2 * nc,)),
            dma((nc,)), dma((nc,)), dma((16,)),
            dma((nc,)), dma((nc,)),
            dma((nb,)), dma((nb,)),
            dma((nc,)), dma((nc,)),
            dma((nb,)), dma((nb,)),
        ],
        compiler_params=pltpu.CompilerParams(
            collective_id=0, has_side_effects=True, vmem_limit_bytes=48 * 1024 * 1024),
        cost_estimate=pl.CostEstimate(
            flops=4 * 65 * comps * 64 * 128 * 256, bytes_accessed=1 << 20, transcendentals=0),
    )(*(pltpu.with_memory_space_constraint(x, pltpu.HBM) for x in (
        estimate, residual, direction, kernels.transpose(1, 0, 2), weight_maps,
        filters_in.transpose(1, 2, 0), biases, filters_out.transpose(1, 2, 0))))
    estimate_next, residual_next, direction_next, turned = pl.pallas_call(
        place,
        out_shape=shapes,
        in_specs=[vmem] * 4,
        out_specs=(anywhere,) * 4,
        scratch_shapes=[dma((4,))],
        compiler_params=pltpu.CompilerParams(vmem_limit_bytes=4 * 1024 * 1024),
    )(*results)
    return estimate_next, residual_next, direction_next, turned.T


def solution(mesh):
    nc, nb = mesh.shape["comp"], mesh.shape["band"]
    return jax.shard_map(
        functools.partial(per_device, nc, nb, 4),
        mesh=mesh,
        in_specs=(
            P("band", None),
            P("band", None),
            P("band", None),
            P("comp", None, None),
            P("comp", "band", None),
            P(),
            P(),
            P(),
        ),
        out_specs=(P("band", None), P("band", None), P("band", None), P("band", "comp")),
        check_vma=False,
    )
```

```python
import functools

import jax
import jax.numpy as jnp
from jax import lax
from jax.experimental import pallas as pl
from jax.experimental.pallas import tpu as pltpu
from jax.sharding import PartitionSpec as P

MESH = pl.DeviceIdType.MESH
F32 = jnp.float32
BF16 = jnp.bfloat16
DAMPING = 0.5
HALF = 32
SPAN = 65
ROWS = 64
WIDTH = 256
FINE = 4
COARSE = 8
BACK_FINE = 8
BACK_COARSE = 4
GROUP = 40


def lane_shift(x, n):
    if n == 0:
        return x
    width = x.shape[1]
    col = lax.broadcasted_iota(jnp.int32, x.shape, 1)
    keep = col < width - n if n > 0 else col >= -n
    return jnp.where(keep, pltpu.roll(x, (-n) % width, 1), jnp.zeros((), x.dtype))


def fold(x):
    x = jnp.sum(x, axis=0, keepdims=True)
    return x[:, :128] + x[:, 128:]


def all_shifts(x):
    yield 0, x
    for s0 in range(BACK_FINE):
        yield 1 + s0, lane_shift(x, 1 + s0)
        yield 1 + BACK_FINE + s0, lane_shift(x, -1 - s0)


def swap_pairs(x):
    return jnp.concatenate(
        [x[(k ^ 1) * ROWS:(k ^ 1) * ROWS + ROWS] for k in range(x.shape[0] // ROWS)], axis=0)


def far_first(fns):
    for hops, fn in sorted(fns, key=lambda pair: -pair[0]):
        fn()


def loop(low, high, fn):
    def body(i, carry):
        fn(i)
        return carry
    lax.fori_loop(low, high, body, 0)


def remote(src, dst, send, recv, comp, band):
    return pltpu.make_async_remote_copy(
        src_ref=src, dst_ref=dst, send_sem=send, recv_sem=recv,
        device_id=(comp, band), device_id_type=MESH,
    )


def kernel(
    nc, nb, unroll,
    est_hbm, res_hbm, dir_hbm, ker_hbm, w_hbm, fin_hbm, bias_hbm, fout_hbm,
    en_ref, rn_ref, dn_ref, den_ref,
    est_ref, res_ref, dir_ref, ker_ref, w_ref, fin_ref, bias_ref, fout_ref, fetch_s,
    edge, edge_halo, kscr, kt, ktj, facc, shaped, hb, hz, ishift, acc,
    part, rsbuf, iblk, iwin, part2, rsbuf2, sca, sca_in, ag, scb, ext,
    h_s, h_r, rs_s, rs_r, iw_s, in_s, iw_r, rt_s, rt_r, sa_s, sa_r, ag_s, ag_r, sb_s, sb_r,
):
    ci = lax.axis_index("comp")
    bi = lax.axis_index("band")
    up = lax.rem(bi + nb - 1, nb)
    down = lax.rem(bi + 1, nb)
    comps = w_ref.shape[0]
    half_nc = nc // 2

    def peers(fn):
        loop(1, nc, lambda d: fn(lax.rem(ci + d, nc)))

    def bands(fn):
        loop(1, nb, lambda d: fn(lax.rem(bi + d, nb)))

    def ring(d, n):
        return min(d, n - d)

    xs = nc // 2
    far_peers = [
        (ring(dx, xs) + 2 * dz,
         lax.rem(lax.div(ci, 2) + dx, xs) * 2 + lax.rem(ci + dz, 2))
        for dx in range(xs) for dz in range(2) if dx or dz
    ]
    if nb % 4 == 0:
        ys = nb // 4
        far_bands = [
            (ring(dy, ys) + dz + dc / 2,
             lax.rem(lax.div(bi, 2 * ys) + dz, 2) * 2 * ys
             + lax.rem(lax.rem(lax.div(bi, 2), ys) + dy, ys) * 2 + lax.rem(bi + dc, 2))
            for dz in range(2) for dy in range(ys) for dc in range(2) if dz or dy or dc
        ]
    else:
        far_bands = [(1, lax.rem(bi + d, nb)) for d in range(1, nb)]

    def to_peers(fn):
        return [(hops, lambda j=j: fn(j)) for hops, j in far_peers]

    def to_bands(fn):
        return [(hops, lambda b=b: fn(b)) for hops, b in far_bands]

    fetches = [
        pltpu.make_async_copy(source, target, fetch_s.at[i])
        for i, (source, target) in enumerate((
            (ker_hbm, ker_ref), (dir_hbm, dir_ref), (w_hbm, w_ref), (res_hbm, res_ref),
            (est_hbm, est_ref), (fin_hbm, fin_ref), (bias_hbm, bias_ref), (fout_hbm, fout_ref)))
    ]
    for copy in fetches:
        copy.start()
    ends = []

    barrier = pltpu.get_barrier_semaphore()

    def greet(comp, band):
        pl.semaphore_signal(barrier, inc=1, device_id=(comp, band), device_id_type=MESH)

    def greet_both(c):
        greet(c, up)
        greet(c, down)
    loop(0, nc, greet_both)
    peers(lambda j: greet(j, bi))
    loop(2, nb - 1, lambda d: greet(ci, lax.rem(bi + d, nb)))

    kscr[...] = jnp.zeros_like(kscr)
    fetches[0].wait()
    for a in range(SPAN):
        kscr[:, a, 0:SPAN] = ker_ref[a].astype(F32)
    for k in range(comps):
        kt[k] = kscr[k].T

    fetches[1].wait()
    fetches[2].wait()
    direction = dir_ref[...]
    for k in range(comps):
        shaped[pl.ds(k * ROWS, ROWS), :] = (w_ref[k].astype(F32) * direction).astype(BF16)

    def band_matrix(table, k, b, first=0):
        row = table[k, pl.ds(b, 1), :]
        spread = jnp.broadcast_to(row, (ROWS, 128))
        return pltpu.roll(spread, first, 1, stride=1, stride_axis=0)

    left = lax.broadcasted_iota(jnp.int32, (ROWS, 128), 1) < ROWS

    def forward_pair(k, b):
        even = band_matrix(kt, k, b)
        odd = band_matrix(kt, k + 1, b, ROWS)
        lower = jnp.where(left, even, odd).astype(BF16)
        upper = jnp.where(left, odd, even).astype(BF16)
        return lower, upper

    def forward_matrices(columns):
        lower, upper = [], []
        for b in columns:
            pairs = [forward_pair(k, b) for k in range(0, comps, 2)]
            lower.append(jnp.concatenate([pair[0] for pair in pairs], axis=1))
            upper.append(jnp.concatenate([pair[1] for pair in pairs], axis=1))
        return jnp.concatenate(lower, axis=0), jnp.concatenate(upper, axis=0)

    for s0 in range(FINE):
        for side, sign in ((0, 1), (1, -1)):
            source = lane_shift(shaped[...], sign * (1 + s0))
            lower, upper = forward_matrices(
                [HALF + sign * (1 + s0 + FINE * s1) for s1 in range(COARSE)])
            for where, matrix, rows in ((0, lower, source), (1, upper, swap_pairs(source))):
                product = jnp.dot(matrix, rows, preferred_element_type=F32)
                if s0 == 0:
                    facc[side, where] = product
                else:
                    facc[side, where] += product
    lower, upper = forward_matrices([HALF])
    for where, matrix, rows in ((0, lower, shaped[...]), (1, upper, swap_pairs(shaped[...]))):
        total = jnp.dot(matrix, rows, preferred_element_type=F32)
        for side, sign in ((0, 1), (1, -1)):
            for s1 in range(COARSE):
                total += lane_shift(
                    facc[side, where, pl.ds(s1 * ROWS, ROWS), :], sign * FINE * s1)
        base = 8 * (1 - where)
        for q in range(8):
            part[base + q] = total[8 * q:8 * q + 8]

    for copy in fetches[3:]:
        copy.wait()
    edge[0, 0] = est_ref[:8]
    edge[0, 1] = dir_ref[:8]
    edge[1, 0] = est_ref[ROWS - 8:]
    edge[1, 1] = dir_ref[ROWS - 8:]
    residual = res_ref[...]
    sca[...] = jnp.zeros_like(sca)
    sca[1:2] = fold(direction * direction)
    sca[2:3] = fold(residual * residual)
    pl.semaphore_wait(barrier, nc - 1 + 2 * nc + nb - 3)

    def rs_up(c):
        return remote(part.at[c], rsbuf.at[nc + ci], rs_s.at[c], rs_r.at[nc + ci], c + half_nc, up)

    def rs_down(c):
        return remote(
            part.at[12 + c], rsbuf.at[nc + ci], rs_s.at[12 + c], rs_r.at[nc + ci], c, down)

    def rs(j):
        return remote(part.at[4 + j], rsbuf.at[ci], rs_s.at[4 + j], rs_r.at[ci], j, bi)

    def rs_in(slot):
        return remote(part.at[0], rsbuf.at[slot], rs_s.at[0], rs_r.at[slot], ci, up)

    def start_far(c):
        rs_up(c).start()
        rs_down(c).start()
    loop(0, half_nc, start_far)
    far_first(to_peers(lambda j: rs(j).start()))
    edges = [
        remote(edge.at[0], edge_halo.at[1], h_s.at[0], h_r.at[1], ci, up),
        remote(edge.at[1], edge_halo.at[0], h_s.at[1], h_r.at[0], ci, down),
    ]
    for copy in edges:
        copy.start()

    def end_far(c):
        rs_up(c).wait_send()
        rs_down(c).wait_send()
    ends.append(lambda: loop(0, half_nc, end_far))
    ends.append(lambda: peers(lambda j: rs(j).wait_send()))
    ends.extend(copy.wait_send for copy in edges)

    size = 128
    anti_r = lax.broadcasted_iota(jnp.int32, (size, size), 0)
    anti_c = lax.broadcasted_iota(jnp.int32, (size, size), 1)
    anti = (anti_r + anti_c == SPAN - 1).astype(BF16)
    for k in range(comps):
        ktj[k] = jnp.dot(kt[k].astype(BF16), anti, preferred_element_type=F32)

    def build_back(s1):
        at = pl.ds(pl.multiple_of(s1 * ROWS, ROWS), ROWS)
        for side, sign in ((0, 1), (1, -1)):
            for s0 in range(BACK_FINE):
                b = HALF - sign * (1 + s0 + BACK_FINE * s1)
                for k in range(comps):
                    hb[side, k, at, pl.ds(s0 * 128, 128)] = band_matrix(ktj, k, b).astype(BF16)
    loop(0, BACK_COARSE, build_back)
    for k in range(comps):
        hz[k] = band_matrix(ktj, k, HALF).astype(BF16)

    rsbuf[ci] = part[4 + ci]
    peers(lambda j: rs_in(j).wait_recv())
    loop(0, nc, lambda j: rs_in(nc + j).wait_recv())
    far = lax.div(ci, half_nc)
    near = rsbuf[0]
    away = rsbuf[nc]
    for j in range(1, nc):
        near += rsbuf[j]
        away += rsbuf[nc + j]
    linked = ((bi > 0) | (far == 1)) & ((bi < nb - 1) | (far == 0))
    block = near + jnp.where(linked, away, 0.0)
    iblk[...] = jnp.concatenate([block[:, :128], block[:, 128:]], axis=0).astype(BF16)
    iwin[ci + 4] = iblk[...]
    far_band = lax.rem(bi + nb - 1 + 2 * far, nb)
    far_slot = ci + 12 - 16 * far

    def to_peer(j):
        return remote(iblk, iwin.at[ci + 4], iw_s.at[j], iw_r.at[ci + 4], j, bi)

    def to_far(j):
        return remote(iblk, iwin.at[far_slot], in_s.at[j], iw_r.at[far_slot], j, far_band)
    loop(0, nc, lambda j: to_far(j).start())
    far_first(to_peers(lambda j: to_peer(j).start()))
    ends.append(lambda: peers(lambda j: to_peer(j).wait_send()))
    ends.append(lambda: loop(0, nc, lambda j: to_far(j).wait_send()))

    def window(at):
        return remote(iblk, iwin.at[at], iw_s.at[0], iw_r.at[at], ci, up)
    peers(lambda j: window(j + 4).wait_recv())

    def wait_far(j):
        window(j).wait_recv()
        window(j + 12).wait_recv()
    loop(0, 4, wait_far)

    inside = ((bi > 0).astype(F32), (bi < nb - 1).astype(F32))
    for r in range(0, 16, 2):
        first, second = iwin[r].astype(F32), iwin[r + 1].astype(F32)
        pair = jnp.concatenate([
            jnp.concatenate([first[:8], first[8:]], axis=1),
            jnp.concatenate([second[:8], second[8:]], axis=1)], axis=0)
        if r < 4:
            pair = pair * inside[0]
        if r >= 12:
            pair = pair * inside[1]
        for at, value in all_shifts(pair.astype(BF16)):
            ishift[at, pl.ds(8 * r, 16), :] = value

    rsum = jnp.zeros((ROWS, WIDTH), F32)
    for k in range(comps):
        back = jnp.dot(hz[k], ishift[0], preferred_element_type=F32)
        for side, sign in ((0, 1), (1, -1)):
            source = ishift[pl.ds(1 + side * BACK_FINE, BACK_FINE)].reshape(BACK_FINE * 128, WIDTH)
            acc[...] = jnp.dot(hb[side, k], source, preferred_element_type=F32)
            for s1 in range(BACK_COARSE):
                back += lane_shift(acc[pl.ds(s1 * ROWS, ROWS), :], sign * BACK_FINE * s1)
        rsum += w_ref[k].astype(F32) * back
    for j in range(8):
        part2[j] = rsum[8 * j:8 * j + 8]

    def rt(j, slot):
        return remote(part2.at[j], rsbuf2.at[slot], rt_s.at[j], rt_r.at[slot], j, bi)
    ends.append(lambda: peers(lambda j: rt(j, ci).wait_send()))
    sca[0:1] = fold(dir_ref[...] * rsum)

    def sa(b, slot):
        return remote(sca, sca_in.at[slot], sa_s.at[b], sa_r.at[slot], ci, b)
    far_first(to_peers(lambda j: rt(j, ci).start()) + to_bands(lambda b: sa(b, bi).start()))
    ends.append(lambda: bands(lambda b: sa(b, bi).wait_send()))
    sca_in[bi] = sca[...]
    rsbuf2[ci] = part2[ci]

    peers(lambda j: rt(j, j).wait_recv())
    block = rsbuf2[0]
    for j in range(1, nc):
        block += rsbuf2[j]
    bands(lambda b: sa(b, b).wait_recv())
    scalars = sca_in[0]
    for b in range(1, nb):
        scalars += sca_in[b]
    ag[ci, 0] = block[:, :128]
    ag[ci, 1] = block[:, 128:]
    ag[ci, 2] = scalars

    def gather(j, slot):
        return remote(ag.at[ci], ag.at[slot], ag_s.at[j], ag_r.at[slot], j, bi)
    far_first(to_peers(lambda j: gather(j, ci).start()))
    ends.append(lambda: peers(lambda j: gather(j, ci).wait_send()))
    peers(lambda j: gather(j, j).wait_recv())

    product = ag[0, 2, 0:1]
    for j in range(1, nc):
        product += ag[j, 2, 0:1]
    product = product + DAMPING * ag[0, 2, 1:2]
    old = jnp.sum(ag[0, 2, 2:3], axis=1, keepdims=True)
    alpha = old / jnp.sum(product, axis=1, keepdims=True)

    for j in range(8):
        for c in range(2):
            at = (slice(8 * j, 8 * j + 8), slice(128 * c, 128 * c + 128))
            rn_ref[at] = res_ref[at] - alpha * (ag[j, c] + DAMPING * dir_ref[at])
    updated = rn_ref[...]
    scb[nb] = jnp.broadcast_to(fold(updated * updated), (8, 128))

    def sb(b, slot):
        return remote(scb.at[nb], scb.at[slot], sb_s.at[b], sb_r.at[slot], ci, b)
    far_first(to_bands(lambda b: sb(b, bi).start()))
    ends.append(lambda: bands(lambda b: sb(b, bi).wait_send()))
    scb[bi] = scb[nb]
    for copy in edges:
        copy.wait_recv()

    estimate_next = est_ref[...] + alpha * dir_ref[...]
    en_ref[...] = estimate_next
    ext[0:8] = (edge_halo[0, 0] + alpha * edge_halo[0, 1]) * inside[0]
    ext[8:72] = estimate_next
    ext[72:80] = (edge_halo[1, 0] + alpha * edge_halo[1, 1]) * inside[1]
    framed = ext[...]
    columns = WIDTH // nc
    start = ci * columns
    pick_r = lax.broadcasted_iota(jnp.int32, (WIDTH, 128), 0)
    pick_c = lax.broadcasted_iota(jnp.int32, (WIDTH, 128), 1)
    group = (pick_c >= GROUP).astype(jnp.int32) + (pick_c >= 2 * GROUP).astype(jnp.int32)
    pick = (pick_r == start - 2 + pick_c - GROUP * group).astype(BF16)
    high = framed.astype(BF16)
    rest = framed - high.astype(F32)
    middle = rest.astype(BF16)
    low = (rest - middle.astype(F32)).astype(BF16)
    tile = (
        jnp.dot(high, pick, preferred_element_type=F32)
        + jnp.dot(middle, pick, preferred_element_type=F32)
        + jnp.dot(low, pick, preferred_element_type=F32)
    )
    tile = jnp.concatenate([tile[6:80], jnp.zeros((14, 128), F32)], axis=0)
    lane = lax.broadcasted_iota(jnp.int32, (24, 128), 1)
    row = lax.broadcasted_iota(jnp.int32, (24, 128), 0)
    third = (lane >= GROUP).astype(jnp.int32) + (lane >= 2 * GROUP).astype(jnp.int32)
    taps = []
    for a in range(3):
        packed = jnp.where(
            third == 0, tile[a:a + 24], jnp.where(third == 1, tile[24 + a:48 + a], tile[48 + a:72 + a]))
        for b in range(3):
            taps.append(packed if b == 0 else pltpu.roll(packed, 128 - b, 1))
    image_row = bi * ROWS - 1 + row + 24 * third
    image_col = start - 1 + lane - GROUP * third
    valid = (image_row >= 0) & (image_row < nb * ROWS) & (image_col >= 0) & (image_col < WIDTH)
    channels = bias_ref.shape[0]
    spreads = []
    for part_of in range(3):
        rows = slice(8 * part_of, 8 * part_of + 8)
        mine = [tap[rows] for tap in taps]

        def channel(c, sums):
            value = mine[0] * fin_ref[0, 0, c] + bias_ref[c]
            for t in range(1, 9):
                value += mine[t] * fin_ref[t // 3, t % 3, c]
            value = jnp.maximum(value, 0.0)
            return tuple(sums[t] + value * fout_ref[t // 3, t % 3, c] for t in range(9))

        sums = lax.fori_loop(
            0, channels, channel, tuple(jnp.zeros((8, 128), F32) for t in range(9)), unroll=unroll)
        spreads.append(sums)
    mixed = jnp.zeros((ROWS, 128), F32)
    for t in range(9):
        a, b = t // 3, t % 3
        whole = jnp.where(valid, jnp.concatenate([s[t] for s in spreads], axis=0), 0.0)
        column = jnp.concatenate(
            [pltpu.roll(whole, (128 - GROUP * g - b) % 128, 1) for g in range(3)], axis=0)
        mixed += column[a:a + ROWS]
    centre = pltpu.roll(tile[2:2 + ROWS], 126, 1)
    den_ref[...] = (centre - mixed).T[:columns]

    bands(lambda b: sb(b, b).wait_recv())
    new = scb[0, 0:1]
    for b in range(1, nb):
        new += scb[b, 0:1]
    new = jnp.sum(new, axis=1, keepdims=True)
    dn_ref[...] = rn_ref[...] + (new / old) * dir_ref[...]

    for end in ends:
        end()


def place(*refs):
    count = len(refs) // 2
    sources, targets, sems = refs[:count], refs[count:2 * count], refs[-1]
    copies = [
        pltpu.make_async_copy(source, target, sems.at[i])
        for i, (source, target) in enumerate(zip(sources, targets))
    ]
    for copy in copies:
        copy.start()
    for copy in copies:
        copy.wait()


def per_device(nc, nb, unroll, estimate, residual, direction, kernels, weight_maps, filters_in, biases, filters_out):
    comps = weight_maps.shape[0]
    columns = WIDTH // nc
    vmem = pl.BlockSpec(memory_space=pltpu.VMEM)
    hbm = pl.BlockSpec(memory_space=pltpu.HBM)
    anywhere = pl.BlockSpec(memory_space=pl.ANY)
    band = jax.ShapeDtypeStruct((ROWS, WIDTH), F32)
    shapes = (band, band, band, jax.ShapeDtypeStruct((columns, ROWS), F32))
    dma = pltpu.SemaphoreType.DMA
    results = pl.pallas_call(
        functools.partial(kernel, nc, nb, unroll),
        out_shape=shapes,
        in_specs=[hbm] * 8,
        out_specs=(vmem,) * 4,
        scratch_shapes=[
            pltpu.VMEM((ROWS, WIDTH), F32),
            pltpu.VMEM((ROWS, WIDTH), F32),
            pltpu.VMEM((ROWS, WIDTH), F32),
            pltpu.VMEM((SPAN, comps, SPAN), BF16),
            pltpu.VMEM((comps, ROWS, WIDTH), BF16),
            pltpu.SMEM((3, 3, filters_in.shape[0]), F32),
            pltpu.SMEM(biases.shape, F32),
            pltpu.SMEM((3, 3, filters_in.shape[0]), F32),
            dma((8,)),
            pltpu.VMEM((2, 2, 8, WIDTH), F32),
            pltpu.VMEM((2, 2, 8, WIDTH), F32),
            pltpu.VMEM((comps, 128, 128), F32),
            pltpu.VMEM((comps, 128, 128), F32),
            pltpu.VMEM((comps, 128, 128), F32),
            pltpu.VMEM((2, 2, COARSE * ROWS, WIDTH), F32),
            pltpu.VMEM((comps * ROWS, WIDTH), BF16),
            pltpu.VMEM((2, comps, BACK_COARSE * ROWS, BACK_FINE * 128), BF16),
            pltpu.VMEM((comps, ROWS, 128), BF16),
            pltpu.VMEM((1 + 2 * BACK_FINE, 128, WIDTH), BF16),
            pltpu.VMEM((BACK_COARSE * ROWS, WIDTH), F32),
            pltpu.VMEM((16, 8, WIDTH), F32),
            pltpu.VMEM((2 * nc, 8, WIDTH), F32),
            pltpu.VMEM((16, 128), BF16),
            pltpu.VMEM((16, 16, 128), BF16),
            pltpu.VMEM((8, 8, WIDTH), F32),
            pltpu.VMEM((8, 8, WIDTH), F32),
            pltpu.VMEM((8, 128), F32),
            pltpu.VMEM((nb, 8, 128), F32),
            pltpu.VMEM((nc, 3, 8, 128), F32),
            pltpu.VMEM((nb + 1, 8, 128), F32),
            pltpu.VMEM((80, WIDTH), F32),
            dma((2,)), dma((2,)),
            dma((16,)), dma((2 * nc,)),
            dma((nc,)), dma((nc,)), dma((16,)),
            dma((nc,)), dma((nc,)),
            dma((nb,)), dma((nb,)),
            dma((nc,)), dma((nc,)),
            dma((nb,)), dma((nb,)),
        ],
        compiler_params=pltpu.CompilerParams(
            collective_id=0, has_side_effects=True, vmem_limit_bytes=48 * 1024 * 1024),
        cost_estimate=pl.CostEstimate(
            flops=4 * 65 * comps * 64 * 128 * 256, bytes_accessed=1 << 20, transcendentals=0),
    )(*(pltpu.with_memory_space_constraint(x, pltpu.HBM) for x in (
        estimate, residual, direction, kernels.transpose(1, 0, 2), weight_maps,
        filters_in.transpose(1, 2, 0), biases, filters_out.transpose(1, 2, 0))))
    estimate_next, residual_next, direction_next, turned = pl.pallas_call(
        place,
        out_shape=shapes,
        in_specs=[vmem] * 4,
        out_specs=(anywhere,) * 4,
        scratch_shapes=[dma((4,))],
        compiler_params=pltpu.CompilerParams(vmem_limit_bytes=4 * 1024 * 1024),
    )(*results)
    return estimate_next, residual_next, direction_next, turned.T


def solution(mesh):
    nc, nb = mesh.shape["comp"], mesh.shape["band"]
    return jax.shard_map(
        functools.partial(per_device, nc, nb, 4),
        mesh=mesh,
        in_specs=(
            P("band", None),
            P("band", None),
            P("band", None),
            P("comp", None, None),
            P("comp", "band", None),
            P(),
            P(),
            P(),
        ),
        out_specs=(P("band", None), P("band", None), P("band", None), P("band", "comp")),
        check_vma=False,
    )
```

```python
import functools

import jax
import jax.numpy as jnp
from jax import lax
from jax.experimental import pallas as pl
from jax.experimental.pallas import tpu as pltpu
from jax.sharding import PartitionSpec as P

MESH = pl.DeviceIdType.MESH
F32 = jnp.float32
BF16 = jnp.bfloat16
DAMPING = 0.5
HALF = 32
SPAN = 65
ROWS = 64
WIDTH = 256
FINE = 4
COARSE = 8
BACK_FINE = 8
BACK_COARSE = 4
GROUP = 40


def lane_shift(x, n):
    if n == 0:
        return x
    width = x.shape[1]
    col = lax.broadcasted_iota(jnp.int32, x.shape, 1)
    keep = col < width - n if n > 0 else col >= -n
    return jnp.where(keep, pltpu.roll(x, (-n) % width, 1), jnp.zeros((), x.dtype))


def fold(x):
    x = jnp.sum(x, axis=0, keepdims=True)
    return x[:, :128] + x[:, 128:]


def all_shifts(x):
    yield 0, x
    for s0 in range(BACK_FINE):
        yield 1 + s0, lane_shift(x, 1 + s0)
        yield 1 + BACK_FINE + s0, lane_shift(x, -1 - s0)


def swap_pairs(x):
    return jnp.concatenate(
        [x[(k ^ 1) * ROWS:(k ^ 1) * ROWS + ROWS] for k in range(x.shape[0] // ROWS)], axis=0)


def far_first(fns):
    for hops, fn in sorted(fns, key=lambda pair: -pair[0]):
        fn()


def loop(low, high, fn):
    def body(i, carry):
        fn(i)
        return carry
    lax.fori_loop(low, high, body, 0)


def remote(src, dst, send, recv, comp, band):
    return pltpu.make_async_remote_copy(
        src_ref=src, dst_ref=dst, send_sem=send, recv_sem=recv,
        device_id=(comp, band), device_id_type=MESH,
    )


def kernel(
    nc, nb, unroll,
    est_hbm, res_hbm, dir_hbm, ker_hbm, w_hbm, fin_hbm, bias_hbm, fout_hbm,
    en_ref, rn_ref, dn_ref, den_ref,
    est_ref, res_ref, dir_ref, ker_ref, w_ref, fin_ref, bias_ref, fout_ref, fetch_s,
    edge, edge_halo, kscr, kt, ktj, facc, shaped, hb, hz, ishift, acc,
    part, rsbuf, iblk, iwin, part2, rsbuf2, sca, sca_in, ag, scb, ext,
    h_s, h_r, rs_s, rs_r, iw_s, iw_r, rt_s, rt_r, sa_s, sa_r, ag_s, ag_r, sb_s, sb_r,
):
    ci = lax.axis_index("comp")
    bi = lax.axis_index("band")
    up = lax.rem(bi + nb - 1, nb)
    down = lax.rem(bi + 1, nb)
    comps = w_ref.shape[0]
    half_nc = nc // 2

    def whole(ref, count, send, recv):
        slots = ref.at[pl.ds(0, count)]
        return remote(slots, slots, send.at[0], recv.at[0], ci, up)

    def ring(d, n):
        return min(d, n - d)

    xs = nc // 2
    far_peers = [
        (ring(dx, xs) + 2 * dz,
         lax.rem(lax.div(ci, 2) + dx, xs) * 2 + lax.rem(ci + dz, 2))
        for dx in range(xs) for dz in range(2) if dx or dz
    ]
    if nb % 4 == 0:
        ys = nb // 4
        far_bands = [
            (ring(dy, ys) + dz + dc / 2,
             lax.rem(lax.div(bi, 2 * ys) + dz, 2) * 2 * ys
             + lax.rem(lax.rem(lax.div(bi, 2), ys) + dy, ys) * 2 + lax.rem(bi + dc, 2))
            for dz in range(2) for dy in range(ys) for dc in range(2) if dz or dy or dc
        ]
    else:
        far_bands = [(1, lax.rem(bi + d, nb)) for d in range(1, nb)]

    def to_peers(fn):
        return [(hops, lambda j=j: fn(j)) for hops, j in far_peers]

    def to_bands(fn):
        return [(hops, lambda b=b: fn(b)) for hops, b in far_bands]

    fetches = [
        pltpu.make_async_copy(source, target, fetch_s.at[i])
        for i, (source, target) in enumerate((
            (ker_hbm, ker_ref), (dir_hbm, dir_ref), (w_hbm, w_ref), (res_hbm, res_ref),
            (est_hbm, est_ref), (fin_hbm, fin_ref), (bias_hbm, bias_ref), (fout_hbm, fout_ref)))
    ]
    for copy in fetches:
        copy.start()
    ends = []

    barrier = pltpu.get_barrier_semaphore()

    def greet(comp, band):
        pl.semaphore_signal(barrier, inc=1, device_id=(comp, band), device_id_type=MESH)

    for c in range(nc):
        greet(c, up)
        greet(c, down)
    for hops, j in far_peers:
        greet(j, bi)
    for d in range(2, nb - 1):
        greet(ci, lax.rem(bi + d, nb))

    kscr[...] = jnp.zeros_like(kscr)
    fetches[0].wait()
    for a in range(SPAN):
        kscr[:, a, 0:SPAN] = ker_ref[a].astype(F32)
    for k in range(comps):
        kt[k] = kscr[k].T

    fetches[1].wait()
    fetches[2].wait()
    direction = dir_ref[...]
    for k in range(comps):
        shaped[pl.ds(k * ROWS, ROWS), :] = (w_ref[k].astype(F32) * direction).astype(BF16)

    def band_matrix(table, k, b, first=0):
        row = table[k, pl.ds(b, 1), :]
        spread = jnp.broadcast_to(row, (ROWS, 128))
        return pltpu.roll(spread, first, 1, stride=1, stride_axis=0)

    left = lax.broadcasted_iota(jnp.int32, (ROWS, 128), 1) < ROWS

    def forward_pair(k, b):
        even = band_matrix(kt, k, b)
        odd = band_matrix(kt, k + 1, b, ROWS)
        lower = jnp.where(left, even, odd).astype(BF16)
        upper = jnp.where(left, odd, even).astype(BF16)
        return lower, upper

    def forward_matrices(columns):
        lower, upper = [], []
        for b in columns:
            pairs = [forward_pair(k, b) for k in range(0, comps, 2)]
            lower.append(jnp.concatenate([pair[0] for pair in pairs], axis=1))
            upper.append(jnp.concatenate([pair[1] for pair in pairs], axis=1))
        return jnp.concatenate(lower, axis=0), jnp.concatenate(upper, axis=0)

    for s0 in range(FINE):
        for side, sign in ((0, 1), (1, -1)):
            source = lane_shift(shaped[...], sign * (1 + s0))
            lower, upper = forward_matrices(
                [HALF + sign * (1 + s0 + FINE * s1) for s1 in range(COARSE)])
            for where, matrix, rows in ((0, lower, source), (1, upper, swap_pairs(source))):
                product = jnp.dot(matrix, rows, preferred_element_type=F32)
                if s0 == 0:
                    facc[side, where] = product
                else:
                    facc[side, where] += product
    lower, upper = forward_matrices([HALF])
    for where, matrix, rows in ((0, lower, shaped[...]), (1, upper, swap_pairs(shaped[...]))):
        total = jnp.dot(matrix, rows, preferred_element_type=F32)
        for side, sign in ((0, 1), (1, -1)):
            for s1 in range(COARSE):
                total += lane_shift(
                    facc[side, where, pl.ds(s1 * ROWS, ROWS), :], sign * FINE * s1)
        base = 8 * (1 - where)
        for q in range(8):
            part[base + q] = total[8 * q:8 * q + 8]

    for copy in fetches[3:]:
        copy.wait()
    edge[0, 0] = est_ref[:8]
    edge[0, 1] = dir_ref[:8]
    edge[1, 0] = est_ref[ROWS - 8:]
    edge[1, 1] = dir_ref[ROWS - 8:]
    residual = res_ref[...]
    sca[...] = jnp.zeros_like(sca)
    sca[1:2] = fold(direction * direction)
    sca[2:3] = fold(residual * residual)
    pl.semaphore_wait(barrier, nc - 1 + 2 * nc + nb - 3)

    def rs_up(c):
        return remote(part.at[c], rsbuf.at[nc + ci], rs_s.at[0], rs_r.at[0], c + half_nc, up)

    def rs_down(c):
        return remote(
            part.at[12 + c], rsbuf.at[nc + ci], rs_s.at[0], rs_r.at[0], c, down)

    def rs(j):
        return remote(part.at[4 + j], rsbuf.at[ci], rs_s.at[0], rs_r.at[0], j, bi)

    for c in range(half_nc):
        rs_up(c).start()
        rs_down(c).start()
    far_first(to_peers(lambda j: rs(j).start()))
    edges = [
        remote(edge.at[0], edge_halo.at[1], h_s.at[0], h_r.at[1], ci, up),
        remote(edge.at[1], edge_halo.at[0], h_s.at[1], h_r.at[0], ci, down),
    ]
    for copy in edges:
        copy.start()

    scattered = whole(part, 2 * nc - 1, rs_s, rs_r)
    ends.append(scattered.wait_send)
    ends.extend(copy.wait_send for copy in edges)

    size = 128
    anti_r = lax.broadcasted_iota(jnp.int32, (size, size), 0)
    anti_c = lax.broadcasted_iota(jnp.int32, (size, size), 1)
    anti = (anti_r + anti_c == SPAN - 1).astype(BF16)
    for k in range(comps):
        ktj[k] = jnp.dot(kt[k].astype(BF16), anti, preferred_element_type=F32)

    def build_back(s1):
        at = pl.ds(pl.multiple_of(s1 * ROWS, ROWS), ROWS)
        for side, sign in ((0, 1), (1, -1)):
            for s0 in range(BACK_FINE):
                b = HALF - sign * (1 + s0 + BACK_FINE * s1)
                for k in range(comps):
                    hb[side, k, at, pl.ds(s0 * 128, 128)] = band_matrix(ktj, k, b).astype(BF16)
    loop(0, BACK_COARSE, build_back)
    for k in range(comps):
        hz[k] = band_matrix(ktj, k, HALF).astype(BF16)

    rsbuf[ci] = part[4 + ci]
    scattered.wait_recv()
    far = lax.div(ci, half_nc)
    near = rsbuf[0]
    away = rsbuf[nc]
    for j in range(1, nc):
        near += rsbuf[j]
        away += rsbuf[nc + j]
    linked = ((bi > 0) | (far == 1)) & ((bi < nb - 1) | (far == 0))
    block = near + jnp.where(linked, away, 0.0)
    iblk[...] = jnp.concatenate([block[:, :128], block[:, 128:]], axis=0).astype(BF16)
    iwin[ci + 4] = iblk[...]
    far_band = lax.rem(bi + nb - 1 + 2 * far, nb)
    far_slot = ci + 12 - 16 * far

    def to_peer(j):
        return remote(iblk, iwin.at[ci + 4], iw_s.at[0], iw_r.at[0], j, bi)

    def to_far(j):
        return remote(iblk, iwin.at[far_slot], iw_s.at[0], iw_r.at[0], j, far_band)
    for j in range(nc):
        to_far(j).start()
    far_first(to_peers(lambda j: to_peer(j).start()))
    shown = whole(iwin, 2 * nc - 1, iw_s, iw_r)
    ends.append(shown.wait_send)
    shown.wait_recv()

    inside = ((bi > 0).astype(F32), (bi < nb - 1).astype(F32))
    for r in range(0, 16, 2):
        first, second = iwin[r].astype(F32), iwin[r + 1].astype(F32)
        pair = jnp.concatenate([
            jnp.concatenate([first[:8], first[8:]], axis=1),
            jnp.concatenate([second[:8], second[8:]], axis=1)], axis=0)
        if r < 4:
            pair = pair * inside[0]
        if r >= 12:
            pair = pair * inside[1]
        for at, value in all_shifts(pair.astype(BF16)):
            ishift[at, pl.ds(8 * r, 16), :] = value

    rsum = jnp.zeros((ROWS, WIDTH), F32)
    for k in range(comps):
        back = jnp.dot(hz[k], ishift[0], preferred_element_type=F32)
        for side, sign in ((0, 1), (1, -1)):
            source = ishift[pl.ds(1 + side * BACK_FINE, BACK_FINE)].reshape(BACK_FINE * 128, WIDTH)
            acc[...] = jnp.dot(hb[side, k], source, preferred_element_type=F32)
            for s1 in range(BACK_COARSE):
                back += lane_shift(acc[pl.ds(s1 * ROWS, ROWS), :], sign * BACK_FINE * s1)
        rsum += w_ref[k].astype(F32) * back
    for j in range(8):
        part2[j] = rsum[8 * j:8 * j + 8]

    def rt(j, slot):
        return remote(part2.at[j], rsbuf2.at[slot], rt_s.at[0], rt_r.at[0], j, bi)
    reduced = whole(rsbuf2, nc - 1, rt_s, rt_r)
    ends.append(reduced.wait_send)
    sca[0:1] = fold(dir_ref[...] * rsum)

    def sa(b, slot):
        return remote(sca, sca_in.at[slot], sa_s.at[0], sa_r.at[0], ci, b)
    far_first(to_peers(lambda j: rt(j, ci).start()) + to_bands(lambda b: sa(b, bi).start()))
    products = whole(sca_in, nb - 1, sa_s, sa_r)
    ends.append(products.wait_send)
    sca_in[bi] = sca[...]
    rsbuf2[ci] = part2[ci]

    reduced.wait_recv()
    block = rsbuf2[0]
    for j in range(1, nc):
        block += rsbuf2[j]
    products.wait_recv()
    scalars = sca_in[0]
    for b in range(1, nb):
        scalars += sca_in[b]
    ag[ci, 0] = block[:, :128]
    ag[ci, 1] = block[:, 128:]
    ag[ci, 2] = scalars

    def gather(j, slot):
        return remote(ag.at[ci], ag.at[slot], ag_s.at[0], ag_r.at[0], j, bi)
    far_first(to_peers(lambda j: gather(j, ci).start()))
    gathered = whole(ag, nc - 1, ag_s, ag_r)
    ends.append(gathered.wait_send)
    gathered.wait_recv()

    product = ag[0, 2, 0:1]
    for j in range(1, nc):
        product += ag[j, 2, 0:1]
    product = product + DAMPING * ag[0, 2, 1:2]
    old = jnp.sum(ag[0, 2, 2:3], axis=1, keepdims=True)
    alpha = old / jnp.sum(product, axis=1, keepdims=True)

    for j in range(8):
        for c in range(2):
            at = (slice(8 * j, 8 * j + 8), slice(128 * c, 128 * c + 128))
            rn_ref[at] = res_ref[at] - alpha * (ag[j, c] + DAMPING * dir_ref[at])
    updated = rn_ref[...]
    scb[nb] = jnp.broadcast_to(fold(updated * updated), (8, 128))

    def sb(b, slot):
        return remote(scb.at[nb], scb.at[slot], sb_s.at[0], sb_r.at[0], ci, b)
    far_first(to_bands(lambda b: sb(b, bi).start()))
    squares = whole(scb, nb - 1, sb_s, sb_r)
    ends.append(squares.wait_send)
    scb[bi] = scb[nb]
    for copy in edges:
        copy.wait_recv()

    estimate_next = est_ref[...] + alpha * dir_ref[...]
    en_ref[...] = estimate_next
    ext[0:8] = (edge_halo[0, 0] + alpha * edge_halo[0, 1]) * inside[0]
    ext[8:72] = estimate_next
    ext[72:80] = (edge_halo[1, 0] + alpha * edge_halo[1, 1]) * inside[1]
    framed = ext[...]
    columns = WIDTH // nc
    start = ci * columns
    pick_r = lax.broadcasted_iota(jnp.int32, (WIDTH, 128), 0)
    pick_c = lax.broadcasted_iota(jnp.int32, (WIDTH, 128), 1)
    group = (pick_c >= GROUP).astype(jnp.int32) + (pick_c >= 2 * GROUP).astype(jnp.int32)
    pick = (pick_r == start - 2 + pick_c - GROUP * group).astype(BF16)
    high = framed.astype(BF16)
    rest = framed - high.astype(F32)
    middle = rest.astype(BF16)
    low = (rest - middle.astype(F32)).astype(BF16)
    tile = (
        jnp.dot(high, pick, preferred_element_type=F32)
        + jnp.dot(middle, pick, preferred_element_type=F32)
        + jnp.dot(low, pick, preferred_element_type=F32)
    )
    tile = jnp.concatenate([tile[6:80], jnp.zeros((14, 128), F32)], axis=0)
    lane = lax.broadcasted_iota(jnp.int32, (24, 128), 1)
    row = lax.broadcasted_iota(jnp.int32, (24, 128), 0)
    third = (lane >= GROUP).astype(jnp.int32) + (lane >= 2 * GROUP).astype(jnp.int32)
    taps = []
    for a in range(3):
        packed = jnp.where(
            third == 0, tile[a:a + 24], jnp.where(third == 1, tile[24 + a:48 + a], tile[48 + a:72 + a]))
        for b in range(3):
            taps.append(packed if b == 0 else pltpu.roll(packed, 128 - b, 1))
    image_row = bi * ROWS - 1 + row + 24 * third
    image_col = start - 1 + lane - GROUP * third
    valid = (image_row >= 0) & (image_row < nb * ROWS) & (image_col >= 0) & (image_col < WIDTH)
    channels = bias_ref.shape[0]
    spreads = []
    for part_of in range(3):
        rows = slice(8 * part_of, 8 * part_of + 8)
        mine = [tap[rows] for tap in taps]

        def channel(c, sums):
            value = mine[0] * fin_ref[0, 0, c] + bias_ref[c]
            for t in range(1, 9):
                value += mine[t] * fin_ref[t // 3, t % 3, c]
            value = jnp.maximum(value, 0.0)
            return tuple(sums[t] + value * fout_ref[t // 3, t % 3, c] for t in range(9))

        sums = lax.fori_loop(
            0, channels, channel, tuple(jnp.zeros((8, 128), F32) for t in range(9)), unroll=unroll)
        spreads.append(sums)
    mixed = jnp.zeros((ROWS, 128), F32)
    for t in range(9):
        a, b = t // 3, t % 3
        whole = jnp.where(valid, jnp.concatenate([s[t] for s in spreads], axis=0), 0.0)
        column = jnp.concatenate(
            [pltpu.roll(whole, (128 - GROUP * g - b) % 128, 1) for g in range(3)], axis=0)
        mixed += column[a:a + ROWS]
    centre = pltpu.roll(tile[2:2 + ROWS], 126, 1)
    den_ref[...] = (centre - mixed).T[:columns]

    for end in ends:
        end()
    squares.wait_recv()
    new = scb[0, 0:1]
    for b in range(1, nb):
        new += scb[b, 0:1]
    new = jnp.sum(new, axis=1, keepdims=True)
    dn_ref[...] = rn_ref[...] + (new / old) * dir_ref[...]


def place(*refs):
    count = len(refs) // 2
    sources, targets, sems = refs[:count], refs[count:2 * count], refs[-1]
    copies = [
        pltpu.make_async_copy(source, target, sems.at[i])
        for i, (source, target) in enumerate(zip(sources, targets))
    ]
    for copy in copies:
        copy.start()
    for copy in copies:
        copy.wait()


def per_device(nc, nb, unroll, estimate, residual, direction, kernels, weight_maps, filters_in, biases, filters_out):
    comps = weight_maps.shape[0]
    columns = WIDTH // nc
    vmem = pl.BlockSpec(memory_space=pltpu.VMEM)
    hbm = pl.BlockSpec(memory_space=pltpu.HBM)
    anywhere = pl.BlockSpec(memory_space=pl.ANY)
    band = jax.ShapeDtypeStruct((ROWS, WIDTH), F32)
    shapes = (band, band, band, jax.ShapeDtypeStruct((columns, ROWS), F32))
    dma = pltpu.SemaphoreType.DMA
    results = pl.pallas_call(
        functools.partial(kernel, nc, nb, unroll),
        out_shape=shapes,
        in_specs=[hbm] * 8,
        out_specs=(vmem,) * 4,
        scratch_shapes=[
            pltpu.VMEM((ROWS, WIDTH), F32),
            pltpu.VMEM((ROWS, WIDTH), F32),
            pltpu.VMEM((ROWS, WIDTH), F32),
            pltpu.VMEM((SPAN, comps, SPAN), BF16),
            pltpu.VMEM((comps, ROWS, WIDTH), BF16),
            pltpu.SMEM((3, 3, filters_in.shape[0]), F32),
            pltpu.SMEM(biases.shape, F32),
            pltpu.SMEM((3, 3, filters_in.shape[0]), F32),
            dma((8,)),
            pltpu.VMEM((2, 2, 8, WIDTH), F32),
            pltpu.VMEM((2, 2, 8, WIDTH), F32),
            pltpu.VMEM((comps, 128, 128), F32),
            pltpu.VMEM((comps, 128, 128), F32),
            pltpu.VMEM((comps, 128, 128), F32),
            pltpu.VMEM((2, 2, COARSE * ROWS, WIDTH), F32),
            pltpu.VMEM((comps * ROWS, WIDTH), BF16),
            pltpu.VMEM((2, comps, BACK_COARSE * ROWS, BACK_FINE * 128), BF16),
            pltpu.VMEM((comps, ROWS, 128), BF16),
            pltpu.VMEM((1 + 2 * BACK_FINE, 128, WIDTH), BF16),
            pltpu.VMEM((BACK_COARSE * ROWS, WIDTH), F32),
            pltpu.VMEM((16, 8, WIDTH), F32),
            pltpu.VMEM((2 * nc, 8, WIDTH), F32),
            pltpu.VMEM((16, 128), BF16),
            pltpu.VMEM((16, 16, 128), BF16),
            pltpu.VMEM((8, 8, WIDTH), F32),
            pltpu.VMEM((8, 8, WIDTH), F32),
            pltpu.VMEM((8, 128), F32),
            pltpu.VMEM((nb, 8, 128), F32),
            pltpu.VMEM((nc, 3, 8, 128), F32),
            pltpu.VMEM((nb + 1, 8, 128), F32),
            pltpu.VMEM((80, WIDTH), F32),
            dma((2,)), dma((2,)),
            *([dma((1,))] * 12),
        ],
        compiler_params=pltpu.CompilerParams(
            collective_id=0, has_side_effects=True, vmem_limit_bytes=48 * 1024 * 1024),
        cost_estimate=pl.CostEstimate(
            flops=4 * 65 * comps * 64 * 128 * 256, bytes_accessed=1 << 20, transcendentals=0),
    )(*(pltpu.with_memory_space_constraint(x, pltpu.HBM) for x in (
        estimate, residual, direction, kernels.transpose(1, 0, 2), weight_maps,
        filters_in.transpose(1, 2, 0), biases, filters_out.transpose(1, 2, 0))))
    estimate_next, residual_next, direction_next, turned = pl.pallas_call(
        place,
        out_shape=shapes,
        in_specs=[vmem] * 4,
        out_specs=(anywhere,) * 4,
        scratch_shapes=[dma((4,))],
        compiler_params=pltpu.CompilerParams(vmem_limit_bytes=4 * 1024 * 1024),
    )(*results)
    return estimate_next, residual_next, direction_next, turned.T


def solution(mesh):
    nc, nb = mesh.shape["comp"], mesh.shape["band"]
    return jax.shard_map(
        functools.partial(per_device, nc, nb, 4),
        mesh=mesh,
        in_specs=(
            P("band", None),
            P("band", None),
            P("band", None),
            P("comp", None, None),
            P("comp", "band", None),
            P(),
            P(),
            P(),
        ),
        out_specs=(P("band", None), P("band", None), P("band", None), P("band", "comp")),
        check_vma=False,
    )
```

```python
import functools

import jax
import jax.numpy as jnp
from jax import lax
from jax.experimental import pallas as pl
from jax.experimental.pallas import tpu as pltpu
from jax.sharding import PartitionSpec as P

MESH = pl.DeviceIdType.MESH
F32 = jnp.float32
BF16 = jnp.bfloat16
DAMPING = 0.5
HALF = 32
SPAN = 65
ROWS = 64
WIDTH = 256
FINE = 4
COARSE = 8
BACK_FINE = 8
BACK_COARSE = 4
GROUP = 40


def lane_shift(x, n):
    if n == 0:
        return x
    width = x.shape[1]
    col = lax.broadcasted_iota(jnp.int32, x.shape, 1)
    keep = col < width - n if n > 0 else col >= -n
    return jnp.where(keep, pltpu.roll(x, (-n) % width, 1), jnp.zeros((), x.dtype))


def fold(x):
    x = jnp.sum(x, axis=0, keepdims=True)
    return x[:, :128] + x[:, 128:]


def all_shifts(x):
    yield 0, x
    for s0 in range(BACK_FINE):
        yield 1 + s0, lane_shift(x, 1 + s0)
        yield 1 + BACK_FINE + s0, lane_shift(x, -1 - s0)


def swap_pairs(x):
    return jnp.concatenate(
        [x[(k ^ 1) * ROWS:(k ^ 1) * ROWS + ROWS] for k in range(x.shape[0] // ROWS)], axis=0)


def far_first(fns):
    for hops, fn in sorted(fns, key=lambda pair: -pair[0]):
        fn()


def loop(low, high, fn):
    def body(i, carry):
        fn(i)
        return carry
    lax.fori_loop(low, high, body, 0)


def remote(src, dst, send, recv, comp, band):
    return pltpu.make_async_remote_copy(
        src_ref=src, dst_ref=dst, send_sem=send, recv_sem=recv,
        device_id=(comp, band), device_id_type=MESH,
    )


def kernel(
    nc, nb, unroll,
    est_hbm, res_hbm, dir_hbm, ker_hbm, w_hbm, fin_hbm, bias_hbm, fout_hbm,
    en_ref, rn_ref, dn_ref, den_ref,
    est_ref, res_ref, dir_ref, ker_ref, w_ref, fin_ref, bias_ref, fout_ref, fetch_s,
    edge, edge_halo, kscr, kt, ktj, facc, shaped, hb, hz, ishift, acc,
    part, rsbuf, iblk, iwin, part2, rsbuf2, sca, sca_in, ag, scb, ext,
    h_s, h_r, rs_s, rs_r, iw_s, iw_r, rt_s, rt_r, sa_s, sa_r, ag_s, ag_r, sb_s, sb_r,
):
    ci = lax.axis_index("comp")
    bi = lax.axis_index("band")
    up = lax.rem(bi + nb - 1, nb)
    down = lax.rem(bi + 1, nb)
    comps = w_ref.shape[0]
    half_nc = nc // 2

    def whole(ref, count, send, recv):
        slots = ref.at[pl.ds(0, count)]
        return remote(slots, slots, send.at[0], recv.at[0], ci, up)

    def ring(d, n):
        return min(d, n - d)

    xs = nc // 2
    far_peers = [
        (ring(dx, xs) + 2 * dz,
         lax.rem(lax.div(ci, 2) + dx, xs) * 2 + lax.rem(ci + dz, 2))
        for dx in range(xs) for dz in range(2) if dx or dz
    ]
    if nb % 4 == 0:
        ys = nb // 4
        far_bands = [
            (ring(dy, ys) + dz + dc / 2,
             lax.rem(lax.div(bi, 2 * ys) + dz, 2) * 2 * ys
             + lax.rem(lax.rem(lax.div(bi, 2), ys) + dy, ys) * 2 + lax.rem(bi + dc, 2))
            for dz in range(2) for dy in range(ys) for dc in range(2) if dz or dy or dc
        ]
    else:
        far_bands = [(1, lax.rem(bi + d, nb)) for d in range(1, nb)]

    def to_peers(fn):
        return [(hops, lambda j=j: fn(j)) for hops, j in far_peers]

    def to_bands(fn):
        return [(hops, lambda b=b: fn(b)) for hops, b in far_bands]

    fetches = [
        pltpu.make_async_copy(source, target, fetch_s.at[i])
        for i, (source, target) in enumerate((
            (ker_hbm, ker_ref), (dir_hbm, dir_ref), (w_hbm, w_ref), (res_hbm, res_ref),
            (est_hbm, est_ref), (fin_hbm, fin_ref), (bias_hbm, bias_ref), (fout_hbm, fout_ref)))
    ]
    for copy in fetches:
        copy.start()
    ends = []

    barrier = pltpu.get_barrier_semaphore()

    def greet(comp, band):
        pl.semaphore_signal(barrier, inc=1, device_id=(comp, band), device_id_type=MESH)

    for c in range(nc):
        greet(c, up)
        greet(c, down)
    for hops, j in far_peers:
        greet(j, bi)
    for d in range(2, nb - 1):
        greet(ci, lax.rem(bi + d, nb))

    kscr[...] = jnp.zeros_like(kscr)
    fetches[0].wait()
    for a in range(SPAN):
        kscr[:, a, 0:SPAN] = ker_ref[a].astype(F32)
    for k in range(comps):
        kt[k] = kscr[k].T

    fetches[1].wait()
    fetches[2].wait()
    direction = dir_ref[...]
    for k in range(comps):
        shaped[pl.ds(k * ROWS, ROWS), :] = (w_ref[k].astype(F32) * direction).astype(BF16)

    def band_matrix(table, k, b, first=0):
        row = table[k, pl.ds(b, 1), :]
        spread = jnp.broadcast_to(row, (ROWS, 128))
        return pltpu.roll(spread, first, 1, stride=1, stride_axis=0)

    left = lax.broadcasted_iota(jnp.int32, (ROWS, 128), 1) < ROWS

    def forward_pair(k, b):
        even = band_matrix(kt, k, b)
        odd = band_matrix(kt, k + 1, b, ROWS)
        lower = jnp.where(left, even, odd).astype(BF16)
        upper = jnp.where(left, odd, even).astype(BF16)
        return lower, upper

    def forward_matrices(columns):
        lower, upper = [], []
        for b in columns:
            pairs = [forward_pair(k, b) for k in range(0, comps, 2)]
            lower.append(jnp.concatenate([pair[0] for pair in pairs], axis=1))
            upper.append(jnp.concatenate([pair[1] for pair in pairs], axis=1))
        return jnp.concatenate(lower, axis=0), jnp.concatenate(upper, axis=0)

    for s0 in range(FINE):
        for side, sign in ((0, 1), (1, -1)):
            source = lane_shift(shaped[...], sign * (1 + s0))
            lower, upper = forward_matrices(
                [HALF + sign * (1 + s0 + FINE * s1) for s1 in range(COARSE)])
            for where, matrix, rows in ((0, lower, source), (1, upper, swap_pairs(source))):
                product = jnp.dot(matrix, rows, preferred_element_type=F32)
                if s0 == 0:
                    facc[side, where] = product
                else:
                    facc[side, where] += product
    lower, upper = forward_matrices([HALF])
    for where, matrix, rows in ((0, lower, shaped[...]), (1, upper, swap_pairs(shaped[...]))):
        total = jnp.dot(matrix, rows, preferred_element_type=F32)
        for side, sign in ((0, 1), (1, -1)):
            for s1 in range(COARSE):
                total += lane_shift(
                    facc[side, where, pl.ds(s1 * ROWS, ROWS), :], sign * FINE * s1)
        base = 8 * (1 - where)
        for q in range(8):
            part[base + q] = total[8 * q:8 * q + 8]

    for copy in fetches[3:]:
        copy.wait()
    edge[0, 0] = est_ref[:8]
    edge[0, 1] = dir_ref[:8]
    edge[1, 0] = est_ref[ROWS - 8:]
    edge[1, 1] = dir_ref[ROWS - 8:]
    residual = res_ref[...]
    energies = (fold(direction * direction), fold(residual * residual))
    pl.semaphore_wait(barrier, nc - 1 + 2 * nc + nb - 3)

    def rs_up(c):
        return remote(part.at[c], rsbuf.at[nc + ci], rs_s.at[0], rs_r.at[0], c + half_nc, up)

    def rs_down(c):
        return remote(
            part.at[12 + c], rsbuf.at[nc + ci], rs_s.at[0], rs_r.at[0], c, down)

    def rs(j):
        return remote(part.at[4 + j], rsbuf.at[ci], rs_s.at[0], rs_r.at[0], j, bi)

    for c in range(half_nc):
        rs_up(c).start()
        rs_down(c).start()
    far_first(to_peers(lambda j: rs(j).start()))
    edges = [
        remote(edge.at[0], edge_halo.at[1], h_s.at[0], h_r.at[1], ci, up),
        remote(edge.at[1], edge_halo.at[0], h_s.at[1], h_r.at[0], ci, down),
    ]
    for copy in edges:
        copy.start()

    scattered = whole(part, 2 * nc - 1, rs_s, rs_r)
    ends.append(scattered.wait_send)
    ends.extend(copy.wait_send for copy in edges)

    size = 128
    anti_r = lax.broadcasted_iota(jnp.int32, (size, size), 0)
    anti_c = lax.broadcasted_iota(jnp.int32, (size, size), 1)
    anti = (anti_r + anti_c == SPAN - 1).astype(BF16)
    for k in range(comps):
        ktj[k] = jnp.dot(kt[k].astype(BF16), anti, preferred_element_type=F32)

    def build_back(s1):
        at = pl.ds(pl.multiple_of(s1 * ROWS, ROWS), ROWS)
        for side, sign in ((0, 1), (1, -1)):
            for s0 in range(BACK_FINE):
                b = HALF - sign * (1 + s0 + BACK_FINE * s1)
                for k in range(comps):
                    hb[side, k, at, pl.ds(s0 * 128, 128)] = band_matrix(ktj, k, b).astype(BF16)
    loop(0, BACK_COARSE, build_back)
    for k in range(comps):
        hz[k] = band_matrix(ktj, k, HALF).astype(BF16)

    rsbuf[ci] = part[4 + ci]
    scattered.wait_recv()
    far = lax.div(ci, half_nc)
    near = rsbuf[0]
    away = rsbuf[nc]
    for j in range(1, nc):
        near += rsbuf[j]
        away += rsbuf[nc + j]
    linked = ((bi > 0) | (far == 1)) & ((bi < nb - 1) | (far == 0))
    block = near + jnp.where(linked, away, 0.0)
    iblk[...] = jnp.concatenate([block[:, :128], block[:, 128:]], axis=0).astype(BF16)
    iwin[ci + 4] = iblk[...]
    far_band = lax.rem(bi + nb - 1 + 2 * far, nb)
    far_slot = ci + 12 - 16 * far

    def to_peer(j):
        return remote(iblk, iwin.at[ci + 4], iw_s.at[0], iw_r.at[0], j, bi)

    def to_far(j):
        return remote(iblk, iwin.at[far_slot], iw_s.at[0], iw_r.at[0], j, far_band)
    for j in range(nc):
        to_far(j).start()
    far_first(to_peers(lambda j: to_peer(j).start()))
    shown = whole(iwin, 2 * nc - 1, iw_s, iw_r)
    ends.append(shown.wait_send)
    shown.wait_recv()

    inside = ((bi > 0).astype(F32), (bi < nb - 1).astype(F32))
    for r in range(0, 16, 2):
        first, second = iwin[r].astype(F32), iwin[r + 1].astype(F32)
        pair = jnp.concatenate([
            jnp.concatenate([first[:8], first[8:]], axis=1),
            jnp.concatenate([second[:8], second[8:]], axis=1)], axis=0)
        if r < 4:
            pair = pair * inside[0]
        if r >= 12:
            pair = pair * inside[1]
        for at, value in all_shifts(pair.astype(BF16)):
            ishift[at, pl.ds(8 * r, 16), :] = value

    rsum = jnp.zeros((ROWS, WIDTH), F32)
    for side in range(2):
        for k in range(comps):
            source = ishift[pl.ds(1 + side * BACK_FINE, BACK_FINE)].reshape(BACK_FINE * 128, WIDTH)
            acc[k, side] = jnp.dot(hb[side, k], source, preferred_element_type=F32)
    for k in range(comps):
        back = jnp.dot(hz[k], ishift[0], preferred_element_type=F32)
        for side, sign in ((0, 1), (1, -1)):
            for s1 in range(BACK_COARSE):
                back += lane_shift(acc[k, side, pl.ds(s1 * ROWS, ROWS), :], sign * BACK_FINE * s1)
        rsum += w_ref[k].astype(F32) * back
    for j in range(8):
        part2[j] = rsum[8 * j:8 * j + 8]

    def rt(j, slot):
        return remote(part2.at[j], rsbuf2.at[slot], rt_s.at[0], rt_r.at[0], j, bi)
    reduced = whole(rsbuf2, nc - 1, rt_s, rt_r)
    ends.append(reduced.wait_send)
    lane_row = lax.broadcasted_iota(jnp.int32, (1, 128), 1)
    quarters = []
    for x in (fold(dir_ref[...] * rsum), *energies):
        x = x + pltpu.roll(x, 64, 1)
        quarters.append(x + pltpu.roll(x, 32, 1))
    sca[...] = jnp.where(
        lane_row < 32, quarters[0], jnp.where(lane_row < 64, quarters[1], quarters[2]))

    def sa(b, slot):
        return remote(sca, sca_in.at[slot], sa_s.at[0], sa_r.at[0], ci, b)
    far_first(to_peers(lambda j: rt(j, ci).start()) + to_bands(lambda b: sa(b, bi).start()))
    products = whole(sca_in, nb - 1, sa_s, sa_r)
    ends.append(products.wait_send)
    sca_in[bi] = sca[...]
    rsbuf2[ci] = part2[ci]

    reduced.wait_recv()
    block = rsbuf2[0]
    for j in range(1, nc):
        block += rsbuf2[j]
    products.wait_recv()
    scalars = sca_in[0]
    for b in range(1, nb):
        scalars += sca_in[b]
    ag[ci, 0] = block[:, :128]
    ag[ci, 1] = block[:, 128:]
    ag[ci, 2] = jnp.broadcast_to(scalars, (8, 128))

    def gather(j, slot):
        return remote(ag.at[ci], ag.at[slot], ag_s.at[0], ag_r.at[0], j, bi)
    far_first(to_peers(lambda j: gather(j, ci).start()))
    gathered = whole(ag, nc - 1, ag_s, ag_r)
    ends.append(gathered.wait_send)
    gathered.wait_recv()

    product = ag[0, 2, 0:1]
    for j in range(1, nc):
        product += ag[j, 2, 0:1]
    scalars = ag[0, 2, 0:1]
    product = jnp.where(lane_row < 32, product, jnp.where(lane_row < 64, DAMPING * scalars, 0.0))
    squared = jnp.where((lane_row >= 64) & (lane_row < 96), scalars, 0.0)
    old = jnp.sum(squared, axis=1, keepdims=True)
    alpha = old / jnp.sum(product, axis=1, keepdims=True)

    for j in range(8):
        for c in range(2):
            at = (slice(8 * j, 8 * j + 8), slice(128 * c, 128 * c + 128))
            rn_ref[at] = res_ref[at] - alpha * (ag[j, c] + DAMPING * dir_ref[at])
    updated = rn_ref[...]
    scb[nb] = fold(updated * updated)

    def sb(b, slot):
        return remote(scb.at[nb], scb.at[slot], sb_s.at[0], sb_r.at[0], ci, b)
    far_first(to_bands(lambda b: sb(b, bi).start()))
    squares = whole(scb, nb - 1, sb_s, sb_r)
    ends.append(squares.wait_send)
    scb[bi] = scb[nb]
    for copy in edges:
        copy.wait_recv()

    estimate_next = est_ref[...] + alpha * dir_ref[...]
    en_ref[...] = estimate_next
    ext[0:8] = (edge_halo[0, 0] + alpha * edge_halo[0, 1]) * inside[0]
    ext[8:72] = estimate_next
    ext[72:80] = (edge_halo[1, 0] + alpha * edge_halo[1, 1]) * inside[1]
    framed = ext[...]
    columns = WIDTH // nc
    start = ci * columns
    pick_r = lax.broadcasted_iota(jnp.int32, (WIDTH, 128), 0)
    pick_c = lax.broadcasted_iota(jnp.int32, (WIDTH, 128), 1)
    group = (pick_c >= GROUP).astype(jnp.int32) + (pick_c >= 2 * GROUP).astype(jnp.int32)
    pick = (pick_r == start - 2 + pick_c - GROUP * group).astype(BF16)
    high = framed.astype(BF16)
    rest = framed - high.astype(F32)
    middle = rest.astype(BF16)
    low = (rest - middle.astype(F32)).astype(BF16)
    tile = (
        jnp.dot(high, pick, preferred_element_type=F32)
        + jnp.dot(middle, pick, preferred_element_type=F32)
        + jnp.dot(low, pick, preferred_element_type=F32)
    )
    tile = jnp.concatenate([tile[6:80], jnp.zeros((14, 128), F32)], axis=0)
    lane = lax.broadcasted_iota(jnp.int32, (24, 128), 1)
    row = lax.broadcasted_iota(jnp.int32, (24, 128), 0)
    third = (lane >= GROUP).astype(jnp.int32) + (lane >= 2 * GROUP).astype(jnp.int32)
    taps = []
    for a in range(3):
        packed = jnp.where(
            third == 0, tile[a:a + 24], jnp.where(third == 1, tile[24 + a:48 + a], tile[48 + a:72 + a]))
        for b in range(3):
            taps.append(packed if b == 0 else pltpu.roll(packed, 128 - b, 1))
    image_row = bi * ROWS - 1 + row + 24 * third
    image_col = start - 1 + lane - GROUP * third
    valid = (image_row >= 0) & (image_row < nb * ROWS) & (image_col >= 0) & (image_col < WIDTH)
    channels = bias_ref.shape[0]
    spreads = []
    for part_of in range(3):
        rows = slice(8 * part_of, 8 * part_of + 8)
        mine = [tap[rows] for tap in taps]

        def channel(c, sums):
            value = mine[0] * fin_ref[0, 0, c] + bias_ref[c]
            for t in range(1, 9):
                value += mine[t] * fin_ref[t // 3, t % 3, c]
            value = jnp.maximum(value, 0.0)
            return tuple(sums[t] + value * fout_ref[t // 3, t % 3, c] for t in range(9))

        sums = lax.fori_loop(
            0, channels, channel, tuple(jnp.zeros((8, 128), F32) for t in range(9)), unroll=unroll)
        spreads.append(sums)
    mixed = jnp.zeros((ROWS, 128), F32)
    for t in range(9):
        a, b = t // 3, t % 3
        whole = jnp.where(valid, jnp.concatenate([s[t] for s in spreads], axis=0), 0.0)
        column = jnp.concatenate(
            [pltpu.roll(whole, (128 - GROUP * g - b) % 128, 1) for g in range(3)], axis=0)
        mixed += column[a:a + ROWS]
    centre = pltpu.roll(tile[2:2 + ROWS], 126, 1)
    den_ref[...] = (centre - mixed).T[:columns]

    for end in ends:
        end()
    squares.wait_recv()
    new = scb[0]
    for b in range(1, nb):
        new += scb[b]
    new = jnp.sum(new, axis=1, keepdims=True)
    dn_ref[...] = rn_ref[...] + (new / old) * dir_ref[...]


def place(*refs):
    count = len(refs) // 2
    sources, targets, sems = refs[:count], refs[count:2 * count], refs[-1]
    copies = [
        pltpu.make_async_copy(source, target, sems.at[i])
        for i, (source, target) in enumerate(zip(sources, targets))
    ]
    for copy in copies:
        copy.start()
    for copy in copies:
        copy.wait()


def per_device(nc, nb, unroll, estimate, residual, direction, kernels, weight_maps, filters_in, biases, filters_out):
    comps = weight_maps.shape[0]
    columns = WIDTH // nc
    vmem = pl.BlockSpec(memory_space=pltpu.VMEM)
    hbm = pl.BlockSpec(memory_space=pltpu.HBM)
    anywhere = pl.BlockSpec(memory_space=pl.ANY)
    band = jax.ShapeDtypeStruct((ROWS, WIDTH), F32)
    shapes = (band, band, band, jax.ShapeDtypeStruct((columns, ROWS), F32))
    dma = pltpu.SemaphoreType.DMA
    results = pl.pallas_call(
        functools.partial(kernel, nc, nb, unroll),
        out_shape=shapes,
        in_specs=[hbm] * 8,
        out_specs=(vmem,) * 4,
        scratch_shapes=[
            pltpu.VMEM((ROWS, WIDTH), F32),
            pltpu.VMEM((ROWS, WIDTH), F32),
            pltpu.VMEM((ROWS, WIDTH), F32),
            pltpu.VMEM((SPAN, comps, SPAN), BF16),
            pltpu.VMEM((comps, ROWS, WIDTH), BF16),
            pltpu.SMEM((3, 3, filters_in.shape[0]), F32),
            pltpu.SMEM(biases.shape, F32),
            pltpu.SMEM((3, 3, filters_in.shape[0]), F32),
            dma((8,)),
            pltpu.VMEM((2, 2, 8, WIDTH), F32),
            pltpu.VMEM((2, 2, 8, WIDTH), F32),
            pltpu.VMEM((comps, 128, 128), F32),
            pltpu.VMEM((comps, 128, 128), F32),
            pltpu.VMEM((comps, 128, 128), F32),
            pltpu.VMEM((2, 2, COARSE * ROWS, WIDTH), F32),
            pltpu.VMEM((comps * ROWS, WIDTH), BF16),
            pltpu.VMEM((2, comps, BACK_COARSE * ROWS, BACK_FINE * 128), BF16),
            pltpu.VMEM((comps, ROWS, 128), BF16),
            pltpu.VMEM((1 + 2 * BACK_FINE, 128, WIDTH), BF16),
            pltpu.VMEM((comps, 2, BACK_COARSE * ROWS, WIDTH), F32),
            pltpu.VMEM((16, 8, WIDTH), F32),
            pltpu.VMEM((2 * nc, 8, WIDTH), F32),
            pltpu.VMEM((16, 128), BF16),
            pltpu.VMEM((16, 16, 128), BF16),
            pltpu.VMEM((8, 8, WIDTH), F32),
            pltpu.VMEM((8, 8, WIDTH), F32),
            pltpu.VMEM((1, 128), F32),
            pltpu.VMEM((nb, 1, 128), F32),
            pltpu.VMEM((nc, 3, 8, 128), F32),
            pltpu.VMEM((nb + 1, 1, 128), F32),
            pltpu.VMEM((80, WIDTH), F32),
            dma((2,)), dma((2,)),
            *([dma((1,))] * 12),
        ],
        compiler_params=pltpu.CompilerParams(
            collective_id=0, has_side_effects=True, vmem_limit_bytes=48 * 1024 * 1024),
        cost_estimate=pl.CostEstimate(
            flops=4 * 65 * comps * 64 * 128 * 256, bytes_accessed=1 << 20, transcendentals=0),
    )(*(pltpu.with_memory_space_constraint(x, pltpu.HBM) for x in (
        estimate, residual, direction, kernels.transpose(1, 0, 2), weight_maps,
        filters_in.transpose(1, 2, 0), biases, filters_out.transpose(1, 2, 0))))
    estimate_next, residual_next, direction_next, turned = pl.pallas_call(
        place,
        out_shape=shapes,
        in_specs=[vmem] * 4,
        out_specs=(anywhere,) * 4,
        scratch_shapes=[dma((4,))],
        compiler_params=pltpu.CompilerParams(vmem_limit_bytes=4 * 1024 * 1024),
    )(*results)
    return estimate_next, residual_next, direction_next, turned.T


def solution(mesh):
    nc, nb = mesh.shape["comp"], mesh.shape["band"]
    return jax.shard_map(
        functools.partial(per_device, nc, nb, 4),
        mesh=mesh,
        in_specs=(
            P("band", None),
            P("band", None),
            P("band", None),
            P("comp", None, None),
            P("comp", "band", None),
            P(),
            P(),
            P(),
        ),
        out_specs=(P("band", None), P("band", None), P("band", None), P("band", "comp")),
        check_vma=False,
    )
```

```python
import functools

import jax
import jax.numpy as jnp
from jax import lax
from jax.experimental import pallas as pl
from jax.experimental.pallas import tpu as pltpu
from jax.sharding import PartitionSpec as P

MESH = pl.DeviceIdType.MESH
F32 = jnp.float32
BF16 = jnp.bfloat16
DAMPING = 0.5
HALF = 32
SPAN = 65
ROWS = 64
WIDTH = 256
FINE = 4
COARSE = 8
BACK_FINE = 8
BACK_COARSE = 4
GROUP = 40


def lane_shift(x, n):
    if n == 0:
        return x
    width = x.shape[1]
    col = lax.broadcasted_iota(jnp.int32, x.shape, 1)
    keep = col < width - n if n > 0 else col >= -n
    return jnp.where(keep, pltpu.roll(x, (-n) % width, 1), jnp.zeros((), x.dtype))


def fold(x):
    x = jnp.sum(x, axis=0, keepdims=True)
    return x[:, :128] + x[:, 128:]


def all_shifts(x):
    yield 0, x
    for s0 in range(BACK_FINE):
        yield 1 + s0, lane_shift(x, 1 + s0)
        yield 1 + BACK_FINE + s0, lane_shift(x, -1 - s0)


def swap_pairs(x):
    return jnp.concatenate(
        [x[(k ^ 1) * ROWS:(k ^ 1) * ROWS + ROWS] for k in range(x.shape[0] // ROWS)], axis=0)


def far_first(fns):
    for hops, fn in sorted(fns, key=lambda pair: -pair[0]):
        fn()


def loop(low, high, fn):
    def body(i, carry):
        fn(i)
        return carry
    lax.fori_loop(low, high, body, 0)


def remote(src, dst, send, recv, comp, band):
    return pltpu.make_async_remote_copy(
        src_ref=src, dst_ref=dst, send_sem=send, recv_sem=recv,
        device_id=(comp, band), device_id_type=MESH,
    )


def kernel(
    nc, nb, unroll,
    est_hbm, res_hbm, dir_hbm, ker_hbm, w_hbm, fin_hbm, bias_hbm, fout_hbm,
    en_ref, rn_ref, dn_ref, den_ref,
    est_ref, res_ref, dir_ref, ker_ref, w_ref, fin_ref, bias_ref, fout_ref, fetch_s,
    edge, edge_halo, kscr, kt, ktj, facc, shaped, hb, hz, ishift, acc,
    part, rsbuf, iblk, iwin, part2, rsbuf2, sca, sca_in, ag, scb, ext,
    h_s, h_r, rs_s, rs_r, iw_s, iw_r, in_r, rt_s, rt_r, sa_s, sa_r, ag_s, ag_r, sb_s, sb_r,
):
    ci = lax.axis_index("comp")
    bi = lax.axis_index("band")
    up = lax.rem(bi + nb - 1, nb)
    down = lax.rem(bi + 1, nb)
    comps = w_ref.shape[0]
    half_nc = nc // 2

    def whole(ref, count, send, recv):
        slots = ref.at[pl.ds(0, count)]
        return remote(slots, slots, send.at[0], recv.at[0], ci, up)

    def ring(d, n):
        return min(d, n - d)

    xs = nc // 2
    far_peers = [
        (ring(dx, xs) + 2 * dz,
         lax.rem(lax.div(ci, 2) + dx, xs) * 2 + lax.rem(ci + dz, 2))
        for dx in range(xs) for dz in range(2) if dx or dz
    ]
    if nb % 4 == 0:
        ys = nb // 4
        far_bands = [
            (ring(dy, ys) + dz + dc / 2,
             lax.rem(lax.div(bi, 2 * ys) + dz, 2) * 2 * ys
             + lax.rem(lax.rem(lax.div(bi, 2), ys) + dy, ys) * 2 + lax.rem(bi + dc, 2))
            for dz in range(2) for dy in range(ys) for dc in range(2) if dz or dy or dc
        ]
    else:
        far_bands = [(1, lax.rem(bi + d, nb)) for d in range(1, nb)]

    def to_peers(fn):
        return [(hops, lambda j=j: fn(j)) for hops, j in far_peers]

    def to_bands(fn):
        return [(hops, lambda b=b: fn(b)) for hops, b in far_bands]

    fetches = [
        pltpu.make_async_copy(source, target, fetch_s.at[i])
        for i, (source, target) in enumerate((
            (ker_hbm, ker_ref), (dir_hbm, dir_ref), (w_hbm, w_ref), (res_hbm, res_ref),
            (est_hbm, est_ref), (fin_hbm, fin_ref), (bias_hbm, bias_ref), (fout_hbm, fout_ref)))
    ]
    for copy in fetches:
        copy.start()
    ends = []

    barrier = pltpu.get_barrier_semaphore()

    def greet(comp, band):
        pl.semaphore_signal(barrier, inc=1, device_id=(comp, band), device_id_type=MESH)

    for c in range(nc):
        greet(c, up)
        greet(c, down)
    for hops, j in far_peers:
        greet(j, bi)
    for d in range(2, nb - 1):
        greet(ci, lax.rem(bi + d, nb))

    kscr[...] = jnp.zeros_like(kscr)
    fetches[0].wait()
    for a in range(SPAN):
        kscr[:, a, 0:SPAN] = ker_ref[a].astype(F32)
    for k in range(comps):
        kt[k] = kscr[k].T

    fetches[1].wait()
    fetches[2].wait()
    direction = dir_ref[...]
    for k in range(comps):
        shaped[pl.ds(k * ROWS, ROWS), :] = (w_ref[k].astype(F32) * direction).astype(BF16)

    def band_matrix(table, k, b, first=0):
        row = table[k, pl.ds(b, 1), :]
        spread = jnp.broadcast_to(row, (ROWS, 128))
        return pltpu.roll(spread, first, 1, stride=1, stride_axis=0)

    left = lax.broadcasted_iota(jnp.int32, (ROWS, 128), 1) < ROWS

    def forward_pair(k, b):
        even = band_matrix(kt, k, b)
        odd = band_matrix(kt, k + 1, b, ROWS)
        lower = jnp.where(left, even, odd).astype(BF16)
        upper = jnp.where(left, odd, even).astype(BF16)
        return lower, upper

    def forward_matrices(columns):
        lower, upper = [], []
        for b in columns:
            pairs = [forward_pair(k, b) for k in range(0, comps, 2)]
            lower.append(jnp.concatenate([pair[0] for pair in pairs], axis=1))
            upper.append(jnp.concatenate([pair[1] for pair in pairs], axis=1))
        return jnp.concatenate(lower, axis=0), jnp.concatenate(upper, axis=0)

    for s0 in range(FINE):
        for side, sign in ((0, 1), (1, -1)):
            source = lane_shift(shaped[...], sign * (1 + s0))
            lower, upper = forward_matrices(
                [HALF + sign * (1 + s0 + FINE * s1) for s1 in range(COARSE)])
            for where, matrix, rows in ((0, lower, source), (1, upper, swap_pairs(source))):
                product = jnp.dot(matrix, rows, preferred_element_type=F32)
                if s0 == 0:
                    facc[side, where] = product
                else:
                    facc[side, where] += product
    lower, upper = forward_matrices([HALF])
    for where, matrix, rows in ((0, lower, shaped[...]), (1, upper, swap_pairs(shaped[...]))):
        total = jnp.dot(matrix, rows, preferred_element_type=F32)
        for side, sign in ((0, 1), (1, -1)):
            for s1 in range(COARSE):
                total += lane_shift(
                    facc[side, where, pl.ds(s1 * ROWS, ROWS), :], sign * FINE * s1)
        base = 8 * (1 - where)
        for q in range(8):
            part[base + q] = total[8 * q:8 * q + 8]

    for copy in fetches[3:]:
        copy.wait()
    edge[0, 0] = est_ref[:8]
    edge[0, 1] = dir_ref[:8]
    edge[1, 0] = est_ref[ROWS - 8:]
    edge[1, 1] = dir_ref[ROWS - 8:]
    residual = res_ref[...]
    energies = (fold(direction * direction), fold(residual * residual))
    pl.semaphore_wait(barrier, nc - 1 + 2 * nc + nb - 3)

    def rs_up(c):
        return remote(part.at[c], rsbuf.at[nc + ci], rs_s.at[0], rs_r.at[0], c + half_nc, up)

    def rs_down(c):
        return remote(
            part.at[12 + c], rsbuf.at[nc + ci], rs_s.at[0], rs_r.at[0], c, down)

    def rs(j):
        return remote(part.at[4 + j], rsbuf.at[ci], rs_s.at[0], rs_r.at[0], j, bi)

    for c in range(half_nc):
        rs_up(c).start()
        rs_down(c).start()
    far_first(to_peers(lambda j: rs(j).start()))
    edges = [
        remote(edge.at[0], edge_halo.at[1], h_s.at[0], h_r.at[1], ci, up),
        remote(edge.at[1], edge_halo.at[0], h_s.at[1], h_r.at[0], ci, down),
    ]
    for copy in edges:
        copy.start()

    scattered = whole(part, 2 * nc - 1, rs_s, rs_r)
    ends.append(scattered.wait_send)
    ends.extend(copy.wait_send for copy in edges)

    size = 128
    anti_r = lax.broadcasted_iota(jnp.int32, (size, size), 0)
    anti_c = lax.broadcasted_iota(jnp.int32, (size, size), 1)
    anti = (anti_r + anti_c == SPAN - 1).astype(BF16)
    for k in range(comps):
        ktj[k] = jnp.dot(kt[k].astype(BF16), anti, preferred_element_type=F32)

    def build_back(s1):
        at = pl.ds(pl.multiple_of(s1 * ROWS, ROWS), ROWS)
        for side, sign in ((0, 1), (1, -1)):
            for s0 in range(BACK_FINE):
                b = HALF - sign * (1 + s0 + BACK_FINE * s1)
                for k in range(comps):
                    hb[side, k, at, pl.ds(s0 * 128, 128)] = band_matrix(ktj, k, b).astype(BF16)
    loop(0, BACK_COARSE, build_back)
    for k in range(comps):
        hz[k] = band_matrix(ktj, k, HALF).astype(BF16)

    rsbuf[ci] = part[4 + ci]
    scattered.wait_recv()
    far = lax.div(ci, half_nc)
    near = rsbuf[0]
    away = rsbuf[nc]
    for j in range(1, nc):
        near += rsbuf[j]
        away += rsbuf[nc + j]
    linked = ((bi > 0) | (far == 1)) & ((bi < nb - 1) | (far == 0))
    block = near + jnp.where(linked, away, 0.0)
    iblk[...] = jnp.concatenate([block[:, :128], block[:, 128:]], axis=0).astype(BF16)
    iwin[ci + 4] = iblk[...]
    far_band = lax.rem(bi + nb - 1 + 2 * far, nb)
    far_slot = ci + 12 - 16 * far

    def to_peer(j):
        return remote(iblk, iwin.at[ci + 4], iw_s.at[0], iw_r.at[0], j, bi)

    def to_far(j):
        return remote(iblk, iwin.at[far_slot], iw_s.at[0], in_r.at[0], j, far_band)
    for j in range(nc):
        to_far(j).start()
    far_first(to_peers(lambda j: to_peer(j).start()))
    shown = whole(iwin, 2 * nc - 1, iw_s, iw_r)
    ends.append(shown.wait_send)
    near_rows = whole(iwin, nc - 1, iw_s, iw_r)
    far_rows = whole(iwin, nc, iw_s, in_r)
    near_rows.wait_recv()

    inside = ((bi > 0).astype(F32), (bi < nb - 1).astype(F32))
    for r in (4, 6, 8, 10, 0, 2, 12, 14):
        if r == 0:
            far_rows.wait_recv()
        first, second = iwin[r].astype(F32), iwin[r + 1].astype(F32)
        pair = jnp.concatenate([
            jnp.concatenate([first[:8], first[8:]], axis=1),
            jnp.concatenate([second[:8], second[8:]], axis=1)], axis=0)
        if r < 4:
            pair = pair * inside[0]
        if r >= 12:
            pair = pair * inside[1]
        for at, value in all_shifts(pair.astype(BF16)):
            ishift[at, pl.ds(8 * r, 16), :] = value

    rsum = jnp.zeros((ROWS, WIDTH), F32)
    for side in range(2):
        for k in range(comps):
            source = ishift[pl.ds(1 + side * BACK_FINE, BACK_FINE)].reshape(BACK_FINE * 128, WIDTH)
            acc[k, side] = jnp.dot(hb[side, k], source, preferred_element_type=F32)
    for k in range(comps):
        back = jnp.dot(hz[k], ishift[0], preferred_element_type=F32)
        for side, sign in ((0, 1), (1, -1)):
            for s1 in range(BACK_COARSE):
                back += lane_shift(acc[k, side, pl.ds(s1 * ROWS, ROWS), :], sign * BACK_FINE * s1)
        rsum += w_ref[k].astype(F32) * back
    for j in range(8):
        part2[j] = rsum[8 * j:8 * j + 8]

    def rt(j, slot):
        return remote(part2.at[j], rsbuf2.at[slot], rt_s.at[0], rt_r.at[0], j, bi)
    reduced = whole(rsbuf2, nc - 1, rt_s, rt_r)
    ends.append(reduced.wait_send)
    lane_row = lax.broadcasted_iota(jnp.int32, (1, 128), 1)
    quarters = []
    for x in (fold(dir_ref[...] * rsum), *energies):
        x = x + pltpu.roll(x, 64, 1)
        quarters.append(x + pltpu.roll(x, 32, 1))
    sca[...] = jnp.where(
        lane_row < 32, quarters[0], jnp.where(lane_row < 64, quarters[1], quarters[2]))

    def sa(b, slot):
        return remote(sca, sca_in.at[slot], sa_s.at[0], sa_r.at[0], ci, b)
    far_first(to_peers(lambda j: rt(j, ci).start()) + to_bands(lambda b: sa(b, bi).start()))
    products = whole(sca_in, nb - 1, sa_s, sa_r)
    ends.append(products.wait_send)
    sca_in[bi] = sca[...]
    rsbuf2[ci] = part2[ci]

    reduced.wait_recv()
    block = rsbuf2[0]
    for j in range(1, nc):
        block += rsbuf2[j]
    products.wait_recv()
    scalars = sca_in[0]
    for b in range(1, nb):
        scalars += sca_in[b]
    ag[ci, 0] = block[:, :128]
    ag[ci, 1] = block[:, 128:]
    ag[ci, 2] = jnp.broadcast_to(scalars, (8, 128))

    def gather(j, slot):
        return remote(ag.at[ci], ag.at[slot], ag_s.at[0], ag_r.at[0], j, bi)
    far_first(to_peers(lambda j: gather(j, ci).start()))
    gathered = whole(ag, nc - 1, ag_s, ag_r)
    ends.append(gathered.wait_send)
    gathered.wait_recv()

    product = ag[0, 2, 0:1]
    for j in range(1, nc):
        product += ag[j, 2, 0:1]
    scalars = ag[0, 2, 0:1]
    product = jnp.where(lane_row < 32, product, jnp.where(lane_row < 64, DAMPING * scalars, 0.0))
    squared = jnp.where((lane_row >= 64) & (lane_row < 96), scalars, 0.0)
    old = jnp.sum(squared, axis=1, keepdims=True)
    alpha = old / jnp.sum(product, axis=1, keepdims=True)

    for j in range(8):
        for c in range(2):
            at = (slice(8 * j, 8 * j + 8), slice(128 * c, 128 * c + 128))
            rn_ref[at] = res_ref[at] - alpha * (ag[j, c] + DAMPING * dir_ref[at])
    updated = rn_ref[...]
    scb[nb] = fold(updated * updated)

    def sb(b, slot):
        return remote(scb.at[nb], scb.at[slot], sb_s.at[0], sb_r.at[0], ci, b)
    far_first(to_bands(lambda b: sb(b, bi).start()))
    squares = whole(scb, nb - 1, sb_s, sb_r)
    ends.append(squares.wait_send)
    scb[bi] = scb[nb]
    for copy in edges:
        copy.wait_recv()

    estimate_next = est_ref[...] + alpha * dir_ref[...]
    en_ref[...] = estimate_next
    ext[0:8] = (edge_halo[0, 0] + alpha * edge_halo[0, 1]) * inside[0]
    ext[8:72] = estimate_next
    ext[72:80] = (edge_halo[1, 0] + alpha * edge_halo[1, 1]) * inside[1]
    framed = ext[...]
    columns = WIDTH // nc
    start = ci * columns
    pick_r = lax.broadcasted_iota(jnp.int32, (WIDTH, 128), 0)
    pick_c = lax.broadcasted_iota(jnp.int32, (WIDTH, 128), 1)
    group = (pick_c >= GROUP).astype(jnp.int32) + (pick_c >= 2 * GROUP).astype(jnp.int32)
    pick = (pick_r == start - 2 + pick_c - GROUP * group).astype(BF16)
    high = framed.astype(BF16)
    rest = framed - high.astype(F32)
    middle = rest.astype(BF16)
    low = (rest - middle.astype(F32)).astype(BF16)
    tile = (
        jnp.dot(high, pick, preferred_element_type=F32)
        + jnp.dot(middle, pick, preferred_element_type=F32)
        + jnp.dot(low, pick, preferred_element_type=F32)
    )
    tile = jnp.concatenate([tile[6:80], jnp.zeros((14, 128), F32)], axis=0)
    lane = lax.broadcasted_iota(jnp.int32, (24, 128), 1)
    row = lax.broadcasted_iota(jnp.int32, (24, 128), 0)
    third = (lane >= GROUP).astype(jnp.int32) + (lane >= 2 * GROUP).astype(jnp.int32)
    taps = []
    for a in range(3):
        packed = jnp.where(
            third == 0, tile[a:a + 24], jnp.where(third == 1, tile[24 + a:48 + a], tile[48 + a:72 + a]))
        for b in range(3):
            taps.append(packed if b == 0 else pltpu.roll(packed, 128 - b, 1))
    image_row = bi * ROWS - 1 + row + 24 * third
    image_col = start - 1 + lane - GROUP * third
    valid = (image_row >= 0) & (image_row < nb * ROWS) & (image_col >= 0) & (image_col < WIDTH)
    channels = bias_ref.shape[0]
    spreads = []
    for part_of in range(3):
        rows = slice(8 * part_of, 8 * part_of + 8)
        mine = [tap[rows] for tap in taps]

        def channel(c, sums):
            value = mine[0] * fin_ref[0, 0, c] + bias_ref[c]
            for t in range(1, 9):
                value += mine[t] * fin_ref[t // 3, t % 3, c]
            value = jnp.maximum(value, 0.0)
            return tuple(sums[t] + value * fout_ref[t // 3, t % 3, c] for t in range(9))

        sums = lax.fori_loop(
            0, channels, channel, tuple(jnp.zeros((8, 128), F32) for t in range(9)), unroll=unroll)
        spreads.append(sums)
    mixed = jnp.zeros((ROWS, 128), F32)
    for t in range(9):
        a, b = t // 3, t % 3
        whole = jnp.where(valid, jnp.concatenate([s[t] for s in spreads], axis=0), 0.0)
        column = jnp.concatenate(
            [pltpu.roll(whole, (128 - GROUP * g - b) % 128, 1) for g in range(3)], axis=0)
        mixed += column[a:a + ROWS]
    centre = pltpu.roll(tile[2:2 + ROWS], 126, 1)
    den_ref[...] = (centre - mixed).T[:columns]

    for end in ends:
        end()
    squares.wait_recv()
    new = scb[0]
    for b in range(1, nb):
        new += scb[b]
    new = jnp.sum(new, axis=1, keepdims=True)
    dn_ref[...] = rn_ref[...] + (new / old) * dir_ref[...]


def place(*refs):
    count = len(refs) // 2
    sources, targets, sems = refs[:count], refs[count:2 * count], refs[-1]
    copies = [
        pltpu.make_async_copy(source, target, sems.at[i])
        for i, (source, target) in enumerate(zip(sources, targets))
    ]
    for copy in copies:
        copy.start()
    for copy in copies:
        copy.wait()


def per_device(nc, nb, unroll, estimate, residual, direction, kernels, weight_maps, filters_in, biases, filters_out):
    comps = weight_maps.shape[0]
    columns = WIDTH // nc
    vmem = pl.BlockSpec(memory_space=pltpu.VMEM)
    hbm = pl.BlockSpec(memory_space=pltpu.HBM)
    anywhere = pl.BlockSpec(memory_space=pl.ANY)
    band = jax.ShapeDtypeStruct((ROWS, WIDTH), F32)
    shapes = (band, band, band, jax.ShapeDtypeStruct((columns, ROWS), F32))
    dma = pltpu.SemaphoreType.DMA
    results = pl.pallas_call(
        functools.partial(kernel, nc, nb, unroll),
        out_shape=shapes,
        in_specs=[hbm] * 8,
        out_specs=(vmem,) * 4,
        scratch_shapes=[
            pltpu.VMEM((ROWS, WIDTH), F32),
            pltpu.VMEM((ROWS, WIDTH), F32),
            pltpu.VMEM((ROWS, WIDTH), F32),
            pltpu.VMEM((SPAN, comps, SPAN), BF16),
            pltpu.VMEM((comps, ROWS, WIDTH), BF16),
            pltpu.SMEM((3, 3, filters_in.shape[0]), F32),
            pltpu.SMEM(biases.shape, F32),
            pltpu.SMEM((3, 3, filters_in.shape[0]), F32),
            dma((8,)),
            pltpu.VMEM((2, 2, 8, WIDTH), F32),
            pltpu.VMEM((2, 2, 8, WIDTH), F32),
            pltpu.VMEM((comps, 128, 128), F32),
            pltpu.VMEM((comps, 128, 128), F32),
            pltpu.VMEM((comps, 128, 128), F32),
            pltpu.VMEM((2, 2, COARSE * ROWS, WIDTH), F32),
            pltpu.VMEM((comps * ROWS, WIDTH), BF16),
            pltpu.VMEM((2, comps, BACK_COARSE * ROWS, BACK_FINE * 128), BF16),
            pltpu.VMEM((comps, ROWS, 128), BF16),
            pltpu.VMEM((1 + 2 * BACK_FINE, 128, WIDTH), BF16),
            pltpu.VMEM((comps, 2, BACK_COARSE * ROWS, WIDTH), F32),
            pltpu.VMEM((16, 8, WIDTH), F32),
            pltpu.VMEM((2 * nc, 8, WIDTH), F32),
            pltpu.VMEM((16, 128), BF16),
            pltpu.VMEM((16, 16, 128), BF16),
            pltpu.VMEM((8, 8, WIDTH), F32),
            pltpu.VMEM((8, 8, WIDTH), F32),
            pltpu.VMEM((1, 128), F32),
            pltpu.VMEM((nb, 1, 128), F32),
            pltpu.VMEM((nc, 3, 8, 128), F32),
            pltpu.VMEM((nb + 1, 1, 128), F32),
            pltpu.VMEM((80, WIDTH), F32),
            dma((2,)), dma((2,)),
            *([dma((1,))] * 13),
        ],
        compiler_params=pltpu.CompilerParams(
            collective_id=0, has_side_effects=True, vmem_limit_bytes=48 * 1024 * 1024),
        cost_estimate=pl.CostEstimate(
            flops=4 * 65 * comps * 64 * 128 * 256, bytes_accessed=1 << 20, transcendentals=0),
    )(*(pltpu.with_memory_space_constraint(x, pltpu.HBM) for x in (
        estimate, residual, direction, kernels.transpose(1, 0, 2), weight_maps,
        filters_in.transpose(1, 2, 0), biases, filters_out.transpose(1, 2, 0))))
    estimate_next, residual_next, direction_next, turned = pl.pallas_call(
        place,
        out_shape=shapes,
        in_specs=[vmem] * 4,
        out_specs=(anywhere,) * 4,
        scratch_shapes=[dma((4,))],
        compiler_params=pltpu.CompilerParams(vmem_limit_bytes=4 * 1024 * 1024),
    )(*results)
    return estimate_next, residual_next, direction_next, turned.T


def solution(mesh):
    nc, nb = mesh.shape["comp"], mesh.shape["band"]
    return jax.shard_map(
        functools.partial(per_device, nc, nb, 4),
        mesh=mesh,
        in_specs=(
            P("band", None),
            P("band", None),
            P("band", None),
            P("comp", None, None),
            P("comp", "band", None),
            P(),
            P(),
            P(),
        ),
        out_specs=(P("band", None), P("band", None), P("band", None), P("band", "comp")),
        check_vma=False,
    )
```

```python
import functools

import jax
import jax.numpy as jnp
from jax import lax
from jax.experimental import pallas as pl
from jax.experimental.pallas import tpu as pltpu
from jax.sharding import PartitionSpec as P

MESH = pl.DeviceIdType.MESH
F32 = jnp.float32
BF16 = jnp.bfloat16
DAMPING = 0.5
HALF = 32
SPAN = 65
ROWS = 64
WIDTH = 256
FINE = 4
COARSE = 8
BACK_FINE = 8
BACK_COARSE = 4
GROUP = 40


def lane_shift(x, n):
    if n == 0:
        return x
    width = x.shape[1]
    col = lax.broadcasted_iota(jnp.int32, x.shape, 1)
    keep = col < width - n if n > 0 else col >= -n
    return jnp.where(keep, pltpu.roll(x, (-n) % width, 1), jnp.zeros((), x.dtype))


def fold(x):
    x = jnp.sum(x, axis=0, keepdims=True)
    return x[:, :128] + x[:, 128:]


def all_shifts(x):
    yield 0, x
    for s0 in range(BACK_FINE):
        yield 1 + s0, lane_shift(x, 1 + s0)
        yield 1 + BACK_FINE + s0, lane_shift(x, -1 - s0)


def swap_pairs(x):
    return jnp.concatenate(
        [x[(k ^ 1) * ROWS:(k ^ 1) * ROWS + ROWS] for k in range(x.shape[0] // ROWS)], axis=0)


def far_first(fns):
    for hops, fn in sorted(fns, key=lambda pair: -pair[0]):
        fn()


def loop(low, high, fn):
    def body(i, carry):
        fn(i)
        return carry
    lax.fori_loop(low, high, body, 0)


def remote(src, dst, send, recv, comp, band):
    return pltpu.make_async_remote_copy(
        src_ref=src, dst_ref=dst, send_sem=send, recv_sem=recv,
        device_id=(comp, band), device_id_type=MESH,
    )


def kernel(
    nc, nb, unroll,
    est_hbm, res_hbm, dir_hbm, ker_hbm, w_hbm, fin_hbm, bias_hbm, fout_hbm,
    en_ref, rn_ref, dn_ref, den_ref,
    est_ref, res_ref, dir_ref, ker_ref, w_ref, fin_ref, bias_ref, fout_ref, fetch_s,
    edge, edge_halo, kscr, kt, ktj, facc, shaped, hb, hz, ishift, acc,
    part, rsbuf, iblk, iwin, part2, rsbuf2, sca, sca_in, ag, scb, ext,
    h_s, h_r, rs_s, rs_r, iw_s, iw_r, rt_s, rt_r, sa_s, sa_r, ag_s, ag_r, sb_s, sb_r,
):
    ci = lax.axis_index("comp")
    bi = lax.axis_index("band")
    up = lax.rem(bi + nb - 1, nb)
    down = lax.rem(bi + 1, nb)
    comps = w_ref.shape[0]
    half_nc = nc // 2

    def whole(ref, count, send, recv):
        slots = ref.at[pl.ds(0, count)]
        return remote(slots, slots, send.at[0], recv.at[0], ci, up)

    def ring(d, n):
        return min(d, n - d)

    xs = nc // 2
    far_peers = [
        (ring(dx, xs) + 2 * dz,
         lax.rem(lax.div(ci, 2) + dx, xs) * 2 + lax.rem(ci + dz, 2))
        for dx in range(xs) for dz in range(2) if dx or dz
    ]
    if nb % 4 == 0:
        ys = nb // 4
        far_bands = [
            (ring(dy, ys) + dz + dc / 2,
             lax.rem(lax.div(bi, 2 * ys) + dz, 2) * 2 * ys
             + lax.rem(lax.rem(lax.div(bi, 2), ys) + dy, ys) * 2 + lax.rem(bi + dc, 2))
            for dz in range(2) for dy in range(ys) for dc in range(2) if dz or dy or dc
        ]
    else:
        far_bands = [(1, lax.rem(bi + d, nb)) for d in range(1, nb)]

    def to_peers(fn):
        return [(hops, lambda j=j: fn(j)) for hops, j in far_peers]

    def to_bands(fn):
        return [(hops, lambda b=b: fn(b)) for hops, b in far_bands]

    fetches = [
        pltpu.make_async_copy(source, target, fetch_s.at[i])
        for i, (source, target) in enumerate((
            (ker_hbm, ker_ref), (dir_hbm, dir_ref), (w_hbm, w_ref), (res_hbm, res_ref),
            (est_hbm, est_ref), (fin_hbm, fin_ref), (bias_hbm, bias_ref), (fout_hbm, fout_ref)))
    ]
    for copy in fetches:
        copy.start()
    ends = []

    barrier = pltpu.get_barrier_semaphore()

    def greet(comp, band):
        pl.semaphore_signal(barrier, inc=1, device_id=(comp, band), device_id_type=MESH)

    over = [
        (hops + 1, lambda j=j, b=b: greet(j, b))
        for hops, j in far_peers + [(0, ci)] for b in (up, down)
    ]
    far_first(over + to_peers(lambda j: greet(j, bi)))
    for d in range(2, nb - 1):
        greet(ci, lax.rem(bi + d, nb))

    kscr[...] = jnp.zeros_like(kscr)
    fetches[0].wait()
    for a in range(SPAN):
        kscr[:, a, 0:SPAN] = ker_ref[a].astype(F32)
    for k in range(comps):
        kt[k] = kscr[k].T

    fetches[1].wait()
    fetches[2].wait()
    direction = dir_ref[...]
    for k in range(comps):
        shaped[pl.ds(k * ROWS, ROWS), :] = (w_ref[k].astype(F32) * direction).astype(BF16)

    def band_matrix(table, k, b, first=0):
        row = table[k, pl.ds(b, 1), :]
        spread = jnp.broadcast_to(row, (ROWS, 128))
        return pltpu.roll(spread, first, 1, stride=1, stride_axis=0)

    left = lax.broadcasted_iota(jnp.int32, (ROWS, 128), 1) < ROWS

    def forward_pair(k, b):
        even = band_matrix(kt, k, b)
        odd = band_matrix(kt, k + 1, b, ROWS)
        lower = jnp.where(left, even, odd).astype(BF16)
        upper = jnp.where(left, odd, even).astype(BF16)
        return lower, upper

    def forward_matrices(columns):
        lower, upper = [], []
        for b in columns:
            pairs = [forward_pair(k, b) for k in range(0, comps, 2)]
            lower.append(jnp.concatenate([pair[0] for pair in pairs], axis=1))
            upper.append(jnp.concatenate([pair[1] for pair in pairs], axis=1))
        return jnp.concatenate(lower, axis=0), jnp.concatenate(upper, axis=0)

    for s0 in range(FINE):
        for side, sign in ((0, 1), (1, -1)):
            source = lane_shift(shaped[...], sign * (1 + s0))
            lower, upper = forward_matrices(
                [HALF + sign * (1 + s0 + FINE * s1) for s1 in range(COARSE)])
            for where, matrix, rows in ((0, lower, source), (1, upper, swap_pairs(source))):
                product = jnp.dot(matrix, rows, preferred_element_type=F32)
                if s0 == 0:
                    facc[side, where] = product
                else:
                    facc[side, where] += product
    lower, upper = forward_matrices([HALF])
    for where, matrix, rows in ((0, lower, shaped[...]), (1, upper, swap_pairs(shaped[...]))):
        total = jnp.dot(matrix, rows, preferred_element_type=F32)
        for side, sign in ((0, 1), (1, -1)):
            for s1 in range(COARSE):
                total += lane_shift(
                    facc[side, where, pl.ds(s1 * ROWS, ROWS), :], sign * FINE * s1)
        base = 8 * (1 - where)
        for q in range(8):
            part[base + q] = total[8 * q:8 * q + 8]

    for copy in fetches[3:]:
        copy.wait()
    edge[0, 0] = est_ref[:8]
    edge[0, 1] = dir_ref[:8]
    edge[1, 0] = est_ref[ROWS - 8:]
    edge[1, 1] = dir_ref[ROWS - 8:]
    residual = res_ref[...]
    energies = (fold(direction * direction), fold(residual * residual))
    pl.semaphore_wait(barrier, nc - 1 + 2 * nc + nb - 3)

    def rs_up(c):
        return remote(part.at[c], rsbuf.at[nc + ci], rs_s.at[0], rs_r.at[0], c + half_nc, up)

    def rs_down(c):
        return remote(
            part.at[12 + c], rsbuf.at[nc + ci], rs_s.at[0], rs_r.at[0], c, down)

    def rs(j):
        return remote(part.at[4 + j], rsbuf.at[ci], rs_s.at[0], rs_r.at[0], j, bi)

    for c in range(half_nc):
        rs_up(c).start()
        rs_down(c).start()
    far_first(to_peers(lambda j: rs(j).start()))
    edges = [
        remote(edge.at[0], edge_halo.at[1], h_s.at[0], h_r.at[1], ci, up),
        remote(edge.at[1], edge_halo.at[0], h_s.at[1], h_r.at[0], ci, down),
    ]
    for copy in edges:
        copy.start()

    scattered = whole(part, 2 * nc - 1, rs_s, rs_r)
    ends.append(scattered.wait_send)
    ends.extend(copy.wait_send for copy in edges)

    size = 128
    anti_r = lax.broadcasted_iota(jnp.int32, (size, size), 0)
    anti_c = lax.broadcasted_iota(jnp.int32, (size, size), 1)
    anti = (anti_r + anti_c == SPAN - 1).astype(BF16)
    for k in range(comps):
        ktj[k] = jnp.dot(kt[k].astype(BF16), anti, preferred_element_type=F32)

    def build_back(s1):
        at = pl.ds(pl.multiple_of(s1 * ROWS, ROWS), ROWS)
        for side, sign in ((0, 1), (1, -1)):
            for s0 in range(BACK_FINE):
                b = HALF - sign * (1 + s0 + BACK_FINE * s1)
                for k in range(comps):
                    hb[side, k, at, pl.ds(s0 * 128, 128)] = band_matrix(ktj, k, b).astype(BF16)
    loop(0, BACK_COARSE, build_back)
    for k in range(comps):
        hz[k] = band_matrix(ktj, k, HALF).astype(BF16)

    rsbuf[ci] = part[4 + ci]
    scattered.wait_recv()
    far = lax.div(ci, half_nc)
    near = rsbuf[0]
    away = rsbuf[nc]
    for j in range(1, nc):
        near += rsbuf[j]
        away += rsbuf[nc + j]
    linked = ((bi > 0) | (far == 1)) & ((bi < nb - 1) | (far == 0))
    block = near + jnp.where(linked, away, 0.0)
    iblk[...] = jnp.concatenate([block[:, :128], block[:, 128:]], axis=0).astype(BF16)
    iwin[ci + 4] = iblk[...]
    far_band = lax.rem(bi + nb - 1 + 2 * far, nb)
    far_slot = ci + 12 - 16 * far

    def to_peer(j):
        return remote(iblk, iwin.at[ci + 4], iw_s.at[0], iw_r.at[0], j, bi)

    def to_far(j):
        return remote(iblk, iwin.at[far_slot], iw_s.at[0], iw_r.at[0], j, far_band)
    over = [(hops + 1, lambda j=j: to_far(j).start()) for hops, j in far_peers + [(0, ci)]]
    far_first(over + to_peers(lambda j: to_peer(j).start()))
    shown = whole(iwin, 2 * nc - 1, iw_s, iw_r)
    ends.append(shown.wait_send)
    shown.wait_recv()

    inside = ((bi > 0).astype(F32), (bi < nb - 1).astype(F32))
    for r in range(0, 16, 2):
        first, second = iwin[r].astype(F32), iwin[r + 1].astype(F32)
        pair = jnp.concatenate([
            jnp.concatenate([first[:8], first[8:]], axis=1),
            jnp.concatenate([second[:8], second[8:]], axis=1)], axis=0)
        if r < 4:
            pair = pair * inside[0]
        if r >= 12:
            pair = pair * inside[1]
        for at, value in all_shifts(pair.astype(BF16)):
            ishift[at, pl.ds(8 * r, 16), :] = value

    rsum = jnp.zeros((ROWS, WIDTH), F32)
    for side in range(2):
        for k in range(comps):
            source = ishift[pl.ds(1 + side * BACK_FINE, BACK_FINE)].reshape(BACK_FINE * 128, WIDTH)
            acc[k, side] = jnp.dot(hb[side, k], source, preferred_element_type=F32)
    for k in range(comps):
        back = jnp.dot(hz[k], ishift[0], preferred_element_type=F32)
        for side, sign in ((0, 1), (1, -1)):
            for s1 in range(BACK_COARSE):
                back += lane_shift(acc[k, side, pl.ds(s1 * ROWS, ROWS), :], sign * BACK_FINE * s1)
        rsum += w_ref[k].astype(F32) * back
    for j in range(8):
        part2[j] = rsum[8 * j:8 * j + 8]

    def rt(j, slot):
        return remote(part2.at[j], rsbuf2.at[slot], rt_s.at[0], rt_r.at[0], j, bi)
    reduced = whole(rsbuf2, nc - 1, rt_s, rt_r)
    ends.append(reduced.wait_send)
    lane_row = lax.broadcasted_iota(jnp.int32, (1, 128), 1)
    quarters = []
    for x in (fold(dir_ref[...] * rsum), *energies):
        x = x + pltpu.roll(x, 64, 1)
        quarters.append(x + pltpu.roll(x, 32, 1))
    sca[...] = jnp.where(
        lane_row < 32, quarters[0], jnp.where(lane_row < 64, quarters[1], quarters[2]))

    def sa(b, slot):
        return remote(sca, sca_in.at[slot], sa_s.at[0], sa_r.at[0], ci, b)
    far_first(to_peers(lambda j: rt(j, ci).start()) + to_bands(lambda b: sa(b, bi).start()))
    products = whole(sca_in, nb - 1, sa_s, sa_r)
    ends.append(products.wait_send)
    sca_in[bi] = sca[...]
    rsbuf2[ci] = part2[ci]

    reduced.wait_recv()
    block = rsbuf2[0]
    for j in range(1, nc):
        block += rsbuf2[j]
    products.wait_recv()
    scalars = sca_in[0]
    for b in range(1, nb):
        scalars += sca_in[b]
    ag[ci, 0] = block[:, :128]
    ag[ci, 1] = block[:, 128:]
    ag[ci, 2] = jnp.broadcast_to(scalars, (8, 128))

    def gather(j, slot):
        return remote(ag.at[ci], ag.at[slot], ag_s.at[0], ag_r.at[0], j, bi)
    far_first(to_peers(lambda j: gather(j, ci).start()))
    gathered = whole(ag, nc - 1, ag_s, ag_r)
    ends.append(gathered.wait_send)
    gathered.wait_recv()

    product = ag[0, 2, 0:1]
    for j in range(1, nc):
        product += ag[j, 2, 0:1]
    scalars = ag[0, 2, 0:1]
    product = jnp.where(lane_row < 32, product, jnp.where(lane_row < 64, DAMPING * scalars, 0.0))
    squared = jnp.where((lane_row >= 64) & (lane_row < 96), scalars, 0.0)
    old = jnp.sum(squared, axis=1, keepdims=True)
    alpha = old / jnp.sum(product, axis=1, keepdims=True)

    for j in range(8):
        for c in range(2):
            at = (slice(8 * j, 8 * j + 8), slice(128 * c, 128 * c + 128))
            rn_ref[at] = res_ref[at] - alpha * (ag[j, c] + DAMPING * dir_ref[at])
    updated = rn_ref[...]
    scb[nb] = fold(updated * updated)

    def sb(b, slot):
        return remote(scb.at[nb], scb.at[slot], sb_s.at[0], sb_r.at[0], ci, b)
    far_first(to_bands(lambda b: sb(b, bi).start()))
    squares = whole(scb, nb - 1, sb_s, sb_r)
    ends.append(squares.wait_send)
    scb[bi] = scb[nb]
    for copy in edges:
        copy.wait_recv()

    estimate_next = est_ref[...] + alpha * dir_ref[...]
    en_ref[...] = estimate_next
    ext[0:8] = (edge_halo[0, 0] + alpha * edge_halo[0, 1]) * inside[0]
    ext[8:72] = estimate_next
    ext[72:80] = (edge_halo[1, 0] + alpha * edge_halo[1, 1]) * inside[1]
    framed = ext[...]
    columns = WIDTH // nc
    start = ci * columns
    pick_r = lax.broadcasted_iota(jnp.int32, (WIDTH, 128), 0)
    pick_c = lax.broadcasted_iota(jnp.int32, (WIDTH, 128), 1)
    group = (pick_c >= GROUP).astype(jnp.int32) + (pick_c >= 2 * GROUP).astype(jnp.int32)
    pick = (pick_r == start - 2 + pick_c - GROUP * group).astype(BF16)
    high = framed.astype(BF16)
    rest = framed - high.astype(F32)
    middle = rest.astype(BF16)
    low = (rest - middle.astype(F32)).astype(BF16)
    tile = (
        jnp.dot(high, pick, preferred_element_type=F32)
        + jnp.dot(middle, pick, preferred_element_type=F32)
        + jnp.dot(low, pick, preferred_element_type=F32)
    )
    tile = jnp.concatenate([tile[6:80], jnp.zeros((14, 128), F32)], axis=0)
    lane = lax.broadcasted_iota(jnp.int32, (24, 128), 1)
    row = lax.broadcasted_iota(jnp.int32, (24, 128), 0)
    third = (lane >= GROUP).astype(jnp.int32) + (lane >= 2 * GROUP).astype(jnp.int32)
    taps = []
    for a in range(3):
        packed = jnp.where(
            third == 0, tile[a:a + 24], jnp.where(third == 1, tile[24 + a:48 + a], tile[48 + a:72 + a]))
        for b in range(3):
            taps.append(packed if b == 0 else pltpu.roll(packed, 128 - b, 1))
    image_row = bi * ROWS - 1 + row + 24 * third
    image_col = start - 1 + lane - GROUP * third
    valid = (image_row >= 0) & (image_row < nb * ROWS) & (image_col >= 0) & (image_col < WIDTH)
    channels = bias_ref.shape[0]
    spreads = []
    for part_of in range(3):
        rows = slice(8 * part_of, 8 * part_of + 8)
        mine = [tap[rows] for tap in taps]

        def channel(c, sums):
            value = mine[0] * fin_ref[0, 0, c] + bias_ref[c]
            for t in range(1, 9):
                value += mine[t] * fin_ref[t // 3, t % 3, c]
            value = jnp.maximum(value, 0.0)
            return tuple(sums[t] + value * fout_ref[t // 3, t % 3, c] for t in range(9))

        sums = lax.fori_loop(
            0, channels, channel, tuple(jnp.zeros((8, 128), F32) for t in range(9)), unroll=unroll)
        spreads.append(sums)
    mixed = jnp.zeros((ROWS, 128), F32)
    for t in range(9):
        a, b = t // 3, t % 3
        whole = jnp.where(valid, jnp.concatenate([s[t] for s in spreads], axis=0), 0.0)
        column = jnp.concatenate(
            [pltpu.roll(whole, (128 - GROUP * g - b) % 128, 1) for g in range(3)], axis=0)
        mixed += column[a:a + ROWS]
    centre = pltpu.roll(tile[2:2 + ROWS], 126, 1)
    den_ref[...] = (centre - mixed).T[:columns]

    for end in ends:
        end()
    squares.wait_recv()
    new = scb[0]
    for b in range(1, nb):
        new += scb[b]
    new = jnp.sum(new, axis=1, keepdims=True)
    dn_ref[...] = rn_ref[...] + (new / old) * dir_ref[...]


def place(*refs):
    count = len(refs) // 2
    sources, targets, sems = refs[:count], refs[count:2 * count], refs[-1]
    copies = [
        pltpu.make_async_copy(source, target, sems.at[i])
        for i, (source, target) in enumerate(zip(sources, targets))
    ]
    for copy in copies:
        copy.start()
    for copy in copies:
        copy.wait()


def per_device(nc, nb, unroll, estimate, residual, direction, kernels, weight_maps, filters_in, biases, filters_out):
    comps = weight_maps.shape[0]
    columns = WIDTH // nc
    vmem = pl.BlockSpec(memory_space=pltpu.VMEM)
    hbm = pl.BlockSpec(memory_space=pltpu.HBM)
    anywhere = pl.BlockSpec(memory_space=pl.ANY)
    band = jax.ShapeDtypeStruct((ROWS, WIDTH), F32)
    shapes = (band, band, band, jax.ShapeDtypeStruct((columns, ROWS), F32))
    dma = pltpu.SemaphoreType.DMA
    results = pl.pallas_call(
        functools.partial(kernel, nc, nb, unroll),
        out_shape=shapes,
        in_specs=[hbm] * 8,
        out_specs=(vmem,) * 4,
        scratch_shapes=[
            pltpu.VMEM((ROWS, WIDTH), F32),
            pltpu.VMEM((ROWS, WIDTH), F32),
            pltpu.VMEM((ROWS, WIDTH), F32),
            pltpu.VMEM((SPAN, comps, SPAN), BF16),
            pltpu.VMEM((comps, ROWS, WIDTH), BF16),
            pltpu.SMEM((3, 3, filters_in.shape[0]), F32),
            pltpu.SMEM(biases.shape, F32),
            pltpu.SMEM((3, 3, filters_in.shape[0]), F32),
            dma((8,)),
            pltpu.VMEM((2, 2, 8, WIDTH), F32),
            pltpu.VMEM((2, 2, 8, WIDTH), F32),
            pltpu.VMEM((comps, 128, 128), F32),
            pltpu.VMEM((comps, 128, 128), F32),
            pltpu.VMEM((comps, 128, 128), F32),
            pltpu.VMEM((2, 2, COARSE * ROWS, WIDTH), F32),
            pltpu.VMEM((comps * ROWS, WIDTH), BF16),
            pltpu.VMEM((2, comps, BACK_COARSE * ROWS, BACK_FINE * 128), BF16),
            pltpu.VMEM((comps, ROWS, 128), BF16),
            pltpu.VMEM((1 + 2 * BACK_FINE, 128, WIDTH), BF16),
            pltpu.VMEM((comps, 2, BACK_COARSE * ROWS, WIDTH), F32),
            pltpu.VMEM((16, 8, WIDTH), F32),
            pltpu.VMEM((2 * nc, 8, WIDTH), F32),
            pltpu.VMEM((16, 128), BF16),
            pltpu.VMEM((16, 16, 128), BF16),
            pltpu.VMEM((8, 8, WIDTH), F32),
            pltpu.VMEM((8, 8, WIDTH), F32),
            pltpu.VMEM((1, 128), F32),
            pltpu.VMEM((nb, 1, 128), F32),
            pltpu.VMEM((nc, 3, 8, 128), F32),
            pltpu.VMEM((nb + 1, 1, 128), F32),
            pltpu.VMEM((80, WIDTH), F32),
            dma((2,)), dma((2,)),
            *([dma((1,))] * 12),
        ],
        compiler_params=pltpu.CompilerParams(
            collective_id=0, has_side_effects=True, vmem_limit_bytes=48 * 1024 * 1024),
        cost_estimate=pl.CostEstimate(
            flops=4 * 65 * comps * 64 * 128 * 256, bytes_accessed=1 << 20, transcendentals=0),
    )(*(pltpu.with_memory_space_constraint(x, pltpu.HBM) for x in (
        estimate, residual, direction, kernels.transpose(1, 0, 2), weight_maps,
        filters_in.transpose(1, 2, 0), biases, filters_out.transpose(1, 2, 0))))
    estimate_next, residual_next, direction_next, turned = pl.pallas_call(
        place,
        out_shape=shapes,
        in_specs=[vmem] * 4,
        out_specs=(anywhere,) * 4,
        scratch_shapes=[dma((4,))],
        compiler_params=pltpu.CompilerParams(vmem_limit_bytes=4 * 1024 * 1024),
    )(*results)
    return estimate_next, residual_next, direction_next, turned.T


def solution(mesh):
    nc, nb = mesh.shape["comp"], mesh.shape["band"]
    return jax.shard_map(
        functools.partial(per_device, nc, nb, 4),
        mesh=mesh,
        in_specs=(
            P("band", None),
            P("band", None),
            P("band", None),
            P("comp", None, None),
            P("comp", "band", None),
            P(),
            P(),
            P(),
        ),
        out_specs=(P("band", None), P("band", None), P("band", None), P("band", "comp")),
        check_vma=False,
    )
```
